256 devices in a mesh: slab: 16 (over z_hi, y, core), dir: 16 (over z_lo, x).
Axes of the slice: x: 4, y: 4, z: 8 (z_hi: 2, z_lo: 4; z = z_hi * 4 + z_lo), core: 2. Of those that a mesh axis runs over, the one named last changes fastest.
Arguments:
- currents: float32 [32, 32, 6, 8, 2, 128], P('slab', 'dir'), may hold values from -6 to 6
- near_tiles: float32 [27, 2, 128, 128], replicated, may hold values from -0.078125 to 0.078125
- radiation: float32 [2, 1024, 128], replicated, may hold values from -0.5 to 0.5
- child_phase: float32 [8, 1024], replicated, may hold values from -3.140625 to 3.140625
- translators: float32 [316, 2, 1024], P(None, None, 'dir'), may hold values from -0.0625 to 0.0625
- far_targets: int32 [768, 16], replicated, may hold values from 0 to 767, as said below
- far_offsets: int32 [768, 16], replicated, may hold values from 0 to 315, as said below
Outputs:
- applied: float32 [32, 32, 6, 8, 2, 128], P('slab', 'dir')
The draws below stay inside these ranges and needn't reach their ends.
Inputs may be any that keep to these rules, and one draw needn't show every extreme that they name: For each source parent s, far_targets[s] holds 16 different parent numbers t inside the grid; along every grid dimension the parent coordinates of t and s differ by at most 3, and along at least one by 2 or more. far_offsets[s, f] names the translation operator of the coordinate difference between far_targets[s, f] and s; equal differences have equal operators and each of the 316 differences has its own.
All inputs are finite; a program needn't handle non-finite values.
Results may differ from the reference program's by a relative error of at most 0.0001.
Values sent between devices are 32-bit elements; how exact they have to be, the bound alone decides.
No kernel may reach another device: no remote copies, remote signals or barrier semaphores. Data moves between devices by JAX's collectives and lax.ppermute only.
A program may use at most 192 MiB of HBM per device.

```python
import jax
import jax.numpy as jnp
from jax import lax

P_SIZE = 128
K = 1024
R = 8
LZ = 6
F = 16
NOFF = 316
GX = 32
GY = 32
NPAR = 768
N_SLAB = 16


def far_lists(key):
    positions = jnp.arange(343, dtype=jnp.int32)
    step_x = positions // 49 - 3
    step_y = positions // 7 % 7 - 3
    step_z = positions % 7 - 3
    reach = jnp.maximum(jnp.maximum(jnp.abs(step_x), jnp.abs(step_y)), jnp.abs(step_z))
    distant = (reach >= 2).astype(jnp.int32)
    operator_id = jnp.cumsum(distant) - 1
    boxes_x = GX // 2
    boxes_y = GY // 2
    boxes_z = LZ // 2
    parents = jnp.arange(NPAR, dtype=jnp.int32)
    coord_x = parents // (boxes_y * boxes_z)
    coord_y = parents // boxes_z % boxes_y
    coord_z = parents % boxes_z
    target_x = coord_x[:, None] + step_x[None, :]
    target_y = coord_y[:, None] + step_y[None, :]
    target_z = coord_z[:, None] + step_z[None, :]
    in_grid = (target_x >= 0) & (target_x < boxes_x) & (target_y >= 0) & (target_y < boxes_y)
    in_grid = in_grid & (target_z >= 0) & (target_z < boxes_z) & (distant[None, :] == 1)
    scores = jax.random.randint(key, (NPAR, 343), 0, 1 << 20, dtype=jnp.int32) * 512 + positions[None, :]
    scores = jnp.where(in_grid, scores, -1)
    chosen = lax.top_k(scores, F)[1].astype(jnp.int32)
    numbers = (target_x * boxes_y + target_y) * boxes_z + target_z
    targets = jnp.take_along_axis(numbers, chosen, axis=1).astype(jnp.int32)
    offsets = operator_id[chosen].astype(jnp.int32)
    return (targets, offsets)


def draw_far_targets(key, part):
    return far_lists(jax.random.fold_in(key, 7))[0]


def draw_far_offsets(key, part):
    return far_lists(jax.random.fold_in(key, 7))[1]


def steps_of(own_key, shape, cuts, low, top_value):
    loudness, own = 1.0, jax.random.fold_in(own_key, 6)
    for position, blocks in cuts:
        heights = jnp.exp(jax.random.uniform(jax.random.fold_in(own, position), (blocks,), jnp.float32, low / len(cuts), top_value / len(cuts)))
        loudness = loudness * jnp.repeat(heights, shape[position] // blocks).reshape([-1 if axis == position else 1 for axis in range(len(shape))])
    return loudness


def gaussian(rng, shape, scale, most, cuts=(), kind=jnp.bfloat16):
    drawn = jax.random.normal(rng, shape, jnp.float32) * scale
    if len(cuts) > 0:
        drawn = steps_of(rng, shape, cuts, -0.22, 0.18) * drawn
    return jnp.clip(drawn, min=-most, max=most).astype(kind)


def setup_inputs(seed: int = 0) -> dict:
    splits = jax.random.split(jax.random.key(seed), 8)
    currents = gaussian(splits[0], (GX, GY, LZ, R, 2, P_SIZE), 1.0, 6.0, ((0, 16), (1, 16)), jnp.float32)
    near_tiles = gaussian(splits[1], (27, 2, P_SIZE, P_SIZE), (54 * P_SIZE) ** -0.5, 0.078125, (), jnp.float32)
    radiation = gaussian(splits[2], (2, K, P_SIZE), P_SIZE ** -0.5, 0.5, (), jnp.float32)
    child_phase = jnp.clip(jax.random.uniform(splits[3], (8, K), jnp.float32, -3.140625, 3.140625), -3.140625, 3.140625)
    translators = gaussian(splits[4], (NOFF, 2, K), ((P_SIZE / (64 * K * F)) ** 0.5), 0.0625, ((2, 16),), jnp.float32)
    far_targets = draw_far_targets(jax.random.fold_in(splits[7], 71), 0)
    far_offsets = draw_far_offsets(jax.random.fold_in(splits[7], 71), 0)
    return {"currents": currents, "near_tiles": near_tiles, "radiation": radiation, "child_phase": child_phase, "translators": translators, "far_targets": far_targets, "far_offsets": far_offsets}


HIGH = lax.Precision.HIGHEST


def block_matrix(real_part, imag_part):
    return jnp.block([[real_part.T, imag_part.T], [-imag_part.T, real_part.T]])


def near_sum(padded_xy, near_tiles):
    width = near_tiles.shape[-1]
    size_x = padded_xy.shape[0] - 2
    size_y = padded_xy.shape[1] - 2
    size_z = padded_xy.shape[2]
    padded = jnp.pad(padded_xy, ((0, 0), (0, 0), (1, 1), (0, 0), (0, 0), (0, 0)))
    out_shape = (size_x, size_y, size_z) + padded.shape[3:]
    total = jnp.zeros((size_x * size_y * size_z * padded.shape[3], 2 * width), jnp.float32)
    for along_x in range(3):
        for along_y in range(3):
            for along_z in range(3):
                offset = along_x * 9 + along_y * 3 + along_z
                matrix = block_matrix(near_tiles[offset, 0], near_tiles[offset, 1])
                view = padded[along_x:along_x + size_x, along_y:along_y + size_y, along_z:along_z + size_z]
                total = total + jnp.dot(view.reshape(-1, 2 * width), matrix, precision=HIGH, preferred_element_type=jnp.float32)
    return total.reshape(out_shape)


def aggregate(block, radiation, child_phase):
    width = radiation.shape[2]
    dirs = radiation.shape[1]
    boxes_y = block.shape[1] // 2
    half_z = block.shape[2] // 2
    sides = block.shape[3]
    matrix = block_matrix(radiation[0], radiation[1])
    flat = jnp.dot(block.reshape(-1, 2 * width), matrix, precision=HIGH, preferred_element_type=jnp.float32)
    leaves = flat.reshape(2, boxes_y, 2, half_z, 2, sides, 2, dirs)
    real_leaf = leaves[..., 0, :]
    imag_leaf = leaves[..., 1, :]
    cos_part = jnp.cos(child_phase).reshape(2, 2, 2, dirs)
    sin_part = jnp.sin(child_phase).reshape(2, 2, 2, dirs)
    form = "ibjpkrq,ijkq->bprq"
    real_par = jnp.einsum(form, real_leaf, cos_part, precision=HIGH) - jnp.einsum(form, imag_leaf, sin_part, precision=HIGH)
    imag_par = jnp.einsum(form, imag_leaf, cos_part, precision=HIGH) + jnp.einsum(form, real_leaf, sin_part, precision=HIGH)
    parents = jnp.stack([real_par, imag_par], axis=3)
    return parents.reshape(boxes_y * half_z, sides, 2, dirs)


def disaggregate(incoming, radiation, child_phase, half_z):
    width = radiation.shape[2]
    dirs = radiation.shape[1]
    sides = incoming.shape[1]
    boxes_y = incoming.shape[0] // half_z
    shaped = incoming.reshape(boxes_y, half_z, sides, 2, dirs)
    real_in = shaped[:, :, :, 0, :][None, :, None, :, None, :, :]
    imag_in = shaped[:, :, :, 1, :][None, :, None, :, None, :, :]
    cos_part = jnp.cos(child_phase).reshape(2, 2, 2, dirs)[:, None, :, None, :, None, :]
    sin_part = jnp.sin(child_phase).reshape(2, 2, 2, dirs)[:, None, :, None, :, None, :]
    real_child = cos_part * real_in + sin_part * imag_in
    imag_child = cos_part * imag_in - sin_part * real_in
    children = jnp.stack([real_child, imag_child], axis=6)
    matrix = block_matrix(radiation[0], radiation[1]).T
    flat = jnp.dot(children.reshape(-1, 2 * dirs), matrix, precision=HIGH, preferred_element_type=jnp.float32)
    return flat.reshape(2, 2 * boxes_y, 2 * half_z, sides, 2, width)


def reference(currents, near_tiles, radiation, child_phase, translators, far_targets, far_offsets):
    half_z = LZ // 2
    slab_rows = NPAR // N_SLAB
    by_slab = currents.reshape((N_SLAB, 2) + currents.shape[1:])
    patterns = lax.map(lambda block: aggregate(block, radiation, child_phase), by_slab)
    patterns = patterns.reshape(NPAR, R, 2, K)
    real_src = patterns[:, :, 0, :]
    imag_src = patterns[:, :, 1, :]
    incoming = jnp.zeros((NPAR, R, 2, K), jnp.float32)
    for slot in range(F):
        picked = translators[far_offsets[:, slot]]
        real_tr = picked[:, 0, :][:, None, :]
        imag_tr = picked[:, 1, :][:, None, :]
        term = jnp.stack([real_tr * real_src - imag_tr * imag_src, real_tr * imag_src + imag_tr * real_src], axis=2)
        incoming = incoming + jax.ops.segment_sum(term, far_targets[:, slot], num_segments=NPAR)
    far_parts = lax.map(lambda rows: disaggregate(rows, radiation, child_phase, half_z), incoming.reshape(N_SLAB, slab_rows, R, 2, K))
    far = far_parts.reshape(currents.shape)
    padded_xy = jnp.pad(currents, ((1, 1), (1, 1), (0, 0), (0, 0), (0, 0), (0, 0)))
    near = near_sum(padded_xy, near_tiles)
    return near + far
```

```python
import functools

import jax
import jax.numpy as jnp
from jax import lax
from jax.experimental import pallas as pl
from jax.experimental.pallas import tpu as pltpu
from jax.sharding import PartitionSpec as P

F32 = jnp.float32
BF16 = jnp.bfloat16
AXES = ("slab", "dir")
VMEM_BYTES = 32 * 1024 * 1024
NT = (((1,), (1,)), ((), ()))
NN = (((1,), (0,)), ((), ()))


def linear(z_hi, y, core, d):
    return (z_hi * 8 + y * 2 + core) * 16 + d


def route_of(move):
    pairs = []
    for s in range(16):
        for d in range(16):
            to = move(s // 8, s // 2 % 4, s % 2, d)
            if to is not None:
                pairs.append((s * 16 + d, linear(*to)))
    return pairs


def exchange_groups():
    return [
        [linear(z_hi, j // 2, j % 2, d) for z_hi in range(2) for d in range(16)] for j in range(8)
    ]


def split(x):
    hi = x.astype(BF16)
    lo = (x - hi.astype(F32)).astype(BF16)
    return hi, lo


def dot3(a, b, dims):
    a_hi, a_lo = a
    b_hi, b_lo = b
    dot = functools.partial(lax.dot_general, dimension_numbers=dims, preferred_element_type=F32)
    return dot(a_hi, b_hi) + (dot(a_lo, b_hi) + dot(a_hi, b_lo))


def lane_sign(shape):
    lane = lax.broadcasted_iota(jnp.int32, shape, len(shape) - 1) % 128
    return jnp.where(lane < 64, -1.0, 1.0).astype(F32)


def times_i(x):
    return lane_sign(x.shape) * pltpu.roll(x, 64, 1)


def swap_bits(x):
    row = lax.broadcasted_iota(jnp.int32, x.shape, 0) // 4 % 2
    lane = lax.broadcasted_iota(jnp.int32, x.shape, 1) // 32 % 2
    other = pltpu.roll(x, 4, 0)
    moved = jnp.where(lane == 1, pltpu.roll(other, 32, 1), pltpu.roll(other, 96, 1))
    return jnp.where(row == lane, x, moved)


def radiation_block(rad_ref, start):
    re = rad_ref[0, pl.ds(start, 128), :]
    im = rad_ref[1, pl.ds(start, 128), :]
    top = jnp.concatenate([re, -im], axis=1)
    low = jnp.concatenate([im, re], axis=1)
    return split(jnp.concatenate([top[:64], low[:64], top[64:], low[64:]], axis=0))


def phase_block(phase_ref, start):
    phase = phase_ref[:, pl.ds(start, 128)]
    lane = lax.broadcasted_iota(jnp.int32, phase.shape, 1)

    def doubled(v):
        turned = pltpu.roll(v, 64, 1)
        return jnp.concatenate(
            [jnp.where(lane < 64, v, turned), jnp.where(lane < 64, turned, v)], axis=1
        )

    return doubled(jnp.cos(phase)), doubled(jnp.sin(phase))


def leaf_row(child, parent):
    i, j, l = child // 4, child // 2 % 2, child % 2
    return ((i * 2 + j) * 6 + parent * 2 + l) * 8


def aggregate_kernel(cur_ref, rad_ref, phase_ref, out_ref):
    rows = cur_ref.shape[0] // 2
    x = jnp.concatenate(
        [cur_ref[pl.ds(0, rows, stride=2), :], cur_ref[pl.ds(1, rows, stride=2), :]], axis=1
    )
    x = split(x)

    @pl.loop(0, 8)
    def _(step):
        start = pl.multiple_of(step * 128, 128)
        leaf = dot3(x, radiation_block(rad_ref, start), NT)
        cos, sin = phase_block(phase_ref, start)
        for parent in range(3):
            a = jnp.zeros((8, 256), F32)
            b = jnp.zeros((8, 256), F32)
            for child in range(8):
                row = leaf_row(child, parent)
                part = leaf[row : row + 8]
                a = a + cos[child : child + 1] * part
                b = b + sin[child : child + 1] * part
            for pair in range(2):
                lanes = slice(pair * 128, pair * 128 + 128)
                block = swap_bits(a[:, lanes] + times_i(b[:, lanes]))
                d = step * 2 + pair
                out_ref[d, parent] = block[:4]
                out_ref[16 + d, parent] = block[4:]


def disaggregate_kernel(in_ref, rad_ref, phase_ref, near_ref, out_ref, acc_ref):
    acc_ref[...] = near_ref[...]

    @pl.loop(0, 8)
    def _(step):
        start = pl.multiple_of(step * 128, 128)
        cos, sin = phase_block(phase_ref, start)
        parents = []
        for parent in range(3):
            halves = []
            for pair in range(2):
                d = step * 2 + pair
                block = jnp.concatenate([in_ref[d, parent], in_ref[16 + d, parent]], axis=0)
                halves.append(swap_bits(block))
            turned = jnp.concatenate([times_i(h) for h in halves], axis=1)
            parents.append((jnp.concatenate(halves, axis=1), turned))
        rows = [None] * 24
        for parent in range(3):
            plain, turned = parents[parent]
            for child in range(8):
                rows[leaf_row(child, parent) // 8] = (
                    cos[child : child + 1] * plain - sin[child : child + 1] * turned
                )
        children = split(jnp.concatenate(rows, axis=0))
        acc_ref[...] += dot3(children, radiation_block(rad_ref, start), NN)

    rows = acc_ref.shape[0]
    out_ref[pl.ds(0, rows, stride=2), :] = acc_ref[:, :128]
    out_ref[pl.ds(1, rows, stride=2), :] = acc_ref[:, 128:]


def near_kernel(own_ref, left_ref, right_ref, down_ref, up_ref, tiles_ref, out_ref, hi_ref, lo_ref, acc_ref):
    def put(ref, at_row, to_x, to_y):
        x = jnp.concatenate(
            [ref[pl.ds(at_row * 96, 48, stride=2), :], ref[pl.ds(at_row * 96 + 1, 48, stride=2), :]],
            axis=1,
        )
        hi, lo = split(x)
        hi_ref[to_x, to_y] = hi
        lo_ref[to_x, to_y] = lo

    for i in range(2):
        for j in range(2):
            put(own_ref, i * 2 + j, 1 + i, 1 + j)
        put(left_ref, i, 0, 1 + i)
        put(right_ref, i, 3, 1 + i)
    for i in range(4):
        put(down_ref, i, i, 0)
        put(up_ref, i, i, 3)
    acc_ref[...] = jnp.zeros_like(acc_ref)

    @pl.loop(0, 9)
    def _(step):
        dx = step // 3
        dy = step - dx * 3
        hi = hi_ref[pl.ds(dx, 2), pl.ds(dy, 2)].reshape(192, 256)
        lo = lo_ref[pl.ds(dx, 2), pl.ds(dy, 2)].reshape(192, 256)
        for dz in range(3):
            re = tiles_ref[step * 3 + dz, 0]
            im = tiles_ref[step * 3 + dz, 1]
            matrix = jnp.concatenate(
                [jnp.concatenate([re, -im], axis=1), jnp.concatenate([im, re], axis=1)], axis=0
            )
            y = dot3((hi, lo), split(matrix), NT).reshape(4, 48, 256)
            if dz == 0:
                acc_ref[:, 8:48] += y[:, 0:40]
            elif dz == 1:
                acc_ref[...] += y
            else:
                acc_ref[:, 0:40] += y[:, 8:48]

    out_ref[...] = acc_ref[...].reshape(192, 256)


def translate_kernel(words_ref, table_ref, src_ref, keep_ref, swap_ref, far_ref, acc_ref):
    acc_ref[...] = jnp.zeros_like(acc_ref)
    row = lax.broadcasted_iota(jnp.int32, (8, 128), 0)

    @pl.loop(0, 96)
    def _(s):
        part = src_ref[s]
        both = jnp.concatenate([part, part], axis=0)
        both = jnp.where(row < 4, both, times_i(both))
        slots, sums = [], []
        for f in range(16):
            word = words_ref[s * 16 + f]
            slot = word >> 9
            kind = word & 511
            slots.append(slot)
            sums.append(acc_ref[slot] + table_ref[kind] * both)
        for f in range(16):
            acc_ref[slots[f]] = sums[f]

    for ref, base in ((keep_ref, 0), (swap_ref, 288)):
        for block in range(3):
            part = acc_ref[pl.ds(base + block * 96, 96)]
            ref[block] = part[:, :4] + part[:, 4:]
    part = acc_ref[pl.ds(576, 96)]
    far_ref[...] = part[:, :4] + part[:, 4:]


def fold_kernel(keep_ref, got_ref, back_ref, mid_ref, ahead_ref):
    back_ref[...] = keep_ref[0] + got_ref[0]
    mid_ref[...] = keep_ref[1] + got_ref[1]
    ahead_ref[...] = keep_ref[2] + got_ref[2]


def call(kernel, out_shape, scratch=(), in_specs=None, flops=0, moved=0):
    extra = {} if in_specs is None else {"in_specs": in_specs}
    return pl.pallas_call(
        kernel,
        out_shape=out_shape,
        scratch_shapes=list(scratch),
        compiler_params=pltpu.CompilerParams(vmem_limit_bytes=VMEM_BYTES),
        cost_estimate=pl.CostEstimate(flops=flops, bytes_accessed=moved, transcendentals=0),
        **extra,
    )


def f32(*shape):
    return jax.ShapeDtypeStruct(shape, F32)


def pair_words(far_targets, far_offsets):
    slab = lax.axis_index("slab")
    ring = slab % 8
    y, core = ring // 2, ring % 2
    targets = lax.dynamic_slice_in_dim(far_targets.reshape(2, 8, 48, 16), ring, 1, 1)
    kinds = lax.dynamic_slice_in_dim(far_offsets.reshape(2, 8, 48, 16), ring, 1, 1)
    to_slab, row = targets // 48, targets % 48
    half, to_ring = to_slab // 8, to_slab % 8
    step = (to_ring // 2 - y + 4) % 4
    near_block = (step + 1) % 4 + jnp.where(to_ring % 2 == core, 0, 3)
    block = jnp.where(step == 2, 6, near_block)
    slot = block * 96 + half * 48 + row
    return (slot * 512 + kinds).reshape(-1)


def operator_table(translators):
    count = translators.shape[0]
    half = lax.axis_index("slab") // 8
    own = lax.dynamic_slice_in_dim(translators, half * 32, 32, 2)
    lanes = jnp.concatenate([own] * 4, axis=2)
    return jnp.broadcast_to(lanes[:, :, None, :], (count, 2, 4, 128)).reshape(count, 8, 128)


def moved_by(block, move):
    return lax.ppermute(block, AXES, route_of(move))


def spread(block, groups):
    return lax.all_to_all(
        block, AXES, split_axis=0, concat_axis=0, axis_index_groups=groups, tiled=True
    )


def halo(currents):
    def along_slab(block, distance):
        return lax.ppermute(
            block, "slab", [(i, i + distance) for i in range(16) if 0 <= i + distance < 16]
        )

    def along_dir(block, distance):
        return lax.ppermute(
            block, "dir", [(i, i + distance) for i in range(16) if 0 <= i + distance < 16]
        )

    left = along_slab(currents[1:2], 1)
    right = along_slab(currents[0:1], -1)
    tall = jnp.concatenate([left, currents, right], axis=0)
    down = along_dir(tall[:, 1:2], 1)
    up = along_dir(tall[:, 0:1], -1)
    return left, right, down, up


def per_device(currents, near_tiles, radiation, child_phase, translators, far_targets, far_offsets):
    groups = exchange_groups()
    rows = currents.reshape(384, 128)
    words = pair_words(far_targets, far_offsets)
    table = operator_table(translators)

    patterns = call(
        aggregate_kernel, f32(32, 3, 4, 128), flops=600_000_000, moved=2_000_000
    )(rows, radiation, child_phase)
    moved = spread(patterns, groups)

    left, right, down, up = halo(currents)
    near = call(
        near_kernel,
        f32(192, 256),
        [pltpu.VMEM((4, 4, 48, 256), BF16), pltpu.VMEM((4, 4, 48, 256), BF16), pltpu.VMEM((4, 48, 256), F32)],
        flops=2_000_000_000,
        moved=5_000_000,
    )(
        rows,
        left.reshape(192, 128),
        right.reshape(192, 128),
        down.reshape(384, 128),
        up.reshape(384, 128),
        near_tiles,
    )

    vmem = pl.BlockSpec(memory_space=pltpu.VMEM)
    keep, swap, far = call(
        translate_kernel,
        (f32(3, 96, 4, 128), f32(3, 96, 4, 128), f32(96, 4, 128)),
        [pltpu.VMEM((672, 8, 128), F32)],
        in_specs=[pl.BlockSpec(memory_space=pltpu.SMEM), vmem, vmem],
        flops=100_000_000,
        moved=3_000_000,
    )(words, table, moved.reshape(96, 4, 128))
    far_in = moved_by(far, lambda z_hi, y, core, d: (z_hi, (y + 2) % 4, 1 - core, d))
    swap_in = moved_by(swap, lambda z_hi, y, core, d: (z_hi, y, 1 - core, d))
    back, mid, ahead = call(
        fold_kernel, (f32(96, 4, 128), f32(96, 4, 128), f32(96, 4, 128)), flops=1_000_000, moved=2_000_000
    )(keep, swap_in)
    back_in = moved_by(back, lambda z_hi, y, core, d: (z_hi, (y + 3) % 4, core, d))
    ahead_in = moved_by(ahead, lambda z_hi, y, core, d: (z_hi, (y + 1) % 4, core, d))
    incoming = (mid + far_in) + (back_in + ahead_in)
    returned = spread(incoming.reshape(32, 3, 4, 128), groups)

    applied = call(
        disaggregate_kernel,
        f32(384, 128),
        [pltpu.VMEM((192, 256), F32)],
        flops=600_000_000,
        moved=2_000_000,
    )(returned, radiation, child_phase, near)
    return applied.reshape(currents.shape)


def solution(mesh):
    in_specs = (
        P("slab", "dir", None, None, None, None),
        P(),
        P(),
        P(),
        P(None, None, "dir"),
        P(),
        P(),
    )
    out_specs = P("slab", "dir", None, None, None, None)
    return jax.shard_map(
        per_device, mesh=mesh, in_specs=in_specs, out_specs=out_specs, check_vma=False
    )
```

```python
import functools

import jax
import jax.numpy as jnp
from jax import lax
from jax.experimental import pallas as pl
from jax.experimental.pallas import tpu as pltpu
from jax.sharding import PartitionSpec as P

F32 = jnp.float32
BF16 = jnp.bfloat16
AXES = ("slab", "dir")
VMEM_BYTES = 32 * 1024 * 1024
NT = (((1,), (1,)), ((), ()))
NN = (((1,), (0,)), ((), ()))


def linear(z_hi, y, core, d):
    return (z_hi * 8 + y * 2 + core) * 16 + d


def route_of(move):
    pairs = []
    for s in range(16):
        for d in range(16):
            to = move(s // 8, s // 2 % 4, s % 2, d)
            if to is not None:
                pairs.append((s * 16 + d, linear(*to)))
    return pairs


def exchange_groups():
    return [
        [linear(z_hi, j // 2, j % 2, d) for z_hi in range(2) for d in range(16)] for j in range(8)
    ]


def split(x):
    hi = x.astype(BF16)
    lo = (x - hi.astype(F32)).astype(BF16)
    return hi, lo


def dot3(a, b, dims):
    a_hi, a_lo = a
    b_hi, b_lo = b
    dot = functools.partial(lax.dot_general, dimension_numbers=dims, preferred_element_type=F32)
    return dot(a_hi, b_hi) + (dot(a_lo, b_hi) + dot(a_hi, b_lo))


def lane_sign(shape):
    lane = lax.broadcasted_iota(jnp.int32, shape, len(shape) - 1) % 128
    return jnp.where(lane < 64, -1.0, 1.0).astype(F32)


def times_i(x):
    return lane_sign(x.shape) * pltpu.roll(x, 64, 1)


def swap_bits(x):
    row = lax.broadcasted_iota(jnp.int32, x.shape, 0) // 4 % 2
    lane = lax.broadcasted_iota(jnp.int32, x.shape, 1) // 32 % 2
    other = pltpu.roll(x, 4, 0)
    moved = jnp.where(lane == 1, pltpu.roll(other, 32, 1), pltpu.roll(other, 96, 1))
    return jnp.where(row == lane, x, moved)


def radiation_copy(rad_hbm, rad_ref, sems, i):
    block = pl.ds(pl.multiple_of(i * 256, 256), 256)
    return pltpu.make_async_copy(rad_hbm.at[:, block], rad_ref.at[:, block], sems.at[i])


def tiles_copy(tiles_hbm, tiles_ref, sems, i):
    block = pl.ds(i * 9, 9)
    return pltpu.make_async_copy(tiles_hbm.at[block], tiles_ref.at[block], sems.at[i])


def radiation_block(rad_ref, start):
    re = rad_ref[0, pl.ds(start, 128), :]
    im = rad_ref[1, pl.ds(start, 128), :]
    top = jnp.concatenate([re, -im], axis=1)
    low = jnp.concatenate([im, re], axis=1)
    return split(jnp.concatenate([top[:64], low[:64], top[64:], low[64:]], axis=0))


def phase_block(phase_ref, start):
    phase = phase_ref[:, pl.ds(start, 128)]
    lane = lax.broadcasted_iota(jnp.int32, phase.shape, 1)

    def doubled(v):
        turned = pltpu.roll(v, 64, 1)
        return jnp.concatenate(
            [jnp.where(lane < 64, v, turned), jnp.where(lane < 64, turned, v)], axis=1
        )

    return doubled(jnp.cos(phase)), doubled(jnp.sin(phase))


def leaf_row(child, parent):
    i, j, l = child // 4, child // 2 % 2, child % 2
    return ((i * 2 + j) * 6 + parent * 2 + l) * 8


def aggregate_kernel(
    core_ref, cur_ref, rad_hbm, phase_ref, out_ref, beside_ref, away_ref, rad_ref, sems,
    unroll=4, groups=(4, 4),
):
    core = core_ref[0]
    beside_ref[...] = cur_ref[pl.ds(pl.multiple_of((1 - core) * 192, 8), 192), :]
    away_ref[...] = cur_ref[pl.ds(pl.multiple_of(core * 192, 8), 192), :]
    for i in range(4):
        radiation_copy(rad_hbm, rad_ref, sems, i).start()
    rows = cur_ref.shape[0] // 2
    x = jnp.concatenate(
        [cur_ref[pl.ds(0, rows, stride=2), :], cur_ref[pl.ds(1, rows, stride=2), :]], axis=1
    )
    x = split(x)

    def directions(step, carry):
        start = pl.multiple_of(step * 128, 128)
        leaf = dot3(x, radiation_block(rad_ref, start), NT)
        cos, sin = phase_block(phase_ref, start)
        for parent in range(3):
            a = jnp.zeros((8, 256), F32)
            b = jnp.zeros((8, 256), F32)
            for child in range(8):
                row = leaf_row(child, parent)
                part = leaf[row : row + 8]
                a = a + cos[child : child + 1] * part
                b = b + sin[child : child + 1] * part
            for pair in range(2):
                lanes = slice(pair * 128, pair * 128 + 128)
                block = swap_bits(a[:, lanes] + times_i(b[:, lanes]))
                d = step * 2 + pair
                out_ref[d, parent] = block[:4]
                out_ref[16 + d, parent] = block[4:]
        return carry

    first = 0
    for count in groups:
        for i in range(first // 2, (first + count) // 2):
            radiation_copy(rad_hbm, rad_ref, sems, i).wait()
        lax.fori_loop(first, first + count, directions, 0, unroll=unroll)
        first += count


def disaggregate_kernel(in_ref, rad_ref, phase_ref, near_ref, out_ref, acc_ref, unroll=4):
    acc_ref[...] = near_ref[...]

    def directions(step, carry):
        start = pl.multiple_of(step * 128, 128)
        cos, sin = phase_block(phase_ref, start)
        parents = []
        for parent in range(3):
            halves = []
            for pair in range(2):
                d = step * 2 + pair
                block = jnp.concatenate([in_ref[d, parent], in_ref[16 + d, parent]], axis=0)
                halves.append(swap_bits(block))
            turned = jnp.concatenate([times_i(h) for h in halves], axis=1)
            parents.append((jnp.concatenate(halves, axis=1), turned))
        rows = [None] * 24
        for parent in range(3):
            plain, turned = parents[parent]
            for child in range(8):
                rows[leaf_row(child, parent) // 8] = (
                    cos[child : child + 1] * plain - sin[child : child + 1] * turned
                )
        children = split(jnp.concatenate(rows, axis=0))
        acc_ref[...] += dot3(children, radiation_block(rad_ref, start), NN)
        return carry

    lax.fori_loop(0, 8, directions, 0, unroll=unroll)
    rows = acc_ref.shape[0]
    out_ref[pl.ds(0, rows, stride=2), :] = acc_ref[:, :128]
    out_ref[pl.ds(1, rows, stride=2), :] = acc_ref[:, 128:]


def near_kernel(
    core_ref, own_ref, beside_ref, away_ref, down_ref, up_ref, tiles_hbm,
    out_ref, tiles_ref, hi_ref, lo_ref, acc_ref, sems,
):
    for i in range(3):
        tiles_copy(tiles_hbm, tiles_ref, sems, i).start()
    to_beside = jnp.where(core_ref[0] == 0, 3, 0)
    to_away = 3 - to_beside

    def put(ref, at_row, to_x, to_y):
        x = jnp.concatenate(
            [ref[pl.ds(at_row * 96, 48, stride=2), :], ref[pl.ds(at_row * 96 + 1, 48, stride=2), :]],
            axis=1,
        )
        hi, lo = split(x)
        hi_ref[to_x, to_y] = hi
        lo_ref[to_x, to_y] = lo

    for i in range(2):
        for j in range(2):
            put(own_ref, i * 2 + j, 1 + i, 1 + j)
        put(beside_ref, i, to_beside, 1 + i)
        put(away_ref, i, to_away, 1 + i)
    for i, to_x in enumerate((1, 2, to_beside, to_away)):
        put(down_ref, i, to_x, 0)
        put(up_ref, i, to_x, 3)
    acc_ref[...] = jnp.zeros_like(acc_ref)

    @pl.loop(0, 3)
    def _(dx):
        tiles_copy(tiles_hbm, tiles_ref, sems, dx).wait()
        for dy in range(3):
            hi = hi_ref[pl.ds(dx, 2), dy : dy + 2].reshape(192, 256)
            lo = lo_ref[pl.ds(dx, 2), dy : dy + 2].reshape(192, 256)
            for dz in range(3):
                re = tiles_ref[dx * 9 + dy * 3 + dz, 0]
                im = tiles_ref[dx * 9 + dy * 3 + dz, 1]
                matrix = jnp.concatenate(
                    [jnp.concatenate([re, -im], axis=1), jnp.concatenate([im, re], axis=1)], axis=0
                )
                y = dot3((hi, lo), split(matrix), NT).reshape(4, 48, 256)
                if dz == 0:
                    acc_ref[:, 8:48] += y[:, 0:40]
                elif dz == 1:
                    acc_ref[...] += y
                else:
                    acc_ref[:, 0:40] += y[:, 8:48]

    out_ref[...] = acc_ref[...].reshape(192, 256)


def translate_kernel(
    slots_ref, kinds_ref, table_ref, src_ref, beside_ref, away_ref,
    keep_ref, swap_ref, far_ref, acc_ref,
):
    acc_ref[...] = jnp.zeros_like(acc_ref)
    row = lax.broadcasted_iota(jnp.int32, (8, 128), 0)

    def tile(first):
        return pl.ds(pl.multiple_of(first, 8), 8)

    def source(s, carry):
        part = src_ref[s]
        both = jnp.concatenate([part, part], axis=0)
        both = jnp.where(row < 4, both, times_i(both))
        slots, sums = [], []
        for f in range(16):
            slot = slots_ref[s * 16 + f]
            slots.append(slot)
            kind = kinds_ref[s * 16 + f]
            sums.append(acc_ref[tile(slot), :] + table_ref[tile(kind), :] * both)
        for f in range(16):
            acc_ref[tile(slots[f]), :] = sums[f]
        return carry

    lax.fori_loop(0, 96, source, 0, unroll=4)

    def folded(block):
        part = acc_ref[pl.ds(block * 768, 768), :].reshape(96, 8, 128)
        return part[:, :4] + part[:, 4:]

    for block in range(3):
        keep_ref[block] = folded(block)
        swap_ref[block] = folded(block + 3)
    far_ref[...] = folded(6)


def fold_kernel(
    keep_ref, got_ref, cur_ref, beside_ref, away_ref,
    back_ref, mid_ref, ahead_ref, down_ref, up_ref,
):
    back_ref[...] = keep_ref[0] + got_ref[0]
    mid_ref[...] = keep_ref[1] + got_ref[1]
    ahead_ref[...] = keep_ref[2] + got_ref[2]
    for ref, j in ((down_ref, 1), (up_ref, 0)):
        for i in range(2):
            ref[pl.ds(i * 96, 96), :] = cur_ref[pl.ds(i * 192 + j * 96, 96), :]
        ref[pl.ds(192, 96), :] = beside_ref[pl.ds(j * 96, 96), :]
        ref[pl.ds(288, 96), :] = away_ref[pl.ds(j * 96, 96), :]


def join_kernel(mid_ref, far_ref, back_ref, ahead_ref, down_ref, up_ref, out_ref):
    out_ref[...] = (mid_ref[...] + far_ref[...]) + (back_ref[...] + ahead_ref[...])


def call(kernel, out_shape, scratch=(), in_specs=None, flops=0, moved=0, vmem_bytes=VMEM_BYTES):
    extra = {} if in_specs is None else {"in_specs": in_specs}
    return pl.pallas_call(
        kernel,
        out_shape=out_shape,
        scratch_shapes=list(scratch),
        compiler_params=pltpu.CompilerParams(vmem_limit_bytes=vmem_bytes),
        cost_estimate=pl.CostEstimate(flops=flops, bytes_accessed=moved, transcendentals=0),
        **extra,
    )


def f32(*shape):
    return jax.ShapeDtypeStruct(shape, F32)


def pair_words(far_targets, far_offsets):
    slab = lax.axis_index("slab")
    ring = slab % 8
    y, core = ring // 2, ring % 2
    targets = lax.dynamic_slice_in_dim(far_targets.reshape(2, 8, 48, 16), ring, 1, 1)
    kinds = lax.dynamic_slice_in_dim(far_offsets.reshape(2, 8, 48, 16), ring, 1, 1)
    to_slab, row = targets // 48, targets % 48
    half, to_ring = to_slab // 8, to_slab % 8
    step = (to_ring // 2 - y + 4) % 4
    near_block = (step + 1) % 4 + jnp.where(to_ring % 2 == core, 0, 3)
    block = jnp.where(step == 2, 6, near_block)
    slot = block * 96 + half * 48 + row
    return (slot * 8).reshape(-1), (kinds * 8).reshape(-1)


def operator_table(translators):
    count = translators.shape[0]
    half = lax.axis_index("slab") // 8
    own = lax.dynamic_slice_in_dim(translators, half * 32, 32, 2)
    lanes = jnp.concatenate([own] * 4, axis=2)
    return jnp.broadcast_to(lanes[:, :, None, :], (count, 2, 4, 128)).reshape(count * 8, 128)


def moved_by(block, move):
    return lax.ppermute(block, AXES, route_of(move))


def spread(block, groups):
    return lax.all_to_all(
        block, AXES, split_axis=0, concat_axis=0, axis_index_groups=groups, tiled=True
    )


def per_device(currents, near_tiles, radiation, child_phase, translators, far_targets, far_offsets):
    groups = exchange_groups()
    rows = currents.reshape(384, 128)
    core = (lax.axis_index("slab") % 2).astype(jnp.int32).reshape(1)
    slots, kinds = pair_words(far_targets, far_offsets)
    table = operator_table(translators)
    vmem = pl.BlockSpec(memory_space=pltpu.VMEM)
    smem = pl.BlockSpec(memory_space=pltpu.SMEM)
    hbm = pl.BlockSpec(memory_space=pl.ANY)

    patterns, beside, away = call(
        aggregate_kernel,
        (f32(32, 3, 4, 128), f32(192, 128), f32(192, 128)),
        [pltpu.VMEM((2, 1024, 128), F32), pltpu.SemaphoreType.DMA((4,))],
        in_specs=[smem, vmem, hbm, vmem],
        flops=600_000_000,
        moved=2_000_000,
        vmem_bytes=62 * 1024 * 1024,
    )(core, rows, radiation, child_phase)
    moved = spread(patterns, groups)
    beside = moved_by(beside, lambda z_hi, y, core, d: (z_hi, y, 1 - core, d))
    away = lax.ppermute(
        away, "slab", [(s, s + 2 * (s % 2) - 1) for s in range(16) if 0 <= s + 2 * (s % 2) - 1 < 16]
    )

    keep, swap, far = call(
        translate_kernel,
        (f32(3, 96, 4, 128), f32(3, 96, 4, 128), f32(96, 4, 128)),
        [pltpu.VMEM((5376, 128), F32)],
        in_specs=[smem, smem, vmem, vmem, hbm, hbm],
        flops=100_000_000,
        moved=3_000_000,
    )(slots, kinds, table, moved.reshape(96, 4, 128), beside, away)
    far_in = moved_by(far, lambda z_hi, y, core, d: (z_hi, (y + 2) % 4, 1 - core, d))
    swap_in = moved_by(swap, lambda z_hi, y, core, d: (z_hi, y, 1 - core, d))
    back, mid, ahead, down, up = call(
        fold_kernel,
        (f32(96, 4, 128),) * 3 + (f32(384, 128),) * 2,
        flops=1_000_000,
        moved=2_000_000,
    )(keep, swap_in, rows, beside, away)
    back_in = moved_by(back, lambda z_hi, y, core, d: (z_hi, (y + 3) % 4, core, d))
    ahead_in = moved_by(ahead, lambda z_hi, y, core, d: (z_hi, (y + 1) % 4, core, d))
    down = lax.ppermute(down, "dir", [(d, d + 1) for d in range(15)])
    up = lax.ppermute(up, "dir", [(d + 1, d) for d in range(15)])
    incoming = call(
        join_kernel,
        f32(96, 4, 128),
        in_specs=[vmem] * 4 + [hbm] * 2,
        flops=1_000_000,
        moved=1_000_000,
    )(mid, far_in, back_in, ahead_in, down, up)
    returned = spread(incoming.reshape(32, 3, 4, 128), groups)

    near = call(
        near_kernel,
        f32(192, 256),
        [
            pltpu.VMEM((27, 2, 128, 128), F32),
            pltpu.VMEM((4, 4, 48, 256), BF16),
            pltpu.VMEM((4, 4, 48, 256), BF16),
            pltpu.VMEM((4, 48, 256), F32),
            pltpu.SemaphoreType.DMA((3,)),
        ],
        in_specs=[smem] + [vmem] * 5 + [hbm],
        flops=2_000_000_000,
        moved=5_000_000,
        vmem_bytes=50 * 1024 * 1024,
    )(core, rows, beside, away, down, up, near_tiles)

    applied = call(
        disaggregate_kernel,
        f32(384, 128),
        [pltpu.VMEM((192, 256), F32)],
        flops=600_000_000,
        moved=2_000_000,
    )(returned, radiation, child_phase, near)
    return applied.reshape(currents.shape)


def solution(mesh):
    in_specs = (
        P("slab", "dir", None, None, None, None),
        P(),
        P(),
        P(),
        P(None, None, "dir"),
        P(),
        P(),
    )
    out_specs = P("slab", "dir", None, None, None, None)
    return jax.shard_map(
        per_device, mesh=mesh, in_specs=in_specs, out_specs=out_specs, check_vma=False
    )
```

```python
import functools

import jax
import jax.numpy as jnp
from jax import lax
from jax.experimental import pallas as pl
from jax.experimental.pallas import tpu as pltpu
from jax.sharding import PartitionSpec as P

F32 = jnp.float32
BF16 = jnp.bfloat16
AXES = ("slab", "dir")
VMEM_BYTES = 32 * 1024 * 1024
NT = (((1,), (1,)), ((), ()))
NN = (((1,), (0,)), ((), ()))


def linear(z_hi, y, core, d):
    return (z_hi * 8 + y * 2 + core) * 16 + d


def route_of(move):
    pairs = []
    for s in range(16):
        for d in range(16):
            to = move(s // 8, s // 2 % 4, s % 2, d)
            if to is not None:
                pairs.append((s * 16 + d, linear(*to)))
    return pairs


def exchange_groups():
    return [
        [linear(z_hi, j // 2, j % 2, d) for z_hi in range(2) for d in range(16)] for j in range(8)
    ]


def split(x):
    hi = x.astype(BF16)
    lo = (x - hi.astype(F32)).astype(BF16)
    return hi, lo


def dot3(a, b, dims):
    a_hi, a_lo = a
    b_hi, b_lo = b
    dot = functools.partial(lax.dot_general, dimension_numbers=dims, preferred_element_type=F32)
    return dot(a_hi, b_hi) + (dot(a_lo, b_hi) + dot(a_hi, b_lo))


def lane_sign(shape):
    lane = lax.broadcasted_iota(jnp.int32, shape, len(shape) - 1) % 128
    return jnp.where(lane < 64, -1.0, 1.0).astype(F32)


def times_i(x):
    return lane_sign(x.shape) * pltpu.roll(x, 64, 1)


def swap_bits(x):
    row = lax.broadcasted_iota(jnp.int32, x.shape, 0) // 4 % 2
    lane = lax.broadcasted_iota(jnp.int32, x.shape, 1) // 32 % 2
    other = pltpu.roll(x, 4, 0)
    moved = jnp.where(lane == 1, pltpu.roll(other, 32, 1), pltpu.roll(other, 96, 1))
    return jnp.where(row == lane, x, moved)


def radiation_copy(rad_hbm, rad_ref, sems, i):
    block = pl.ds(pl.multiple_of(i * 256, 256), 256)
    return pltpu.make_async_copy(rad_hbm.at[:, block], rad_ref.at[:, block], sems.at[i])


def tiles_copy(tiles_hbm, tiles_ref, sems, i):
    block = pl.ds(i * 9, 9)
    return pltpu.make_async_copy(tiles_hbm.at[block], tiles_ref.at[block], sems.at[i])


def radiation_block(rad_ref, start):
    re = rad_ref[0, pl.ds(start, 128), :]
    im = rad_ref[1, pl.ds(start, 128), :]
    top = jnp.concatenate([re, -im], axis=1)
    low = jnp.concatenate([im, re], axis=1)
    return split(jnp.concatenate([top[:64], low[:64], top[64:], low[64:]], axis=0))


def phase_block(phase_ref, start):
    phase = phase_ref[:, pl.ds(start, 128)]
    lane = lax.broadcasted_iota(jnp.int32, phase.shape, 1)

    def doubled(v):
        turned = pltpu.roll(v, 64, 1)
        return jnp.concatenate(
            [jnp.where(lane < 64, v, turned), jnp.where(lane < 64, turned, v)], axis=1
        )

    return doubled(jnp.cos(phase)), doubled(jnp.sin(phase))


def leaf_row(child, parent):
    i, j, l = child // 4, child // 2 % 2, child % 2
    return ((i * 2 + j) * 6 + parent * 2 + l) * 8


def aggregate_kernel(
    cur_ref, rad_hbm, phase_ref, out_ref, down_ref, up_ref, rad_ref, sems, unroll=4, groups=(4, 4)
):
    for i in range(4):
        radiation_copy(rad_hbm, rad_ref, sems, i).start()
    for i in range(2):
        down_ref[pl.ds(i * 96, 96), :] = cur_ref[pl.ds(i * 192 + 96, 96), :]
        up_ref[pl.ds(i * 96, 96), :] = cur_ref[pl.ds(i * 192, 96), :]
    rows = cur_ref.shape[0] // 2
    x = jnp.concatenate(
        [cur_ref[pl.ds(0, rows, stride=2), :], cur_ref[pl.ds(1, rows, stride=2), :]], axis=1
    )
    x = split(x)

    def directions(step, carry):
        start = pl.multiple_of(step * 128, 128)
        leaf = dot3(x, radiation_block(rad_ref, start), NT)
        cos, sin = phase_block(phase_ref, start)
        for parent in range(3):
            a = jnp.zeros((8, 256), F32)
            b = jnp.zeros((8, 256), F32)
            for child in range(8):
                row = leaf_row(child, parent)
                part = leaf[row : row + 8]
                a = a + cos[child : child + 1] * part
                b = b + sin[child : child + 1] * part
            for pair in range(2):
                lanes = slice(pair * 128, pair * 128 + 128)
                block = swap_bits(a[:, lanes] + times_i(b[:, lanes]))
                d = step * 2 + pair
                out_ref[d, parent] = block[:4]
                out_ref[16 + d, parent] = block[4:]
        return carry

    first = 0
    for count in groups:
        for i in range(first // 2, (first + count) // 2):
            radiation_copy(rad_hbm, rad_ref, sems, i).wait()
        lax.fori_loop(first, first + count, directions, 0, unroll=unroll)
        first += count


def disaggregate_kernel(in_ref, rad_ref, phase_ref, near_ref, out_ref, acc_ref, unroll=4):
    acc_ref[...] = near_ref[...]

    def directions(step, carry):
        start = pl.multiple_of(step * 128, 128)
        cos, sin = phase_block(phase_ref, start)
        parents = []
        for parent in range(3):
            halves = []
            for pair in range(2):
                d = step * 2 + pair
                block = jnp.concatenate([in_ref[d, parent], in_ref[16 + d, parent]], axis=0)
                halves.append(swap_bits(block))
            turned = jnp.concatenate([times_i(h) for h in halves], axis=1)
            parents.append((jnp.concatenate(halves, axis=1), turned))
        rows = [None] * 24
        for parent in range(3):
            plain, turned = parents[parent]
            for child in range(8):
                rows[leaf_row(child, parent) // 8] = (
                    cos[child : child + 1] * plain - sin[child : child + 1] * turned
                )
        children = split(jnp.concatenate(rows, axis=0))
        acc_ref[...] += dot3(children, radiation_block(rad_ref, start), NN)
        return carry

    lax.fori_loop(0, 8, directions, 0, unroll=unroll)
    rows = acc_ref.shape[0]
    out_ref[pl.ds(0, rows, stride=2), :] = acc_ref[:, :128]
    out_ref[pl.ds(1, rows, stride=2), :] = acc_ref[:, 128:]


def near_kernel(
    core_ref, own_ref, beside_ref, away_ref, down_ref, up_ref, tiles_hbm,
    out_ref, tiles_ref, hi_ref, lo_ref, acc_ref, sems,
):
    for i in range(3):
        tiles_copy(tiles_hbm, tiles_ref, sems, i).start()
    to_beside = jnp.where(core_ref[0] == 0, 3, 0)
    to_away = 3 - to_beside

    def put(ref, at_row, to_x, to_y):
        x = jnp.concatenate(
            [ref[pl.ds(at_row * 96, 48, stride=2), :], ref[pl.ds(at_row * 96 + 1, 48, stride=2), :]],
            axis=1,
        )
        hi, lo = split(x)
        hi_ref[to_x, to_y] = hi
        lo_ref[to_x, to_y] = lo

    for i in range(2):
        for j in range(2):
            put(own_ref, i * 2 + j, 1 + i, 1 + j)
        put(down_ref, i, 1 + i, 0)
        put(up_ref, i, 1 + i, 3)
    for i, to_y in enumerate((1, 2, 0, 3)):
        put(beside_ref, i, to_beside, to_y)
        put(away_ref, i, to_away, to_y)
    acc_ref[...] = jnp.zeros_like(acc_ref)

    @pl.loop(0, 3)
    def _(dx):
        tiles_copy(tiles_hbm, tiles_ref, sems, dx).wait()
        for dy in range(3):
            hi = hi_ref[pl.ds(dx, 2), dy : dy + 2].reshape(192, 256)
            lo = lo_ref[pl.ds(dx, 2), dy : dy + 2].reshape(192, 256)
            for dz in range(3):
                re = tiles_ref[dx * 9 + dy * 3 + dz, 0]
                im = tiles_ref[dx * 9 + dy * 3 + dz, 1]
                matrix = jnp.concatenate(
                    [jnp.concatenate([re, -im], axis=1), jnp.concatenate([im, re], axis=1)], axis=0
                )
                y = dot3((hi, lo), split(matrix), NT).reshape(4, 48, 256)
                if dz == 0:
                    acc_ref[:, 8:48] += y[:, 0:40]
                elif dz == 1:
                    acc_ref[...] += y
                else:
                    acc_ref[:, 0:40] += y[:, 8:48]

    out_ref[...] = acc_ref[...].reshape(192, 256)


def translate_kernel(
    slots_ref, kinds_ref, table_ref, src_ref, down_ref, up_ref,
    keep_ref, swap_ref, far_ref, acc_ref,
):
    acc_ref[...] = jnp.zeros_like(acc_ref)
    row = lax.broadcasted_iota(jnp.int32, (8, 128), 0)

    def tile(first):
        return pl.ds(pl.multiple_of(first, 8), 8)

    def source(s, carry):
        part = src_ref[s]
        both = jnp.concatenate([part, part], axis=0)
        both = jnp.where(row < 4, both, times_i(both))
        slots, sums = [], []
        for f in range(16):
            slot = slots_ref[s * 16 + f]
            slots.append(slot)
            kind = kinds_ref[s * 16 + f]
            sums.append(acc_ref[tile(slot), :] + table_ref[tile(kind), :] * both)
        for f in range(16):
            acc_ref[tile(slots[f]), :] = sums[f]
        return carry

    lax.fori_loop(0, 96, source, 0, unroll=4)

    def folded(block):
        part = acc_ref[pl.ds(block * 768, 768), :].reshape(96, 8, 128)
        return part[:, :4] + part[:, 4:]

    for block in range(3):
        keep_ref[block] = folded(block)
        swap_ref[block] = folded(block + 3)
    far_ref[...] = folded(6)


def fold_kernel(
    core_ref, keep_ref, got_ref, cur_ref, down_ref, up_ref,
    back_ref, mid_ref, ahead_ref, beside_ref, away_ref,
):
    back_ref[...] = keep_ref[0] + got_ref[0]
    mid_ref[...] = keep_ref[1] + got_ref[1]
    ahead_ref[...] = keep_ref[2] + got_ref[2]
    core = core_ref[0]
    for ref, row in ((beside_ref, 1 - core), (away_ref, core)):
        ref[pl.ds(0, 192), :] = cur_ref[pl.ds(pl.multiple_of(row * 192, 8), 192), :]
        ref[pl.ds(192, 96), :] = down_ref[pl.ds(pl.multiple_of(row * 96, 8), 96), :]
        ref[pl.ds(288, 96), :] = up_ref[pl.ds(pl.multiple_of(row * 96, 8), 96), :]


def join_kernel(mid_ref, far_ref, back_ref, ahead_ref, beside_ref, away_ref, out_ref):
    out_ref[...] = (mid_ref[...] + far_ref[...]) + (back_ref[...] + ahead_ref[...])


def call(kernel, out_shape, scratch=(), in_specs=None, flops=0, moved=0, vmem_bytes=VMEM_BYTES):
    extra = {} if in_specs is None else {"in_specs": in_specs}
    return pl.pallas_call(
        kernel,
        out_shape=out_shape,
        scratch_shapes=list(scratch),
        compiler_params=pltpu.CompilerParams(vmem_limit_bytes=vmem_bytes),
        cost_estimate=pl.CostEstimate(flops=flops, bytes_accessed=moved, transcendentals=0),
        **extra,
    )


def f32(*shape):
    return jax.ShapeDtypeStruct(shape, F32)


def pair_words(far_targets, far_offsets):
    slab = lax.axis_index("slab")
    ring = slab % 8
    y, core = ring // 2, ring % 2

    def own(table):
        return jnp.concatenate(
            [lax.dynamic_slice_in_dim(table, (ring + z_hi * 8) * 48, 48, 0) for z_hi in range(2)]
        )

    targets, kinds = own(far_targets), own(far_offsets)
    to_slab, row = targets // 48, targets % 48
    half, to_ring = to_slab // 8, to_slab % 8
    step = (to_ring // 2 - y + 4) % 4
    near_block = (step + 1) % 4 + jnp.where(to_ring % 2 == core, 0, 3)
    block = jnp.where(step == 2, 6, near_block)
    slot = block * 96 + half * 48 + row
    return (slot * 8).reshape(-1), (kinds * 8).reshape(-1)


def operator_table(translators):
    count = translators.shape[0]
    half = lax.axis_index("slab") // 8
    own = lax.dynamic_slice_in_dim(translators, half * 32, 32, 2)
    lanes = jnp.concatenate([own] * 4, axis=2)
    return jnp.broadcast_to(lanes[:, :, None, :], (count, 2, 4, 128)).reshape(count * 8, 128)


def moved_by(block, move):
    return lax.ppermute(block, AXES, route_of(move))


def spread(block, groups):
    return lax.all_to_all(
        block, AXES, split_axis=0, concat_axis=0, axis_index_groups=groups, tiled=True
    )


def per_device(currents, near_tiles, radiation, child_phase, translators, far_targets, far_offsets):
    groups = exchange_groups()
    rows = currents.reshape(384, 128)
    core = (lax.axis_index("slab") % 2).astype(jnp.int32).reshape(1)
    slots, kinds = pair_words(far_targets, far_offsets)
    table = operator_table(translators)
    vmem = pl.BlockSpec(memory_space=pltpu.VMEM)
    smem = pl.BlockSpec(memory_space=pltpu.SMEM)
    hbm = pl.BlockSpec(memory_space=pl.ANY)

    patterns, down, up = call(
        aggregate_kernel,
        (f32(32, 3, 4, 128), f32(192, 128), f32(192, 128)),
        [pltpu.VMEM((2, 1024, 128), F32), pltpu.SemaphoreType.DMA((4,))],
        in_specs=[vmem, hbm, vmem],
        flops=600_000_000,
        moved=2_000_000,
        vmem_bytes=62 * 1024 * 1024,
    )(rows, radiation, child_phase)
    moved = spread(patterns, groups)
    down = lax.ppermute(down, "dir", [(d, d + 1) for d in range(15)])
    up = lax.ppermute(up, "dir", [(d + 1, d) for d in range(15)])

    keep, swap, far = call(
        translate_kernel,
        (f32(3, 96, 4, 128), f32(3, 96, 4, 128), f32(96, 4, 128)),
        [pltpu.VMEM((5376, 128), F32)],
        in_specs=[smem, smem, vmem, vmem, hbm, hbm],
        flops=100_000_000,
        moved=3_000_000,
    )(slots, kinds, table, moved.reshape(96, 4, 128), down, up)
    far_in = moved_by(far, lambda z_hi, y, core, d: (z_hi, (y + 2) % 4, 1 - core, d))
    swap_in = moved_by(swap, lambda z_hi, y, core, d: (z_hi, y, 1 - core, d))
    back, mid, ahead, beside, away = call(
        fold_kernel,
        (f32(96, 4, 128),) * 3 + (f32(384, 128),) * 2,
        in_specs=[smem] + [vmem] * 5,
        flops=1_000_000,
        moved=2_000_000,
    )(core, keep, swap_in, rows, down, up)
    back_in = moved_by(back, lambda z_hi, y, core, d: (z_hi, (y + 3) % 4, core, d))
    ahead_in = moved_by(ahead, lambda z_hi, y, core, d: (z_hi, (y + 1) % 4, core, d))
    beside = moved_by(beside, lambda z_hi, y, core, d: (z_hi, y, 1 - core, d))
    away = lax.ppermute(
        away, "slab", [(s, s + 2 * (s % 2) - 1) for s in range(16) if 0 <= s + 2 * (s % 2) - 1 < 16]
    )
    incoming = call(
        join_kernel,
        f32(96, 4, 128),
        in_specs=[vmem] * 4 + [hbm] * 2,
        flops=1_000_000,
        moved=1_000_000,
    )(mid, far_in, back_in, ahead_in, beside, away)
    returned = spread(incoming.reshape(32, 3, 4, 128), groups)

    near = call(
        near_kernel,
        f32(192, 256),
        [
            pltpu.VMEM((27, 2, 128, 128), F32),
            pltpu.VMEM((4, 4, 48, 256), BF16),
            pltpu.VMEM((4, 4, 48, 256), BF16),
            pltpu.VMEM((4, 48, 256), F32),
            pltpu.SemaphoreType.DMA((3,)),
        ],
        in_specs=[smem] + [vmem] * 5 + [hbm],
        flops=2_000_000_000,
        moved=5_000_000,
        vmem_bytes=50 * 1024 * 1024,
    )(core, rows, beside, away, down, up, near_tiles)

    applied = call(
        disaggregate_kernel,
        f32(384, 128),
        [pltpu.VMEM((192, 256), F32)],
        flops=600_000_000,
        moved=2_000_000,
    )(returned, radiation, child_phase, near)
    return applied.reshape(currents.shape)


def solution(mesh):
    in_specs = (
        P("slab", "dir", None, None, None, None),
        P(),
        P(),
        P(),
        P(None, None, "dir"),
        P(),
        P(),
    )
    out_specs = P("slab", "dir", None, None, None, None)
    return jax.shard_map(
        per_device, mesh=mesh, in_specs=in_specs, out_specs=out_specs, check_vma=False
    )
```

```python
import functools

import jax
import jax.numpy as jnp
from jax import lax
from jax.experimental import pallas as pl
from jax.experimental.pallas import tpu as pltpu
from jax.sharding import PartitionSpec as P

F32 = jnp.float32
BF16 = jnp.bfloat16
AXES = ("slab", "dir")
VMEM_BYTES = 32 * 1024 * 1024
NT = (((1,), (1,)), ((), ()))
NN = (((1,), (0,)), ((), ()))


def linear(z_hi, y, core, d):
    return (z_hi * 8 + y * 2 + core) * 16 + d


def route_of(move):
    pairs = []
    for s in range(16):
        for d in range(16):
            to = move(s // 8, s // 2 % 4, s % 2, d)
            if to is not None:
                pairs.append((s * 16 + d, linear(*to)))
    return pairs


def exchange_groups():
    return [
        [linear(z_hi, j // 2, j % 2, d) for z_hi in range(2) for d in range(16)] for j in range(8)
    ]


def split(x):
    hi = x.astype(BF16)
    lo = (x - hi.astype(F32)).astype(BF16)
    return hi, lo


def dot3(a, b, dims):
    a_hi, a_lo = a
    b_hi, b_lo = b
    dot = functools.partial(lax.dot_general, dimension_numbers=dims, preferred_element_type=F32)
    return dot(a_hi, b_hi) + (dot(a_lo, b_hi) + dot(a_hi, b_lo))


def lane_sign(shape):
    lane = lax.broadcasted_iota(jnp.int32, shape, len(shape) - 1) % 128
    return jnp.where(lane < 64, -1.0, 1.0).astype(F32)


def times_i(x):
    return lane_sign(x.shape) * pltpu.roll(x, 64, 1)


def swap_bits(x):
    row = lax.broadcasted_iota(jnp.int32, x.shape, 0) // 4 % 2
    lane = lax.broadcasted_iota(jnp.int32, x.shape, 1) // 32 % 2
    other = pltpu.roll(x, 4, 0)
    moved = jnp.where(lane == 1, pltpu.roll(other, 32, 1), pltpu.roll(other, 96, 1))
    return jnp.where(row == lane, x, moved)


def radiation_copy(rad_hbm, rad_ref, sems, i):
    block = pl.ds(pl.multiple_of(i * 256, 256), 256)
    return pltpu.make_async_copy(rad_hbm.at[:, block], rad_ref.at[:, block], sems.at[i])


def tiles_copy(tiles_hbm, tiles_ref, sems, i):
    block = pl.ds(i * 9, 9)
    return pltpu.make_async_copy(tiles_hbm.at[block], tiles_ref.at[block], sems.at[i])


def radiation_block(rad_ref, start):
    re = rad_ref[0, pl.ds(start, 128), :]
    im = rad_ref[1, pl.ds(start, 128), :]
    top = jnp.concatenate([re, -im], axis=1)
    low = jnp.concatenate([im, re], axis=1)
    return split(jnp.concatenate([top[:64], low[:64], top[64:], low[64:]], axis=0))


def phase_block(phase_ref, start):
    phase = phase_ref[:, pl.ds(start, 128)]
    lane = lax.broadcasted_iota(jnp.int32, phase.shape, 1)

    def doubled(v):
        turned = pltpu.roll(v, 64, 1)
        return jnp.concatenate(
            [jnp.where(lane < 64, v, turned), jnp.where(lane < 64, turned, v)], axis=1
        )

    return doubled(jnp.cos(phase)), doubled(jnp.sin(phase))


def leaf_row(child, parent):
    i, j, l = child // 4, child // 2 % 2, child % 2
    return ((i * 2 + j) * 6 + parent * 2 + l) * 8


def aggregate_kernel(
    cur_ref, rad_hbm, phase_ref, out_ref, down_ref, up_ref, rad_ref, sems, unroll=4, groups=(4, 4)
):
    for i in range(4):
        radiation_copy(rad_hbm, rad_ref, sems, i).start()
    for i in range(2):
        down_ref[pl.ds(i * 96, 96), :] = cur_ref[pl.ds(i * 192 + 96, 96), :]
        up_ref[pl.ds(i * 96, 96), :] = cur_ref[pl.ds(i * 192, 96), :]
    rows = cur_ref.shape[0] // 2
    x = jnp.concatenate(
        [cur_ref[pl.ds(0, rows, stride=2), :], cur_ref[pl.ds(1, rows, stride=2), :]], axis=1
    )
    x = split(x)

    def directions(step, carry):
        start = pl.multiple_of(step * 128, 128)
        leaf = dot3(x, radiation_block(rad_ref, start), NT)
        cos, sin = phase_block(phase_ref, start)
        for parent in range(3):
            a = jnp.zeros((8, 256), F32)
            b = jnp.zeros((8, 256), F32)
            for child in range(8):
                row = leaf_row(child, parent)
                part = leaf[row : row + 8]
                a = a + cos[child : child + 1] * part
                b = b + sin[child : child + 1] * part
            for pair in range(2):
                lanes = slice(pair * 128, pair * 128 + 128)
                block = swap_bits(a[:, lanes] + times_i(b[:, lanes]))
                d = step * 2 + pair
                out_ref[d, parent] = block[:4]
                out_ref[16 + d, parent] = block[4:]
        return carry

    first = 0
    for count in groups:
        for i in range(first // 2, (first + count) // 2):
            radiation_copy(rad_hbm, rad_ref, sems, i).wait()
        lax.fori_loop(first, first + count, directions, 0, unroll=unroll)
        first += count


def disaggregate_kernel(in_ref, rad_ref, phase_ref, near_ref, out_ref, acc_ref, unroll=4):
    acc_ref[...] = near_ref[...]

    def directions(step, carry):
        start = pl.multiple_of(step * 128, 128)
        cos, sin = phase_block(phase_ref, start)
        parents = []
        for parent in range(3):
            halves = []
            for pair in range(2):
                d = step * 2 + pair
                block = jnp.concatenate([in_ref[d, parent], in_ref[16 + d, parent]], axis=0)
                halves.append(swap_bits(block))
            turned = jnp.concatenate([times_i(h) for h in halves], axis=1)
            parents.append((jnp.concatenate(halves, axis=1), turned))
        rows = [None] * 24
        for parent in range(3):
            plain, turned = parents[parent]
            for child in range(8):
                rows[leaf_row(child, parent) // 8] = (
                    cos[child : child + 1] * plain - sin[child : child + 1] * turned
                )
        children = split(jnp.concatenate(rows, axis=0))
        acc_ref[...] += dot3(children, radiation_block(rad_ref, start), NN)
        return carry

    lax.fori_loop(0, 8, directions, 0, unroll=unroll)
    rows = acc_ref.shape[0]
    out_ref[pl.ds(0, rows, stride=2), :] = acc_ref[:, :128]
    out_ref[pl.ds(1, rows, stride=2), :] = acc_ref[:, 128:]


def near_kernel(
    core_ref, own_ref, beside_ref, away_ref, down_ref, up_ref, tiles_hbm,
    out_ref, tiles_ref, hi_ref, lo_ref, acc_ref, sems,
):
    for i in range(3):
        tiles_copy(tiles_hbm, tiles_ref, sems, i).start()
    to_beside = jnp.where(core_ref[0] == 0, 3, 0)
    to_away = 3 - to_beside

    def put(ref, at_row, to_x, to_y):
        x = jnp.concatenate(
            [ref[pl.ds(at_row * 96, 48, stride=2), :], ref[pl.ds(at_row * 96 + 1, 48, stride=2), :]],
            axis=1,
        )
        hi, lo = split(x)
        hi_ref[to_x, to_y] = hi
        lo_ref[to_x, to_y] = lo

    for i in range(2):
        for j in range(2):
            put(own_ref, i * 2 + j, 1 + i, 1 + j)
        put(down_ref, i, 1 + i, 0)
        put(up_ref, i, 1 + i, 3)
    for i, to_y in enumerate((1, 2, 0, 3)):
        put(beside_ref, i, to_beside, to_y)
        put(away_ref, i, to_away, to_y)
    acc_ref[...] = jnp.zeros_like(acc_ref)

    @pl.loop(0, 3)
    def _(dx):
        tiles_copy(tiles_hbm, tiles_ref, sems, dx).wait()
        for dy in range(3):
            hi = hi_ref[pl.ds(dx, 2), dy : dy + 2].reshape(192, 256)
            lo = lo_ref[pl.ds(dx, 2), dy : dy + 2].reshape(192, 256)
            for dz in range(3):
                re = tiles_ref[dx * 9 + dy * 3 + dz, 0]
                im = tiles_ref[dx * 9 + dy * 3 + dz, 1]
                matrix = jnp.concatenate(
                    [jnp.concatenate([re, -im], axis=1), jnp.concatenate([im, re], axis=1)], axis=0
                )
                y = dot3((hi, lo), split(matrix), NT).reshape(4, 48, 256)
                if dz == 0:
                    acc_ref[:, 8:48] += y[:, 0:40]
                elif dz == 1:
                    acc_ref[...] += y
                else:
                    acc_ref[:, 0:40] += y[:, 8:48]

    out_ref[...] = acc_ref[...].reshape(192, 256)


def translate_kernel(
    slots_ref, kinds_ref, table_ref, src_ref, down_ref, up_ref,
    keep_ref, swap_ref, far_ref, acc_ref,
):
    acc_ref[...] = jnp.zeros_like(acc_ref)
    row = lax.broadcasted_iota(jnp.int32, (8, 128), 0)

    def tile(first):
        return pl.ds(pl.multiple_of(first, 8), 8)

    def source(s, carry):
        part = src_ref[s]
        both = jnp.concatenate([part, part], axis=0)
        both = jnp.where(row < 4, both, times_i(both))
        slots, sums = [], []
        for f in range(16):
            slot = slots_ref[s * 16 + f]
            slots.append(slot)
            kind = kinds_ref[s * 16 + f]
            sums.append(acc_ref[tile(slot), :] + table_ref[tile(kind), :] * both)
        for f in range(16):
            acc_ref[tile(slots[f]), :] = sums[f]
        return carry

    lax.fori_loop(0, 96, source, 0, unroll=4)

    def folded(block):
        part = acc_ref[pl.ds(block * 768, 768), :].reshape(96, 8, 128)
        return part[:, :4] + part[:, 4:]

    for block in range(3):
        keep_ref[block] = folded(block)
        swap_ref[block] = folded(block + 3)
    far_ref[...] = folded(6)


def fold_kernel(
    core_ref, keep_ref, got_ref, far_ref, cur_ref, down_ref, up_ref,
    back_ref, mid_ref, ahead_ref, beside_ref, away_ref,
):
    core = core_ref[0]
    far = far_ref[...]
    zero = jnp.zeros_like(far)
    back_ref[...] = keep_ref[0] + got_ref[0] + jnp.where(core == 1, far, zero)
    mid_ref[...] = keep_ref[1] + got_ref[1]
    ahead_ref[...] = keep_ref[2] + got_ref[2] + jnp.where(core == 0, far, zero)
    for ref, row in ((beside_ref, 1 - core), (away_ref, core)):
        ref[pl.ds(0, 192), :] = cur_ref[pl.ds(pl.multiple_of(row * 192, 8), 192), :]
        ref[pl.ds(192, 96), :] = down_ref[pl.ds(pl.multiple_of(row * 96, 8), 96), :]
        ref[pl.ds(288, 96), :] = up_ref[pl.ds(pl.multiple_of(row * 96, 8), 96), :]


def join_kernel(mid_ref, back_ref, ahead_ref, out_ref):
    out_ref[...] = mid_ref[...] + (back_ref[...] + ahead_ref[...])


def call(kernel, out_shape, scratch=(), in_specs=None, flops=0, moved=0, vmem_bytes=VMEM_BYTES):
    extra = {} if in_specs is None else {"in_specs": in_specs}
    return pl.pallas_call(
        kernel,
        out_shape=out_shape,
        scratch_shapes=list(scratch),
        compiler_params=pltpu.CompilerParams(vmem_limit_bytes=vmem_bytes),
        cost_estimate=pl.CostEstimate(flops=flops, bytes_accessed=moved, transcendentals=0),
        **extra,
    )


def f32(*shape):
    return jax.ShapeDtypeStruct(shape, F32)


def pair_words(far_targets, far_offsets):
    slab = lax.axis_index("slab")
    ring = slab % 8
    y, core = ring // 2, ring % 2

    def own(table):
        return jnp.concatenate(
            [lax.dynamic_slice_in_dim(table, (ring + z_hi * 8) * 48, 48, 0) for z_hi in range(2)]
        )

    targets, kinds = own(far_targets), own(far_offsets)
    to_slab, row = targets // 48, targets % 48
    half, to_ring = to_slab // 8, to_slab % 8
    step = (to_ring // 2 - y + 4) % 4
    near_block = (step + 1) % 4 + jnp.where(to_ring % 2 == core, 0, 3)
    block = jnp.where(step == 2, 6, near_block)
    slot = block * 96 + half * 48 + row
    return (slot * 8).reshape(-1), (kinds * 8).reshape(-1)


def operator_table(translators):
    count = translators.shape[0]
    half = lax.axis_index("slab") // 8
    own = lax.dynamic_slice_in_dim(translators, half * 32, 32, 2)
    lanes = jnp.concatenate([own] * 4, axis=2)
    return jnp.broadcast_to(lanes[:, :, None, :], (count, 2, 4, 128)).reshape(count * 8, 128)


def moved_by(block, move):
    return lax.ppermute(block, AXES, route_of(move))


def spread(block, groups):
    return lax.all_to_all(
        block, AXES, split_axis=0, concat_axis=0, axis_index_groups=groups, tiled=True
    )


def per_device(currents, near_tiles, radiation, child_phase, translators, far_targets, far_offsets):
    groups = exchange_groups()
    rows = currents.reshape(384, 128)
    core = (lax.axis_index("slab") % 2).astype(jnp.int32).reshape(1)
    slots, kinds = pair_words(far_targets, far_offsets)
    table = operator_table(translators)
    vmem = pl.BlockSpec(memory_space=pltpu.VMEM)
    smem = pl.BlockSpec(memory_space=pltpu.SMEM)
    hbm = pl.BlockSpec(memory_space=pl.ANY)

    patterns, down, up = call(
        aggregate_kernel,
        (f32(32, 3, 4, 128), f32(192, 128), f32(192, 128)),
        [pltpu.VMEM((2, 1024, 128), F32), pltpu.SemaphoreType.DMA((4,))],
        in_specs=[vmem, hbm, vmem],
        flops=600_000_000,
        moved=2_000_000,
        vmem_bytes=62 * 1024 * 1024,
    )(rows, radiation, child_phase)
    moved = spread(patterns, groups)
    down = lax.ppermute(down, "dir", [(d, d + 1) for d in range(15)])
    up = lax.ppermute(up, "dir", [(d + 1, d) for d in range(15)])

    keep, swap, far = call(
        translate_kernel,
        (f32(3, 96, 4, 128), f32(3, 96, 4, 128), f32(96, 4, 128)),
        [pltpu.VMEM((5376, 128), F32)],
        in_specs=[smem, smem, vmem, vmem, hbm, hbm],
        flops=100_000_000,
        moved=3_000_000,
    )(slots, kinds, table, moved.reshape(96, 4, 128), down, up)
    far_in = moved_by(far, lambda z_hi, y, core, d: (z_hi, (y + 2 * core - 1) % 4, 1 - core, d))
    swap_in = moved_by(swap, lambda z_hi, y, core, d: (z_hi, y, 1 - core, d))
    back, mid, ahead, beside, away = call(
        fold_kernel,
        (f32(96, 4, 128),) * 3 + (f32(384, 128),) * 2,
        in_specs=[smem] + [vmem] * 6,
        flops=1_000_000,
        moved=2_000_000,
    )(core, keep, swap_in, far_in, rows, down, up)
    back_in = moved_by(back, lambda z_hi, y, core, d: (z_hi, (y + 3) % 4, core, d))
    ahead_in = moved_by(ahead, lambda z_hi, y, core, d: (z_hi, (y + 1) % 4, core, d))
    beside = moved_by(beside, lambda z_hi, y, core, d: (z_hi, y, 1 - core, d))
    away = lax.ppermute(
        away, "slab", [(s, s + 2 * (s % 2) - 1) for s in range(16) if 0 <= s + 2 * (s % 2) - 1 < 16]
    )
    incoming = call(
        join_kernel,
        f32(96, 4, 128),
        flops=1_000_000,
        moved=1_000_000,
    )(mid, back_in, ahead_in)
    returned = spread(incoming.reshape(32, 3, 4, 128), groups)

    near = call(
        near_kernel,
        f32(192, 256),
        [
            pltpu.VMEM((27, 2, 128, 128), F32),
            pltpu.VMEM((4, 4, 48, 256), BF16),
            pltpu.VMEM((4, 4, 48, 256), BF16),
            pltpu.VMEM((4, 48, 256), F32),
            pltpu.SemaphoreType.DMA((3,)),
        ],
        in_specs=[smem] + [vmem] * 5 + [hbm],
        flops=2_000_000_000,
        moved=5_000_000,
        vmem_bytes=50 * 1024 * 1024,
    )(core, rows, beside, away, down, up, near_tiles)

    applied = call(
        disaggregate_kernel,
        f32(384, 128),
        [pltpu.VMEM((192, 256), F32)],
        flops=600_000_000,
        moved=2_000_000,
    )(returned, radiation, child_phase, near)
    return applied.reshape(currents.shape)


def solution(mesh):
    in_specs = (
        P("slab", "dir", None, None, None, None),
        P(),
        P(),
        P(),
        P(None, None, "dir"),
        P(),
        P(),
    )
    out_specs = P("slab", "dir", None, None, None, None)
    return jax.shard_map(
        per_device, mesh=mesh, in_specs=in_specs, out_specs=out_specs, check_vma=False
    )
```

```python
import functools

import jax
import jax.numpy as jnp
from jax import lax
from jax.experimental import pallas as pl
from jax.experimental.pallas import tpu as pltpu
from jax.sharding import PartitionSpec as P

F32 = jnp.float32
BF16 = jnp.bfloat16
AXES = ("slab", "dir")
VMEM_BYTES = 32 * 1024 * 1024
NT = (((1,), (1,)), ((), ()))
NN = (((1,), (0,)), ((), ()))


def linear(z_hi, y, core, d):
    return (z_hi * 8 + y * 2 + core) * 16 + d


def route_of(move):
    pairs = []
    for s in range(16):
        for d in range(16):
            to = move(s // 8, s // 2 % 4, s % 2, d)
            if to is not None:
                pairs.append((s * 16 + d, linear(*to)))
    return pairs


def exchange_groups():
    return [
        [linear(z_hi, j // 2, j % 2, d) for z_hi in range(2) for d in range(16)] for j in range(8)
    ]


def split(x):
    hi = x.astype(BF16)
    lo = (x - hi.astype(F32)).astype(BF16)
    return hi, lo


def dot3(a, b, dims):
    a_hi, a_lo = a
    b_hi, b_lo = b
    dot = functools.partial(lax.dot_general, dimension_numbers=dims, preferred_element_type=F32)
    return dot(a_hi, b_hi) + (dot(a_lo, b_hi) + dot(a_hi, b_lo))


def lane_sign(shape):
    lane = lax.broadcasted_iota(jnp.int32, shape, len(shape) - 1) % 128
    return jnp.where(lane < 64, -1.0, 1.0).astype(F32)


def times_i(x):
    return lane_sign(x.shape) * pltpu.roll(x, 64, 1)


def swap_bits(x):
    row = lax.broadcasted_iota(jnp.int32, x.shape, 0) // 4 % 2
    lane = lax.broadcasted_iota(jnp.int32, x.shape, 1) // 32 % 2
    other = pltpu.roll(x, 4, 0)
    moved = jnp.where(lane == 1, pltpu.roll(other, 32, 1), pltpu.roll(other, 96, 1))
    return jnp.where(row == lane, x, moved)


def radiation_copy(rad_hbm, rad_ref, sems, i):
    block = pl.ds(pl.multiple_of(i * 256, 256), 256)
    return pltpu.make_async_copy(rad_hbm.at[:, block], rad_ref.at[:, block], sems.at[i])


def tiles_copy(tiles_hbm, tiles_ref, sems, i):
    block = pl.ds(i * 9, 9)
    return pltpu.make_async_copy(tiles_hbm.at[block], tiles_ref.at[block], sems.at[i])


def radiation_block(rad_ref, start):
    re = rad_ref[0, pl.ds(start, 128), :]
    im = rad_ref[1, pl.ds(start, 128), :]
    top = jnp.concatenate([re, -im], axis=1)
    low = jnp.concatenate([im, re], axis=1)
    return split(jnp.concatenate([top[:64], low[:64], top[64:], low[64:]], axis=0))


def phase_block(phase_ref, start):
    phase = phase_ref[:, pl.ds(start, 128)]
    lane = lax.broadcasted_iota(jnp.int32, phase.shape, 1)

    def doubled(v):
        turned = pltpu.roll(v, 64, 1)
        return jnp.concatenate(
            [jnp.where(lane < 64, v, turned), jnp.where(lane < 64, turned, v)], axis=1
        )

    return doubled(jnp.cos(phase)), doubled(jnp.sin(phase))


def leaf_row(child, parent):
    i, j, l = child // 4, child // 2 % 2, child % 2
    return ((i * 2 + j) * 6 + parent * 2 + l) * 8


def aggregate_kernel(
    cur_hbm, rad_hbm, phase_hbm, out_ref, down_ref, up_ref, cur_ref, rad_ref, phase_ref, sems,
    unroll=4, groups=(4, 4),
):
    cur_copy = pltpu.make_async_copy(cur_hbm, cur_ref, sems.at[4])
    phase_copy = pltpu.make_async_copy(phase_hbm, phase_ref, sems.at[5])
    cur_copy.start()
    for i in range(4):
        radiation_copy(rad_hbm, rad_ref, sems, i).start()
        if i == 1:
            phase_copy.start()
    cur_copy.wait()
    for i in range(2):
        down_ref[pl.ds(i * 96, 96), :] = cur_ref[pl.ds(i * 192 + 96, 96), :]
        up_ref[pl.ds(i * 96, 96), :] = cur_ref[pl.ds(i * 192, 96), :]
    rows = cur_ref.shape[0] // 2
    x = jnp.concatenate(
        [cur_ref[pl.ds(0, rows, stride=2), :], cur_ref[pl.ds(1, rows, stride=2), :]], axis=1
    )
    x = split(x)

    def directions(step, carry):
        start = pl.multiple_of(step * 128, 128)
        leaf = dot3(x, radiation_block(rad_ref, start), NT)
        cos, sin = phase_block(phase_ref, start)
        for parent in range(3):
            a = jnp.zeros((8, 256), F32)
            b = jnp.zeros((8, 256), F32)
            for child in range(8):
                row = leaf_row(child, parent)
                part = leaf[row : row + 8]
                a = a + cos[child : child + 1] * part
                b = b + sin[child : child + 1] * part
            for pair in range(2):
                lanes = slice(pair * 128, pair * 128 + 128)
                block = swap_bits(a[:, lanes] + times_i(b[:, lanes]))
                d = step * 2 + pair
                out_ref[d, parent] = block[:4]
                out_ref[16 + d, parent] = block[4:]
        return carry

    phase_copy.wait()
    first = 0
    for count in groups:
        for i in range(first // 2, (first + count) // 2):
            radiation_copy(rad_hbm, rad_ref, sems, i).wait()
        lax.fori_loop(first, first + count, directions, 0, unroll=unroll)
        first += count


def disaggregate_kernel(in_ref, rad_ref, phase_ref, near_ref, out_ref, acc_ref, unroll=4):
    acc_ref[...] = near_ref[...]

    def directions(step, carry):
        start = pl.multiple_of(step * 128, 128)
        cos, sin = phase_block(phase_ref, start)
        parents = []
        for parent in range(3):
            halves = []
            for pair in range(2):
                d = step * 2 + pair
                block = jnp.concatenate([in_ref[d, parent], in_ref[16 + d, parent]], axis=0)
                halves.append(swap_bits(block))
            turned = jnp.concatenate([times_i(h) for h in halves], axis=1)
            parents.append((jnp.concatenate(halves, axis=1), turned))
        rows = [None] * 24
        for parent in range(3):
            plain, turned = parents[parent]
            for child in range(8):
                rows[leaf_row(child, parent) // 8] = (
                    cos[child : child + 1] * plain - sin[child : child + 1] * turned
                )
        children = split(jnp.concatenate(rows, axis=0))
        acc_ref[...] += dot3(children, radiation_block(rad_ref, start), NN)
        return carry

    lax.fori_loop(0, 8, directions, 0, unroll=unroll)
    rows = acc_ref.shape[0]
    out_ref[pl.ds(0, rows, stride=2), :] = acc_ref[:, :128]
    out_ref[pl.ds(1, rows, stride=2), :] = acc_ref[:, 128:]


def near_kernel(
    core_ref, own_ref, beside_ref, away_ref, down_ref, up_ref, tiles_hbm,
    out_ref, tiles_ref, hi_ref, lo_ref, acc_ref, sems,
):
    for i in range(3):
        tiles_copy(tiles_hbm, tiles_ref, sems, i).start()
    to_beside = jnp.where(core_ref[0] == 0, 3, 0)
    to_away = 3 - to_beside

    def put(ref, at_row, to_x, to_y):
        x = jnp.concatenate(
            [ref[pl.ds(at_row * 96, 48, stride=2), :], ref[pl.ds(at_row * 96 + 1, 48, stride=2), :]],
            axis=1,
        )
        hi, lo = split(x)
        hi_ref[to_x, to_y] = hi
        lo_ref[to_x, to_y] = lo

    for i in range(2):
        for j in range(2):
            put(own_ref, i * 2 + j, 1 + i, 1 + j)
        put(down_ref, i, 1 + i, 0)
        put(up_ref, i, 1 + i, 3)
    for i, to_y in enumerate((1, 2, 0, 3)):
        put(beside_ref, i, to_beside, to_y)
        put(away_ref, i, to_away, to_y)
    acc_ref[...] = jnp.zeros_like(acc_ref)

    @pl.loop(0, 3)
    def _(dx):
        tiles_copy(tiles_hbm, tiles_ref, sems, dx).wait()
        for dy in range(3):
            hi = hi_ref[pl.ds(dx, 2), dy : dy + 2].reshape(192, 256)
            lo = lo_ref[pl.ds(dx, 2), dy : dy + 2].reshape(192, 256)
            for dz in range(3):
                re = tiles_ref[dx * 9 + dy * 3 + dz, 0]
                im = tiles_ref[dx * 9 + dy * 3 + dz, 1]
                matrix = jnp.concatenate(
                    [jnp.concatenate([re, -im], axis=1), jnp.concatenate([im, re], axis=1)], axis=0
                )
                y = dot3((hi, lo), split(matrix), NT).reshape(4, 48, 256)
                if dz == 0:
                    acc_ref[:, 8:48] += y[:, 0:40]
                elif dz == 1:
                    acc_ref[...] += y
                else:
                    acc_ref[:, 0:40] += y[:, 8:48]

    out_ref[...] = acc_ref[...].reshape(192, 256)


def translate_kernel(
    slots_ref, kinds_ref, table_ref, src_ref, down_ref, up_ref,
    keep_ref, swap_ref, far_ref, acc_ref,
):
    acc_ref[...] = jnp.zeros_like(acc_ref)
    row = lax.broadcasted_iota(jnp.int32, (8, 128), 0)

    def tile(first):
        return pl.ds(pl.multiple_of(first, 8), 8)

    def source(s, carry):
        part = src_ref[s]
        both = jnp.concatenate([part, part], axis=0)
        both = jnp.where(row < 4, both, times_i(both))
        slots, sums = [], []
        for f in range(16):
            slot = slots_ref[s * 16 + f]
            slots.append(slot)
            kind = kinds_ref[s * 16 + f]
            sums.append(acc_ref[tile(slot), :] + table_ref[tile(kind), :] * both)
        for f in range(16):
            acc_ref[tile(slots[f]), :] = sums[f]
        return carry

    lax.fori_loop(0, 96, source, 0, unroll=4)

    def folded(block):
        part = acc_ref[pl.ds(block * 768, 768), :].reshape(96, 8, 128)
        return part[:, :4] + part[:, 4:]

    for block in range(3):
        keep_ref[block] = folded(block)
        swap_ref[block] = folded(block + 3)
    far_ref[...] = folded(6)


def fold_kernel(
    core_ref, keep_ref, got_ref, cur_ref, down_ref, up_ref,
    back_ref, mid_ref, ahead_ref, beside_ref, away_ref,
):
    back_ref[...] = keep_ref[0] + got_ref[0]
    mid_ref[...] = keep_ref[1] + got_ref[1]
    ahead_ref[...] = keep_ref[2] + got_ref[2]
    core = core_ref[0]
    for ref, row in ((beside_ref, 1 - core), (away_ref, core)):
        ref[pl.ds(0, 192), :] = cur_ref[pl.ds(pl.multiple_of(row * 192, 8), 192), :]
        ref[pl.ds(192, 96), :] = down_ref[pl.ds(pl.multiple_of(row * 96, 8), 96), :]
        ref[pl.ds(288, 96), :] = up_ref[pl.ds(pl.multiple_of(row * 96, 8), 96), :]


def join_kernel(mid_ref, far_ref, back_ref, ahead_ref, out_ref):
    out_ref[...] = (mid_ref[...] + far_ref[...]) + (back_ref[...] + ahead_ref[...])


def call(kernel, out_shape, scratch=(), in_specs=None, flops=0, moved=0, vmem_bytes=VMEM_BYTES):
    extra = {} if in_specs is None else {"in_specs": in_specs}
    return pl.pallas_call(
        kernel,
        out_shape=out_shape,
        scratch_shapes=list(scratch),
        compiler_params=pltpu.CompilerParams(vmem_limit_bytes=vmem_bytes),
        cost_estimate=pl.CostEstimate(flops=flops, bytes_accessed=moved, transcendentals=0),
        **extra,
    )


def f32(*shape):
    return jax.ShapeDtypeStruct(shape, F32)


def pair_words(far_targets, far_offsets):
    slab = lax.axis_index("slab")
    ring = slab % 8
    y, core = ring // 2, ring % 2

    def own(table):
        return jnp.concatenate(
            [lax.dynamic_slice_in_dim(table, (ring + z_hi * 8) * 48, 48, 0) for z_hi in range(2)]
        )

    targets, kinds = own(far_targets), own(far_offsets)
    to_slab, row = targets // 48, targets % 48
    half, to_ring = to_slab // 8, to_slab % 8
    step = (to_ring // 2 - y + 4) % 4
    near_block = (step + 1) % 4 + jnp.where(to_ring % 2 == core, 0, 3)
    block = jnp.where(step == 2, 6, near_block)
    slot = block * 96 + half * 48 + row
    return (slot * 8).reshape(-1), (kinds * 8).reshape(-1)


def operator_table(translators):
    count = translators.shape[0]
    half = lax.axis_index("slab") // 8
    own = lax.dynamic_slice_in_dim(translators, half * 32, 32, 2)
    lanes = jnp.concatenate([own] * 4, axis=2)
    return jnp.broadcast_to(lanes[:, :, None, :], (count, 2, 4, 128)).reshape(count * 8, 128)


def moved_by(block, move):
    return lax.ppermute(block, AXES, route_of(move))


def spread(block, groups):
    return lax.all_to_all(
        block, AXES, split_axis=0, concat_axis=0, axis_index_groups=groups, tiled=True
    )


def per_device(currents, near_tiles, radiation, child_phase, translators, far_targets, far_offsets):
    groups = exchange_groups()
    rows = currents.reshape(384, 128)
    core = (lax.axis_index("slab") % 2).astype(jnp.int32).reshape(1)
    slots, kinds = pair_words(far_targets, far_offsets)
    table = operator_table(translators)
    vmem = pl.BlockSpec(memory_space=pltpu.VMEM)
    smem = pl.BlockSpec(memory_space=pltpu.SMEM)
    hbm = pl.BlockSpec(memory_space=pl.ANY)

    patterns, down, up = call(
        aggregate_kernel,
        (f32(32, 3, 4, 128), f32(192, 128), f32(192, 128)),
        [
            pltpu.VMEM((384, 128), F32),
            pltpu.VMEM((2, 1024, 128), F32),
            pltpu.VMEM((8, 1024), F32),
            pltpu.SemaphoreType.DMA((6,)),
        ],
        in_specs=[hbm] * 3,
        flops=600_000_000,
        moved=2_000_000,
        vmem_bytes=62 * 1024 * 1024,
    )(rows, radiation, child_phase)
    moved = spread(patterns, groups)
    down = lax.ppermute(down, "dir", [(d, d + 1) for d in range(15)])
    up = lax.ppermute(up, "dir", [(d + 1, d) for d in range(15)])

    keep, swap, far = call(
        translate_kernel,
        (f32(3, 96, 4, 128), f32(3, 96, 4, 128), f32(96, 4, 128)),
        [pltpu.VMEM((5376, 128), F32)],
        in_specs=[smem, smem, vmem, vmem, hbm, hbm],
        flops=100_000_000,
        moved=3_000_000,
    )(slots, kinds, table, moved.reshape(96, 4, 128), down, up)
    far_in = moved_by(far, lambda z_hi, y, core, d: (z_hi, (y + 2) % 4, 1 - core, d))
    swap_in = moved_by(swap, lambda z_hi, y, core, d: (z_hi, y, 1 - core, d))
    back, mid, ahead, beside, away = call(
        fold_kernel,
        (f32(96, 4, 128),) * 3 + (f32(384, 128),) * 2,
        in_specs=[smem] + [vmem] * 5,
        flops=1_000_000,
        moved=2_000_000,
    )(core, keep, swap_in, rows, down, up)
    back_in = moved_by(back, lambda z_hi, y, core, d: (z_hi, (y + 3) % 4, core, d))
    ahead_in = moved_by(ahead, lambda z_hi, y, core, d: (z_hi, (y + 1) % 4, core, d))
    beside = moved_by(beside, lambda z_hi, y, core, d: (z_hi, y, 1 - core, d))
    away = lax.ppermute(
        away, "slab", [(s, s + 2 * (s % 2) - 1) for s in range(16) if 0 <= s + 2 * (s % 2) - 1 < 16]
    )
    incoming = call(
        join_kernel, f32(96, 4, 128), flops=1_000_000, moved=1_000_000
    )(mid, far_in, back_in, ahead_in)
    returned = spread(incoming.reshape(32, 3, 4, 128), groups)

    near = call(
        near_kernel,
        f32(192, 256),
        [
            pltpu.VMEM((27, 2, 128, 128), F32),
            pltpu.VMEM((4, 4, 48, 256), BF16),
            pltpu.VMEM((4, 4, 48, 256), BF16),
            pltpu.VMEM((4, 48, 256), F32),
            pltpu.SemaphoreType.DMA((3,)),
        ],
        in_specs=[smem] + [vmem] * 5 + [hbm],
        flops=2_000_000_000,
        moved=5_000_000,
        vmem_bytes=50 * 1024 * 1024,
    )(core, rows, beside, away, down, up, near_tiles)

    applied = call(
        disaggregate_kernel,
        f32(384, 128),
        [pltpu.VMEM((192, 256), F32)],
        flops=600_000_000,
        moved=2_000_000,
    )(returned, radiation, child_phase, near)
    return applied.reshape(currents.shape)


def solution(mesh):
    in_specs = (
        P("slab", "dir", None, None, None, None),
        P(),
        P(),
        P(),
        P(None, None, "dir"),
        P(),
        P(),
    )
    out_specs = P("slab", "dir", None, None, None, None)
    return jax.shard_map(
        per_device, mesh=mesh, in_specs=in_specs, out_specs=out_specs, check_vma=False
    )
```

```python
import functools

import jax
import jax.numpy as jnp
from jax import lax
from jax.experimental import pallas as pl
from jax.experimental.pallas import tpu as pltpu
from jax.sharding import PartitionSpec as P

F32 = jnp.float32
BF16 = jnp.bfloat16
AXES = ("slab", "dir")
VMEM_BYTES = 32 * 1024 * 1024
NT = (((1,), (1,)), ((), ()))
NN = (((1,), (0,)), ((), ()))


def linear(z_hi, y, core, d):
    return (z_hi * 8 + y * 2 + core) * 16 + d


def route_of(move):
    pairs = []
    for s in range(16):
        for d in range(16):
            to = move(s // 8, s // 2 % 4, s % 2, d)
            if to is not None:
                pairs.append((s * 16 + d, linear(*to)))
    return pairs


def exchange_groups():
    return [
        [linear(z_hi, j // 2, j % 2, d) for z_hi in range(2) for d in range(16)] for j in range(8)
    ]


def split(x):
    hi = x.astype(BF16)
    lo = (x - hi.astype(F32)).astype(BF16)
    return hi, lo


def dot3(a, b, dims):
    a_hi, a_lo = a
    b_hi, b_lo = b
    dot = functools.partial(lax.dot_general, dimension_numbers=dims, preferred_element_type=F32)
    return dot(a_hi, b_hi) + (dot(a_lo, b_hi) + dot(a_hi, b_lo))


def lane_sign(shape):
    lane = lax.broadcasted_iota(jnp.int32, shape, len(shape) - 1) % 128
    return jnp.where(lane < 64, -1.0, 1.0).astype(F32)


def times_i(x):
    return lane_sign(x.shape) * pltpu.roll(x, 64, 1)


def swap_bits(x):
    row = lax.broadcasted_iota(jnp.int32, x.shape, 0) // 4 % 2
    lane = lax.broadcasted_iota(jnp.int32, x.shape, 1) // 32 % 2
    other = pltpu.roll(x, 4, 0)
    moved = jnp.where(lane == 1, pltpu.roll(other, 32, 1), pltpu.roll(other, 96, 1))
    return jnp.where(row == lane, x, moved)


def radiation_copy(rad_hbm, rad_ref, sems, i):
    block = pl.ds(pl.multiple_of(i * 256, 256), 256)
    return pltpu.make_async_copy(rad_hbm.at[:, block], rad_ref.at[:, block], sems.at[i])


def tiles_copy(tiles_hbm, tiles_ref, sems, i):
    block = pl.ds(i * 9, 9)
    return pltpu.make_async_copy(tiles_hbm.at[block], tiles_ref.at[block], sems.at[i])


def radiation_block(rad_ref, start):
    re = rad_ref[0, pl.ds(start, 128), :]
    im = rad_ref[1, pl.ds(start, 128), :]
    top = jnp.concatenate([re, -im], axis=1)
    low = jnp.concatenate([im, re], axis=1)
    return split(jnp.concatenate([top[:64], low[:64], top[64:], low[64:]], axis=0))


def phase_block(phase_ref, start):
    phase = phase_ref[:, pl.ds(start, 128)]
    lane = lax.broadcasted_iota(jnp.int32, phase.shape, 1)

    def doubled(v):
        turned = pltpu.roll(v, 64, 1)
        return jnp.concatenate(
            [jnp.where(lane < 64, v, turned), jnp.where(lane < 64, turned, v)], axis=1
        )

    return doubled(jnp.cos(phase)), doubled(jnp.sin(phase))


def leaf_row(child, parent):
    i, j, l = child // 4, child // 2 % 2, child % 2
    return ((i * 2 + j) * 6 + parent * 2 + l) * 8


def aggregate_kernel(
    core_ref, cur_hbm, rad_hbm, phase_hbm, out_ref, lent_ref, cur_ref, rad_ref, phase_ref, sems,
    unroll=4, groups=(4, 4),
):
    cur_copy = pltpu.make_async_copy(cur_hbm, cur_ref, sems.at[4])
    phase_copy = pltpu.make_async_copy(phase_hbm, phase_ref, sems.at[5])
    cur_copy.start()
    for i in range(4):
        radiation_copy(rad_hbm, rad_ref, sems, i).start()
        if i == 1:
            phase_copy.start()
    cur_copy.wait()
    for i in range(2):
        first = pl.multiple_of(i * 192 + core_ref[0] * 96, 8)
        lent_ref[pl.ds(i * 96, 96), :] = cur_ref[pl.ds(first, 96), :]
    rows = cur_ref.shape[0] // 2
    x = jnp.concatenate(
        [cur_ref[pl.ds(0, rows, stride=2), :], cur_ref[pl.ds(1, rows, stride=2), :]], axis=1
    )
    x = split(x)

    def directions(step, carry):
        start = pl.multiple_of(step * 128, 128)
        leaf = dot3(x, radiation_block(rad_ref, start), NT)
        cos, sin = phase_block(phase_ref, start)
        for parent in range(3):
            a = jnp.zeros((8, 256), F32)
            b = jnp.zeros((8, 256), F32)
            for child in range(8):
                row = leaf_row(child, parent)
                part = leaf[row : row + 8]
                a = a + cos[child : child + 1] * part
                b = b + sin[child : child + 1] * part
            for pair in range(2):
                lanes = slice(pair * 128, pair * 128 + 128)
                block = swap_bits(a[:, lanes] + times_i(b[:, lanes]))
                d = step * 2 + pair
                out_ref[d, parent] = block[:4]
                out_ref[16 + d, parent] = block[4:]
        return carry

    phase_copy.wait()
    first = 0
    for count in groups:
        for i in range(first // 2, (first + count) // 2):
            radiation_copy(rad_hbm, rad_ref, sems, i).wait()
        lax.fori_loop(first, first + count, directions, 0, unroll=unroll)
        first += count


def disaggregate_kernel(in_ref, rad_ref, phase_ref, near_ref, out_ref, acc_ref, unroll=4):
    acc_ref[...] = near_ref[...]

    def directions(step, carry):
        start = pl.multiple_of(step * 128, 128)
        cos, sin = phase_block(phase_ref, start)
        parents = []
        for parent in range(3):
            halves = []
            for pair in range(2):
                d = step * 2 + pair
                block = jnp.concatenate([in_ref[d, parent], in_ref[16 + d, parent]], axis=0)
                halves.append(swap_bits(block))
            turned = jnp.concatenate([times_i(h) for h in halves], axis=1)
            parents.append((jnp.concatenate(halves, axis=1), turned))
        rows = [None] * 24
        for parent in range(3):
            plain, turned = parents[parent]
            for child in range(8):
                rows[leaf_row(child, parent) // 8] = (
                    cos[child : child + 1] * plain - sin[child : child + 1] * turned
                )
        children = split(jnp.concatenate(rows, axis=0))
        acc_ref[...] += dot3(children, radiation_block(rad_ref, start), NN)
        return carry

    lax.fori_loop(0, 8, directions, 0, unroll=unroll)
    rows = acc_ref.shape[0]
    out_ref[pl.ds(0, rows, stride=2), :] = acc_ref[:, :128]
    out_ref[pl.ds(1, rows, stride=2), :] = acc_ref[:, 128:]


def near_kernel(
    core_ref, own_ref, side_ref, cross_ref, away_ref, tiles_hbm,
    out_ref, tiles_ref, hi_ref, lo_ref, acc_ref, sems,
):
    for i in range(3):
        tiles_copy(tiles_hbm, tiles_ref, sems, i).start()
    core = core_ref[0]
    to_beside = 3 - 3 * core
    to_away = 3 * core
    side_y = 3 * core
    cross_y = 3 - 3 * core

    def put(ref, first, to_x, to_y):
        first = pl.multiple_of(first, 8)
        x = jnp.concatenate(
            [ref[pl.ds(first, 48, stride=2), :], ref[pl.ds(first + 1, 48, stride=2), :]], axis=1
        )
        hi, lo = split(x)
        hi_ref[to_x, to_y] = hi
        lo_ref[to_x, to_y] = lo

    for i in range(2):
        for j in range(2):
            put(own_ref, (i * 2 + j) * 96, 1 + i, 1 + j)
        put(side_ref, i * 96, 1 + i, side_y)
        put(cross_ref, i * 96, 1 + i, cross_y)
        put(cross_ref, 288 + i * 96, to_beside, 1 + i)
    put(side_ref, 192 + core * 96, to_beside, side_y)
    put(cross_ref, 192, to_beside, cross_y)
    for i, to_y in enumerate((1, 2, 0, 3)):
        put(away_ref, i * 96, to_away, to_y)
    acc_ref[...] = jnp.zeros_like(acc_ref)

    @pl.loop(0, 3)
    def _(dx):
        tiles_copy(tiles_hbm, tiles_ref, sems, dx).wait()
        for dy in range(3):
            hi = hi_ref[pl.ds(dx, 2), dy : dy + 2].reshape(192, 256)
            lo = lo_ref[pl.ds(dx, 2), dy : dy + 2].reshape(192, 256)
            for dz in range(3):
                re = tiles_ref[dx * 9 + dy * 3 + dz, 0]
                im = tiles_ref[dx * 9 + dy * 3 + dz, 1]
                matrix = jnp.concatenate(
                    [jnp.concatenate([re, -im], axis=1), jnp.concatenate([im, re], axis=1)], axis=0
                )
                y = dot3((hi, lo), split(matrix), NT).reshape(4, 48, 256)
                if dz == 0:
                    acc_ref[:, 8:48] += y[:, 0:40]
                elif dz == 1:
                    acc_ref[...] += y
                else:
                    acc_ref[:, 0:40] += y[:, 8:48]

    out_ref[...] = acc_ref[...].reshape(192, 256)


def translate_kernel(
    slots_ref, kinds_ref, table_ref, src_ref, side_ref,
    keep_ref, swap_ref, far_ref, acc_ref,
):
    acc_ref[...] = jnp.zeros_like(acc_ref)
    row = lax.broadcasted_iota(jnp.int32, (8, 128), 0)

    def tile(first):
        return pl.ds(pl.multiple_of(first, 8), 8)

    def source(s, carry):
        part = src_ref[s]
        both = jnp.concatenate([part, part], axis=0)
        both = jnp.where(row < 4, both, times_i(both))
        slots, sums = [], []
        for f in range(16):
            slot = slots_ref[f, s]
            slots.append(slot)
            kind = kinds_ref[f, s]
            sums.append(acc_ref[tile(slot), :] + table_ref[tile(kind), :] * both)
        for f in range(16):
            acc_ref[tile(slots[f]), :] = sums[f]
        return carry

    lax.fori_loop(0, 96, source, 0, unroll=4)

    def folded(block):
        part = acc_ref[pl.ds(block * 768, 768), :].reshape(96, 8, 128)
        return part[:, :4] + part[:, 4:]

    for block in range(3):
        keep_ref[block] = folded(block)
        swap_ref[block] = folded(block + 3)
    far_ref[...] = folded(6)


def pair_kernel(core_ref, cur_ref, got_ref, out_ref):
    j = 1 - core_ref[0]
    for i in range(2):
        first = pl.multiple_of(i * 192 + j * 96, 8)
        out_ref[pl.ds(i * 96, 96), :] = cur_ref[pl.ds(first, 96), :]
    out_ref[pl.ds(192, 192), :] = got_ref[...]


def lists_kernel(slab_ref, targets_ref, kinds_ref, tr_ref, order_ref, slots_ref, rows_ref, table_ref):
    slab = slab_ref[0]
    ring, z_hi = slab & 7, slab >> 3
    y, core = ring >> 1, ring & 1
    lane = lax.broadcasted_iota(jnp.int32, (16, 128), 1)

    def own(ref):
        low = pltpu.roll(ref[...], (16 - ring) * 48, 1)
        high = pltpu.roll(ref[...], (9 - ring) * 48, 1)
        return jnp.where(lane < 48, low[:, :128], high[:, :128])

    target = own(targets_ref)
    to_slab = (target * 683) >> 15
    to_ring = to_slab & 7
    step = ((to_ring >> 1) - y + 4) & 3
    near_block = ((step + 1) & 3) + jnp.where((to_ring & 1) == core, 0, 3)
    block = jnp.where(step == 2, 6, near_block)
    slots_ref[...] = (block * 96 + (to_slab >> 3) * 48 + (target - to_slab * 48)) * 8
    rows_ref[...] = own(kinds_ref) * 8

    def part(c):
        half = tr_ref[c, pl.ds(pl.multiple_of(z_hi * 32, 32), 32), :]
        lanes = jnp.concatenate([half] * 4, axis=0).T
        return jnp.broadcast_to(lanes[:, None, :], (lanes.shape[0], 4, 128))

    table_ref[...] = jnp.concatenate([part(0), part(1)], axis=1)


def fold_kernel(
    core_ref, keep_ref, got_ref, cur_ref, side_ref, back_ref, mid_ref, ahead_ref, cross_ref
):
    back_ref[...] = keep_ref[0] + got_ref[0]
    mid_ref[...] = keep_ref[1] + got_ref[1]
    ahead_ref[...] = keep_ref[2] + got_ref[2]
    row = 1 - core_ref[0]
    cross_ref[pl.ds(0, 192), :] = side_ref[pl.ds(192, 192), :]
    cross_ref[pl.ds(192, 96), :] = side_ref[pl.ds(pl.multiple_of(row * 96, 8), 96), :]
    cross_ref[pl.ds(288, 192), :] = cur_ref[pl.ds(pl.multiple_of(row * 192, 8), 192), :]


def away_kernel(core_ref, cur_ref, side_ref, cross_ref, far_ref, out_ref):
    core = core_ref[0]
    first = pl.multiple_of(core * 96, 8)
    out_ref[pl.ds(0, 192), :] = cur_ref[pl.ds(pl.multiple_of(core * 192, 8), 192), :]
    out_ref[pl.ds(pl.multiple_of(192 + core * 96, 8), 96), :] = side_ref[pl.ds(first, 96), :]
    out_ref[pl.ds(pl.multiple_of(288 - core * 96, 8), 96), :] = cross_ref[pl.ds(first, 96), :]


def join_kernel(mid_ref, far_ref, back_ref, ahead_ref, out_ref):
    out_ref[...] = (mid_ref[...] + far_ref[...]) + (back_ref[...] + ahead_ref[...])


def call(kernel, out_shape, scratch=(), in_specs=None, flops=0, moved=0, vmem_bytes=VMEM_BYTES):
    extra = {} if in_specs is None else {"in_specs": in_specs}
    return pl.pallas_call(
        kernel,
        out_shape=out_shape,
        scratch_shapes=list(scratch),
        compiler_params=pltpu.CompilerParams(vmem_limit_bytes=vmem_bytes),
        cost_estimate=pl.CostEstimate(flops=flops, bytes_accessed=moved, transcendentals=0),
        **extra,
    )


def f32(*shape):
    return jax.ShapeDtypeStruct(shape, F32)


def moved_by(block, move):
    return lax.ppermute(block, AXES, route_of(move))


def spread(block, groups):
    return lax.all_to_all(
        block, AXES, split_axis=0, concat_axis=0, axis_index_groups=groups, tiled=True
    )


def per_device(currents, near_tiles, radiation, child_phase, translators, far_targets, far_offsets):
    groups = exchange_groups()
    rows = currents.reshape(384, 128)
    slab = lax.axis_index("slab").astype(jnp.int32).reshape(1)
    core = slab & 1
    vmem = pl.BlockSpec(memory_space=pltpu.VMEM)
    smem = pl.BlockSpec(memory_space=pltpu.SMEM)
    hbm = pl.BlockSpec(memory_space=pl.ANY)

    patterns, lent = call(
        aggregate_kernel,
        (f32(32, 3, 4, 128), f32(192, 128)),
        [
            pltpu.VMEM((384, 128), F32),
            pltpu.VMEM((2, 1024, 128), F32),
            pltpu.VMEM((8, 1024), F32),
            pltpu.SemaphoreType.DMA((6,)),
        ],
        in_specs=[smem] + [hbm] * 3,
        flops=600_000_000,
        moved=2_000_000,
        vmem_bytes=62 * 1024 * 1024,
    )(core, rows, radiation, child_phase)
    moved = spread(patterns, groups)
    got = moved_by(lent, lambda z_hi, y, core, d: (z_hi, y, 1 - core, d))
    side = call(
        pair_kernel, f32(384, 128), in_specs=[smem, vmem, vmem], flops=1000, moved=400_000
    )(core, rows, got)
    count = translators.shape[0]
    lists = jax.ShapeDtypeStruct((16, 128), jnp.int32)
    slots, kinds, table = call(
        lists_kernel,
        (lists, lists, f32(count, 8, 128)),
        in_specs=[smem] + [vmem] * 3 + [hbm],
        flops=1_000_000,
        moved=2_000_000,
    )(slab, far_targets.T, far_offsets.T, translators.transpose(1, 2, 0), side)
    table = table.reshape(count * 8, 128)
    side = moved_by(
        side,
        lambda z_hi, y, core, d: (z_hi, y, core, d + 1 - 2 * core)
        if 0 <= d + 1 - 2 * core < 16
        else None,
    )

    keep, swap, far = call(
        translate_kernel,
        (f32(3, 96, 4, 128), f32(3, 96, 4, 128), f32(96, 4, 128)),
        [pltpu.VMEM((5376, 128), F32)],
        in_specs=[smem, smem, vmem, vmem, hbm],
        flops=100_000_000,
        moved=3_000_000,
    )(slots, kinds, table, moved.reshape(96, 4, 128), side)
    far_in = moved_by(far, lambda z_hi, y, core, d: (z_hi, (y + 2) % 4, 1 - core, d))
    swap_in = moved_by(swap, lambda z_hi, y, core, d: (z_hi, y, 1 - core, d))
    back, mid, ahead, cross = call(
        fold_kernel,
        (f32(96, 4, 128),) * 3 + (f32(480, 128),),
        in_specs=[smem] + [vmem] * 4,
        flops=1_000_000,
        moved=2_000_000,
    )(core, keep, swap_in, rows, side)
    back_in = moved_by(back, lambda z_hi, y, core, d: (z_hi, (y + 3) % 4, core, d))
    ahead_in = moved_by(ahead, lambda z_hi, y, core, d: (z_hi, (y + 1) % 4, core, d))
    cross = moved_by(cross, lambda z_hi, y, core, d: (z_hi, y, 1 - core, d))
    payload = call(
        away_kernel, f32(384, 128), in_specs=[smem] + [vmem] * 3 + [hbm], flops=1000, moved=400_000
    )(core, rows, side, cross, far_in)
    away = lax.ppermute(
        payload, "slab", [(s, s + 2 * (s % 2) - 1) for s in range(16) if 0 <= s + 2 * (s % 2) - 1 < 16]
    )
    incoming = call(
        join_kernel,
        f32(96, 4, 128),
        flops=1_000_000,
        moved=1_000_000,
    )(mid, far_in, back_in, ahead_in)
    returned = spread(incoming.reshape(32, 3, 4, 128), groups)

    near = call(
        near_kernel,
        f32(192, 256),
        [
            pltpu.VMEM((27, 2, 128, 128), F32),
            pltpu.VMEM((4, 4, 48, 256), BF16),
            pltpu.VMEM((4, 4, 48, 256), BF16),
            pltpu.VMEM((4, 48, 256), F32),
            pltpu.SemaphoreType.DMA((3,)),
        ],
        in_specs=[smem] + [vmem] * 4 + [hbm],
        flops=2_000_000_000,
        moved=5_000_000,
        vmem_bytes=50 * 1024 * 1024,
    )(core, rows, side, cross, away, near_tiles)

    applied = call(
        disaggregate_kernel,
        f32(384, 128),
        [pltpu.VMEM((192, 256), F32)],
        flops=600_000_000,
        moved=2_000_000,
    )(returned, radiation, child_phase, near)
    return applied.reshape(currents.shape)


def solution(mesh):
    in_specs = (
        P("slab", "dir", None, None, None, None),
        P(),
        P(),
        P(),
        P(None, None, "dir"),
        P(),
        P(),
    )
    out_specs = P("slab", "dir", None, None, None, None)
    return jax.shard_map(
        per_device, mesh=mesh, in_specs=in_specs, out_specs=out_specs, check_vma=False
    )
```

```python
import functools

import jax
import jax.numpy as jnp
from jax import lax
from jax.experimental import pallas as pl
from jax.experimental.pallas import tpu as pltpu
from jax.sharding import PartitionSpec as P

F32 = jnp.float32
BF16 = jnp.bfloat16
AXES = ("slab", "dir")
VMEM_BYTES = 32 * 1024 * 1024
NT = (((1,), (1,)), ((), ()))
NN = (((1,), (0,)), ((), ()))


def linear(z_hi, y, core, d):
    return (z_hi * 8 + y * 2 + core) * 16 + d


def route_of(move):
    pairs = []
    for s in range(16):
        for d in range(16):
            to = move(s // 8, s // 2 % 4, s % 2, d)
            if to is not None:
                pairs.append((s * 16 + d, linear(*to)))
    return pairs


def exchange_groups():
    return [
        [linear(z_hi, j // 2, j % 2, d) for z_hi in range(2) for d in range(16)] for j in range(8)
    ]


def split(x):
    hi = x.astype(BF16)
    lo = (x - hi.astype(F32)).astype(BF16)
    return hi, lo


def dot3(a, b, dims):
    a_hi, a_lo = a
    b_hi, b_lo = b
    dot = functools.partial(lax.dot_general, dimension_numbers=dims, preferred_element_type=F32)
    return dot(a_hi, b_hi) + (dot(a_lo, b_hi) + dot(a_hi, b_lo))


def lane_sign(shape):
    lane = lax.broadcasted_iota(jnp.int32, shape, len(shape) - 1) % 128
    return jnp.where(lane < 64, -1.0, 1.0).astype(F32)


def times_i(x):
    return lane_sign(x.shape) * pltpu.roll(x, 64, 1)


def swap_bits(x):
    row = lax.broadcasted_iota(jnp.int32, x.shape, 0) // 4 % 2
    lane = lax.broadcasted_iota(jnp.int32, x.shape, 1) // 32 % 2
    other = pltpu.roll(x, 4, 0)
    moved = jnp.where(lane == 1, pltpu.roll(other, 32, 1), pltpu.roll(other, 96, 1))
    return jnp.where(row == lane, x, moved)


def radiation_copy(rad_hbm, rad_ref, sems, i):
    block = pl.ds(pl.multiple_of(i * 256, 256), 256)
    return pltpu.make_async_copy(rad_hbm.at[:, block], rad_ref.at[:, block], sems.at[i])


def tiles_copy(tiles_hbm, tiles_ref, sems, i):
    block = pl.ds(i * 9, 9)
    return pltpu.make_async_copy(tiles_hbm.at[block], tiles_ref.at[block], sems.at[i])


def radiation_block(rad_ref, start):
    re = rad_ref[0, pl.ds(start, 128), :]
    im = rad_ref[1, pl.ds(start, 128), :]
    top = jnp.concatenate([re, -im], axis=1)
    low = jnp.concatenate([im, re], axis=1)
    return split(jnp.concatenate([top[:64], low[:64], top[64:], low[64:]], axis=0))


def phase_block(phase_ref, start):
    phase = phase_ref[:, pl.ds(start, 128)]
    lane = lax.broadcasted_iota(jnp.int32, phase.shape, 1)

    def doubled(v):
        turned = pltpu.roll(v, 64, 1)
        return jnp.concatenate(
            [jnp.where(lane < 64, v, turned), jnp.where(lane < 64, turned, v)], axis=1
        )

    return doubled(jnp.cos(phase)), doubled(jnp.sin(phase))


def leaf_row(child, parent):
    i, j, l = child // 4, child // 2 % 2, child % 2
    return ((i * 2 + j) * 6 + parent * 2 + l) * 8


def aggregate_kernel(
    core_ref, cur_hbm, rad_hbm, phase_hbm, out_ref, beside_ref, away_ref,
    cur_ref, rad_ref, phase_ref, sems, unroll=8, groups=(8,),
):
    cur_copy = pltpu.make_async_copy(cur_hbm, cur_ref, sems.at[4])
    phase_copy = pltpu.make_async_copy(phase_hbm, phase_ref, sems.at[5])
    cur_copy.start()
    for i in range(4):
        radiation_copy(rad_hbm, rad_ref, sems, i).start()
        if i == 1:
            phase_copy.start()
    cur_copy.wait()
    core = core_ref[0]
    beside_ref[...] = cur_ref[pl.ds(pl.multiple_of((1 - core) * 192, 8), 192), :]
    away_ref[...] = cur_ref[pl.ds(pl.multiple_of(core * 192, 8), 192), :]
    rows = cur_ref.shape[0] // 2
    x = jnp.concatenate(
        [cur_ref[pl.ds(0, rows, stride=2), :], cur_ref[pl.ds(1, rows, stride=2), :]], axis=1
    )
    x = split(x)

    def directions(step, carry):
        start = pl.multiple_of(step * 128, 128)
        leaf = dot3(x, radiation_block(rad_ref, start), NT)
        cos, sin = phase_block(phase_ref, start)
        for parent in range(3):
            a = jnp.zeros((8, 256), F32)
            b = jnp.zeros((8, 256), F32)
            for child in range(8):
                row = leaf_row(child, parent)
                part = leaf[row : row + 8]
                a = a + cos[child : child + 1] * part
                b = b + sin[child : child + 1] * part
            for pair in range(2):
                lanes = slice(pair * 128, pair * 128 + 128)
                block = swap_bits(a[:, lanes] + times_i(b[:, lanes]))
                d = step * 2 + pair
                out_ref[d, parent] = block[:4]
                out_ref[16 + d, parent] = block[4:]
        return carry

    phase_copy.wait()
    first = 0
    for count in groups:
        for i in range(first // 2, (first + count) // 2):
            radiation_copy(rad_hbm, rad_ref, sems, i).wait()
        lax.fori_loop(first, first + count, directions, 0, unroll=unroll)
        first += count


def disaggregate_kernel(in_ref, rad_ref, phase_ref, near_ref, out_ref, acc_ref, unroll=8):
    acc_ref[...] = near_ref[...]

    def directions(step, carry):
        start = pl.multiple_of(step * 128, 128)
        cos, sin = phase_block(phase_ref, start)
        parents = []
        for parent in range(3):
            halves = []
            for pair in range(2):
                d = step * 2 + pair
                block = jnp.concatenate([in_ref[d, parent], in_ref[16 + d, parent]], axis=0)
                halves.append(swap_bits(block))
            turned = jnp.concatenate([times_i(h) for h in halves], axis=1)
            parents.append((jnp.concatenate(halves, axis=1), turned))
        rows = [None] * 24
        for parent in range(3):
            plain, turned = parents[parent]
            for child in range(8):
                rows[leaf_row(child, parent) // 8] = (
                    cos[child : child + 1] * plain - sin[child : child + 1] * turned
                )
        children = split(jnp.concatenate(rows, axis=0))
        acc_ref[...] += dot3(children, radiation_block(rad_ref, start), NN)
        return carry

    lax.fori_loop(0, 8, directions, 0, unroll=unroll)
    rows = acc_ref.shape[0]
    out_ref[pl.ds(0, rows, stride=2), :] = acc_ref[:, :128]
    out_ref[pl.ds(1, rows, stride=2), :] = acc_ref[:, 128:]


def near_kernel(
    core_ref, own_ref, beside_ref, away_ref, down_ref, up_ref, tiles_hbm,
    out_ref, tiles_ref, hi_ref, lo_ref, acc_ref, sems,
):
    for i in range(3):
        tiles_copy(tiles_hbm, tiles_ref, sems, i).start()
    to_beside = jnp.where(core_ref[0] == 0, 3, 0)
    to_away = 3 - to_beside

    def put(ref, at_row, to_x, to_y):
        x = jnp.concatenate(
            [ref[pl.ds(at_row * 96, 48, stride=2), :], ref[pl.ds(at_row * 96 + 1, 48, stride=2), :]],
            axis=1,
        )
        hi, lo = split(x)
        hi_ref[to_x, to_y] = hi
        lo_ref[to_x, to_y] = lo

    for i in range(2):
        for j in range(2):
            put(own_ref, i * 2 + j, 1 + i, 1 + j)
        put(beside_ref, i, to_beside, 1 + i)
        put(away_ref, i, to_away, 1 + i)
    for i, to_x in enumerate((1, 2, to_beside, to_away)):
        put(down_ref, i, to_x, 0)
        put(up_ref, i, to_x, 3)
    acc_ref[...] = jnp.zeros_like(acc_ref)

    @pl.loop(0, 3)
    def _(dx):
        tiles_copy(tiles_hbm, tiles_ref, sems, dx).wait()
        for dy in range(3):
            hi = hi_ref[pl.ds(dx, 2), dy : dy + 2].reshape(192, 256)
            lo = lo_ref[pl.ds(dx, 2), dy : dy + 2].reshape(192, 256)
            for dz in range(3):
                re = tiles_ref[dx * 9 + dy * 3 + dz, 0]
                im = tiles_ref[dx * 9 + dy * 3 + dz, 1]
                matrix = jnp.concatenate(
                    [jnp.concatenate([re, -im], axis=1), jnp.concatenate([im, re], axis=1)], axis=0
                )
                y = dot3((hi, lo), split(matrix), NT).reshape(4, 48, 256)
                if dz == 0:
                    acc_ref[:, 8:48] += y[:, 0:40]
                elif dz == 1:
                    acc_ref[...] += y
                else:
                    acc_ref[:, 0:40] += y[:, 8:48]

    out_ref[...] = acc_ref[...].reshape(192, 256)


def translate_kernel(
    slots_ref, kinds_ref, table_ref, src_ref, beside_ref, away_ref,
    keep_ref, swap_ref, far_ref, acc_ref,
):
    acc_ref[...] = jnp.zeros_like(acc_ref)
    row = lax.broadcasted_iota(jnp.int32, (8, 128), 0)

    def tile(first):
        return pl.ds(pl.multiple_of(first, 8), 8)

    def source(s, carry):
        part = src_ref[s]
        both = jnp.concatenate([part, part], axis=0)
        both = jnp.where(row < 4, both, times_i(both))
        slots, sums = [], []
        for f in range(16):
            slot = slots_ref[s * 16 + f]
            slots.append(slot)
            kind = kinds_ref[s * 16 + f]
            sums.append(acc_ref[tile(slot), :] + table_ref[tile(kind), :] * both)
        for f in range(16):
            acc_ref[tile(slots[f]), :] = sums[f]
        return carry

    lax.fori_loop(0, 96, source, 0, unroll=4)

    def folded(block):
        part = acc_ref[pl.ds(block * 768, 768), :].reshape(96, 8, 128)
        return part[:, :4] + part[:, 4:]

    for block in range(3):
        keep_ref[block] = folded(block)
        swap_ref[block] = folded(block + 3)
    far_ref[...] = folded(6)


def fold_kernel(
    keep_ref, got_ref, cur_ref, beside_ref, away_ref, back_ref, mid_ref, ahead_ref, down_ref, up_ref
):
    back_ref[...] = keep_ref[0] + got_ref[0]
    mid_ref[...] = keep_ref[1] + got_ref[1]
    ahead_ref[...] = keep_ref[2] + got_ref[2]
    for ref, j in ((down_ref, 1), (up_ref, 0)):
        for i in range(2):
            ref[pl.ds(i * 96, 96), :] = cur_ref[pl.ds(i * 192 + j * 96, 96), :]
        ref[pl.ds(192, 96), :] = beside_ref[pl.ds(j * 96, 96), :]
        ref[pl.ds(288, 96), :] = away_ref[pl.ds(j * 96, 96), :]


def join_kernel(mid_ref, far_ref, back_ref, ahead_ref, out_ref):
    out_ref[...] = (mid_ref[...] + far_ref[...]) + (back_ref[...] + ahead_ref[...])


def call(kernel, out_shape, scratch=(), in_specs=None, flops=0, moved=0, vmem_bytes=VMEM_BYTES):
    extra = {} if in_specs is None else {"in_specs": in_specs}
    return pl.pallas_call(
        kernel,
        out_shape=out_shape,
        scratch_shapes=list(scratch),
        compiler_params=pltpu.CompilerParams(vmem_limit_bytes=vmem_bytes),
        cost_estimate=pl.CostEstimate(flops=flops, bytes_accessed=moved, transcendentals=0),
        **extra,
    )


def f32(*shape):
    return jax.ShapeDtypeStruct(shape, F32)


def pair_words(far_targets, far_offsets):
    slab = lax.axis_index("slab")
    ring = slab % 8
    y, core = ring // 2, ring % 2

    def own(table):
        return jnp.concatenate(
            [lax.dynamic_slice_in_dim(table, (ring + z_hi * 8) * 48, 48, 0) for z_hi in range(2)]
        )

    targets, kinds = own(far_targets), own(far_offsets)
    to_slab, row = targets // 48, targets % 48
    half, to_ring = to_slab // 8, to_slab % 8
    step = (to_ring // 2 - y + 4) % 4
    near_block = (step + 1) % 4 + jnp.where(to_ring % 2 == core, 0, 3)
    block = jnp.where(step == 2, 6, near_block)
    slot = block * 96 + half * 48 + row
    return (slot * 8).reshape(-1), (kinds * 8).reshape(-1)


def operator_table(translators):
    count = translators.shape[0]
    half = lax.axis_index("slab") // 8
    own = lax.dynamic_slice_in_dim(translators, half * 32, 32, 2)
    lanes = jnp.concatenate([own] * 4, axis=2)
    return jnp.broadcast_to(lanes[:, :, None, :], (count, 2, 4, 128)).reshape(count * 8, 128)


def moved_by(block, move):
    return lax.ppermute(block, AXES, route_of(move))


def spread(block, groups):
    return lax.all_to_all(
        block, AXES, split_axis=0, concat_axis=0, axis_index_groups=groups, tiled=True
    )


def per_device(currents, near_tiles, radiation, child_phase, translators, far_targets, far_offsets):
    groups = exchange_groups()
    rows = currents.reshape(384, 128)
    core = (lax.axis_index("slab") % 2).astype(jnp.int32).reshape(1)
    slots, kinds = pair_words(far_targets, far_offsets)
    table = operator_table(translators)
    vmem = pl.BlockSpec(memory_space=pltpu.VMEM)
    smem = pl.BlockSpec(memory_space=pltpu.SMEM)
    hbm = pl.BlockSpec(memory_space=pl.ANY)

    patterns, beside, away = call(
        aggregate_kernel,
        (f32(32, 3, 4, 128), f32(192, 128), f32(192, 128)),
        [
            pltpu.VMEM((384, 128), F32),
            pltpu.VMEM((2, 1024, 128), F32),
            pltpu.VMEM((8, 1024), F32),
            pltpu.SemaphoreType.DMA((6,)),
        ],
        in_specs=[smem] + [hbm] * 3,
        flops=600_000_000,
        moved=2_000_000,
        vmem_bytes=62 * 1024 * 1024,
    )(core, rows, radiation, child_phase)
    moved = spread(patterns, groups)
    beside = moved_by(beside, lambda z_hi, y, core, d: (z_hi, y, 1 - core, d))
    away = lax.ppermute(
        away, "slab", [(s, s + 2 * (s % 2) - 1) for s in range(16) if 0 <= s + 2 * (s % 2) - 1 < 16]
    )

    keep, swap, far = call(
        translate_kernel,
        (f32(3, 96, 4, 128), f32(3, 96, 4, 128), f32(96, 4, 128)),
        [pltpu.VMEM((5376, 128), F32)],
        in_specs=[smem, smem, vmem, vmem, hbm, hbm],
        flops=100_000_000,
        moved=3_000_000,
    )(slots, kinds, table, moved.reshape(96, 4, 128), beside, away)
    far_in = moved_by(far, lambda z_hi, y, core, d: (z_hi, (y + 2) % 4, 1 - core, d))
    swap_in = moved_by(swap, lambda z_hi, y, core, d: (z_hi, y, 1 - core, d))
    back, mid, ahead, down, up = call(
        fold_kernel,
        (f32(96, 4, 128),) * 3 + (f32(384, 128),) * 2,
        flops=1_000_000,
        moved=2_000_000,
    )(keep, swap_in, rows, beside, away)
    back_in = moved_by(back, lambda z_hi, y, core, d: (z_hi, (y + 3) % 4, core, d))
    ahead_in = moved_by(ahead, lambda z_hi, y, core, d: (z_hi, (y + 1) % 4, core, d))
    down = lax.ppermute(down, "dir", [(d, d + 1) for d in range(15)])
    up = lax.ppermute(up, "dir", [(d + 1, d) for d in range(15)])
    incoming = call(
        join_kernel, f32(96, 4, 128), flops=1_000_000, moved=1_000_000
    )(mid, far_in, back_in, ahead_in)
    returned = spread(incoming.reshape(32, 3, 4, 128), groups)

    near = call(
        near_kernel,
        f32(192, 256),
        [
            pltpu.VMEM((27, 2, 128, 128), F32),
            pltpu.VMEM((4, 4, 48, 256), BF16),
            pltpu.VMEM((4, 4, 48, 256), BF16),
            pltpu.VMEM((4, 48, 256), F32),
            pltpu.SemaphoreType.DMA((3,)),
        ],
        in_specs=[smem] + [vmem] * 5 + [hbm],
        flops=2_000_000_000,
        moved=5_000_000,
        vmem_bytes=50 * 1024 * 1024,
    )(core, rows, beside, away, down, up, near_tiles)

    applied = call(
        disaggregate_kernel,
        f32(384, 128),
        [pltpu.VMEM((192, 256), F32)],
        flops=600_000_000,
        moved=2_000_000,
    )(returned, radiation, child_phase, near)
    return applied.reshape(currents.shape)


def solution(mesh):
    in_specs = (
        P("slab", "dir", None, None, None, None),
        P(),
        P(),
        P(),
        P(None, None, "dir"),
        P(),
        P(),
    )
    out_specs = P("slab", "dir", None, None, None, None)
    return jax.shard_map(
        per_device, mesh=mesh, in_specs=in_specs, out_specs=out_specs, check_vma=False
    )
```

```python
import functools

import jax
import jax.numpy as jnp
from jax import lax
from jax.experimental import pallas as pl
from jax.experimental.pallas import tpu as pltpu
from jax.sharding import PartitionSpec as P

F32 = jnp.float32
BF16 = jnp.bfloat16
AXES = ("slab", "dir")
VMEM_BYTES = 32 * 1024 * 1024
NT = (((1,), (1,)), ((), ()))
NN = (((1,), (0,)), ((), ()))


def linear(z_hi, y, core, d):
    return (z_hi * 8 + y * 2 + core) * 16 + d


def route_of(move):
    pairs = []
    for s in range(16):
        for d in range(16):
            to = move(s // 8, s // 2 % 4, s % 2, d)
            if to is not None:
                pairs.append((s * 16 + d, linear(*to)))
    return pairs


def exchange_groups():
    return [
        [linear(z_hi, j // 2, j % 2, d) for z_hi in range(2) for d in range(16)] for j in range(8)
    ]


def split(x):
    hi = x.astype(BF16)
    lo = (x - hi.astype(F32)).astype(BF16)
    return hi, lo


def dot3(a, b, dims):
    a_hi, a_lo = a
    b_hi, b_lo = b
    dot = functools.partial(lax.dot_general, dimension_numbers=dims, preferred_element_type=F32)
    return dot(a_hi, b_hi) + (dot(a_lo, b_hi) + dot(a_hi, b_lo))


def lane_sign(shape):
    lane = lax.broadcasted_iota(jnp.int32, shape, len(shape) - 1) % 128
    return jnp.where(lane < 64, -1.0, 1.0).astype(F32)


def times_i(x):
    return lane_sign(x.shape) * pltpu.roll(x, 64, 1)


def swap_bits(x):
    row = lax.broadcasted_iota(jnp.int32, x.shape, 0) // 4 % 2
    lane = lax.broadcasted_iota(jnp.int32, x.shape, 1) // 32 % 2
    other = pltpu.roll(x, 4, 0)
    moved = jnp.where(lane == 1, pltpu.roll(other, 32, 1), pltpu.roll(other, 96, 1))
    return jnp.where(row == lane, x, moved)


def radiation_copy(rad_hbm, rad_ref, sems, i):
    block = pl.ds(pl.multiple_of(i * 256, 256), 256)
    return pltpu.make_async_copy(rad_hbm.at[:, block], rad_ref.at[:, block], sems.at[i])


def tiles_copy(tiles_hbm, tiles_ref, sems, i):
    block = pl.ds(i * 9, 9)
    return pltpu.make_async_copy(tiles_hbm.at[block], tiles_ref.at[block], sems.at[i])


def radiation_block(rad_ref, start):
    re = rad_ref[0, pl.ds(start, 128), :]
    im = rad_ref[1, pl.ds(start, 128), :]
    top = jnp.concatenate([re, -im], axis=1)
    low = jnp.concatenate([im, re], axis=1)
    return split(jnp.concatenate([top[:64], low[:64], top[64:], low[64:]], axis=0))


def phase_block(phase_ref, start):
    phase = phase_ref[:, pl.ds(start, 128)]
    lane = lax.broadcasted_iota(jnp.int32, phase.shape, 1)

    def doubled(v):
        turned = pltpu.roll(v, 64, 1)
        return jnp.concatenate(
            [jnp.where(lane < 64, v, turned), jnp.where(lane < 64, turned, v)], axis=1
        )

    return doubled(jnp.cos(phase)), doubled(jnp.sin(phase))


def leaf_row(child, parent):
    i, j, l = child // 4, child // 2 % 2, child % 2
    return ((i * 2 + j) * 6 + parent * 2 + l) * 8


def aggregate_kernel(
    cur_hbm, rad_hbm, phase_hbm, out_ref, down_ref, up_ref, cur_ref, rad_ref, phase_ref, sems,
    unroll=8, groups=(8,),
):
    cur_copy = pltpu.make_async_copy(cur_hbm, cur_ref, sems.at[4])
    phase_copy = pltpu.make_async_copy(phase_hbm, phase_ref, sems.at[5])
    cur_copy.start()
    for i in range(4):
        radiation_copy(rad_hbm, rad_ref, sems, i).start()
        if i == 1:
            phase_copy.start()
    cur_copy.wait()
    for i in range(2):
        down_ref[pl.ds(i * 96, 96), :] = cur_ref[pl.ds(i * 192 + 96, 96), :]
        up_ref[pl.ds(i * 96, 96), :] = cur_ref[pl.ds(i * 192, 96), :]
    rows = cur_ref.shape[0] // 2
    x = jnp.concatenate(
        [cur_ref[pl.ds(0, rows, stride=2), :], cur_ref[pl.ds(1, rows, stride=2), :]], axis=1
    )
    x = split(x)

    def directions(step, carry):
        start = pl.multiple_of(step * 128, 128)
        leaf = dot3(x, radiation_block(rad_ref, start), NT)
        cos, sin = phase_block(phase_ref, start)
        for parent in range(3):
            a = jnp.zeros((8, 256), F32)
            b = jnp.zeros((8, 256), F32)
            for child in range(8):
                row = leaf_row(child, parent)
                part = leaf[row : row + 8]
                a = a + cos[child : child + 1] * part
                b = b + sin[child : child + 1] * part
            for pair in range(2):
                lanes = slice(pair * 128, pair * 128 + 128)
                block = swap_bits(a[:, lanes] + times_i(b[:, lanes]))
                d = step * 2 + pair
                out_ref[d, parent] = block[:4]
                out_ref[16 + d, parent] = block[4:]
        return carry

    phase_copy.wait()
    first = 0
    for count in groups:
        for i in range(first // 2, (first + count) // 2):
            radiation_copy(rad_hbm, rad_ref, sems, i).wait()
        lax.fori_loop(first, first + count, directions, 0, unroll=unroll)
        first += count


def disaggregate_kernel(in_ref, rad_ref, phase_ref, near_ref, out_ref, acc_ref, unroll=8):
    acc_ref[...] = near_ref[...]

    def directions(step, carry):
        start = pl.multiple_of(step * 128, 128)
        cos, sin = phase_block(phase_ref, start)
        parents = []
        for parent in range(3):
            halves = []
            for pair in range(2):
                d = step * 2 + pair
                block = jnp.concatenate([in_ref[d, parent], in_ref[16 + d, parent]], axis=0)
                halves.append(swap_bits(block))
            turned = jnp.concatenate([times_i(h) for h in halves], axis=1)
            parents.append((jnp.concatenate(halves, axis=1), turned))
        rows = [None] * 24
        for parent in range(3):
            plain, turned = parents[parent]
            for child in range(8):
                rows[leaf_row(child, parent) // 8] = (
                    cos[child : child + 1] * plain - sin[child : child + 1] * turned
                )
        children = split(jnp.concatenate(rows, axis=0))
        acc_ref[...] += dot3(children, radiation_block(rad_ref, start), NN)
        return carry

    lax.fori_loop(0, 8, directions, 0, unroll=unroll)
    rows = acc_ref.shape[0]
    out_ref[pl.ds(0, rows, stride=2), :] = acc_ref[:, :128]
    out_ref[pl.ds(1, rows, stride=2), :] = acc_ref[:, 128:]


def near_kernel(
    core_ref, own_ref, beside_ref, away_ref, down_ref, up_ref, tiles_hbm,
    out_ref, tiles_ref, hi_ref, lo_ref, acc_ref, sems,
):
    for i in range(3):
        tiles_copy(tiles_hbm, tiles_ref, sems, i).start()
    to_beside = jnp.where(core_ref[0] == 0, 3, 0)
    to_away = 3 - to_beside

    def put(ref, at_row, to_x, to_y):
        x = jnp.concatenate(
            [ref[pl.ds(at_row * 96, 48, stride=2), :], ref[pl.ds(at_row * 96 + 1, 48, stride=2), :]],
            axis=1,
        )
        hi, lo = split(x)
        hi_ref[to_x, to_y] = hi
        lo_ref[to_x, to_y] = lo

    for i in range(2):
        for j in range(2):
            put(own_ref, i * 2 + j, 1 + i, 1 + j)
        put(down_ref, i, 1 + i, 0)
        put(up_ref, i, 1 + i, 3)
    for i, to_y in enumerate((1, 2, 0, 3)):
        put(beside_ref, i, to_beside, to_y)
        put(away_ref, i, to_away, to_y)
    acc_ref[...] = jnp.zeros_like(acc_ref)

    @pl.loop(0, 3)
    def _(dx):
        tiles_copy(tiles_hbm, tiles_ref, sems, dx).wait()
        for dy in range(3):
            hi = hi_ref[pl.ds(dx, 2), dy : dy + 2].reshape(192, 256)
            lo = lo_ref[pl.ds(dx, 2), dy : dy + 2].reshape(192, 256)
            for dz in range(3):
                re = tiles_ref[dx * 9 + dy * 3 + dz, 0]
                im = tiles_ref[dx * 9 + dy * 3 + dz, 1]
                matrix = jnp.concatenate(
                    [jnp.concatenate([re, -im], axis=1), jnp.concatenate([im, re], axis=1)], axis=0
                )
                y = dot3((hi, lo), split(matrix), NT).reshape(4, 48, 256)
                if dz == 0:
                    acc_ref[:, 8:48] += y[:, 0:40]
                elif dz == 1:
                    acc_ref[...] += y
                else:
                    acc_ref[:, 0:40] += y[:, 8:48]

    out_ref[...] = acc_ref[...].reshape(192, 256)


def translate_kernel(
    slots_ref, kinds_ref, table_ref, src_ref, down_ref, up_ref,
    keep_ref, swap_ref, far_ref, acc_ref,
):
    acc_ref[...] = jnp.zeros_like(acc_ref)
    row = lax.broadcasted_iota(jnp.int32, (8, 128), 0)

    def tile(first):
        return pl.ds(pl.multiple_of(first, 8), 8)

    def source(s, carry):
        part = src_ref[s]
        both = jnp.concatenate([part, part], axis=0)
        both = jnp.where(row < 4, both, times_i(both))
        slots, sums = [], []
        for f in range(16):
            slot = slots_ref[s * 16 + f]
            slots.append(slot)
            kind = kinds_ref[s * 16 + f]
            sums.append(acc_ref[tile(slot), :] + table_ref[tile(kind), :] * both)
        for f in range(16):
            acc_ref[tile(slots[f]), :] = sums[f]
        return carry

    lax.fori_loop(0, 96, source, 0, unroll=4)

    def folded(block):
        part = acc_ref[pl.ds(block * 768, 768), :].reshape(96, 8, 128)
        return part[:, :4] + part[:, 4:]

    for block in range(3):
        keep_ref[block] = folded(block)
        swap_ref[block] = folded(block + 3)
    far_ref[...] = folded(6)


def fold_kernel(
    core_ref, keep_ref, got_ref, cur_ref, down_ref, up_ref,
    back_ref, mid_ref, ahead_ref, beside_ref, away_ref,
):
    back_ref[...] = keep_ref[0] + got_ref[0]
    mid_ref[...] = keep_ref[1] + got_ref[1]
    ahead_ref[...] = keep_ref[2] + got_ref[2]
    core = core_ref[0]
    for ref, row in ((beside_ref, 1 - core), (away_ref, core)):
        ref[pl.ds(0, 192), :] = cur_ref[pl.ds(pl.multiple_of(row * 192, 8), 192), :]
        ref[pl.ds(192, 96), :] = down_ref[pl.ds(pl.multiple_of(row * 96, 8), 96), :]
        ref[pl.ds(288, 96), :] = up_ref[pl.ds(pl.multiple_of(row * 96, 8), 96), :]


def join_kernel(mid_ref, far_ref, back_ref, ahead_ref, out_ref):
    out_ref[...] = (mid_ref[...] + far_ref[...]) + (back_ref[...] + ahead_ref[...])


def call(kernel, out_shape, scratch=(), in_specs=None, flops=0, moved=0, vmem_bytes=VMEM_BYTES):
    extra = {} if in_specs is None else {"in_specs": in_specs}
    return pl.pallas_call(
        kernel,
        out_shape=out_shape,
        scratch_shapes=list(scratch),
        compiler_params=pltpu.CompilerParams(vmem_limit_bytes=vmem_bytes),
        cost_estimate=pl.CostEstimate(flops=flops, bytes_accessed=moved, transcendentals=0),
        **extra,
    )


def f32(*shape):
    return jax.ShapeDtypeStruct(shape, F32)


def pair_words(far_targets, far_offsets):
    slab = lax.axis_index("slab")
    ring = slab % 8
    y, core = ring // 2, ring % 2

    def own(table):
        return jnp.concatenate(
            [lax.dynamic_slice_in_dim(table, (ring + z_hi * 8) * 48, 48, 0) for z_hi in range(2)]
        )

    targets, kinds = own(far_targets), own(far_offsets)
    to_slab, row = targets // 48, targets % 48
    half, to_ring = to_slab // 8, to_slab % 8
    step = (to_ring // 2 - y + 4) % 4
    near_block = (step + 1) % 4 + jnp.where(to_ring % 2 == core, 0, 3)
    block = jnp.where(step == 2, 6, near_block)
    slot = block * 96 + half * 48 + row
    return (slot * 8).reshape(-1), (kinds * 8).reshape(-1)


def operator_table(translators):
    count = translators.shape[0]
    half = lax.axis_index("slab") // 8
    own = lax.dynamic_slice_in_dim(translators, half * 32, 32, 2)
    lanes = jnp.concatenate([own] * 4, axis=2)
    return jnp.broadcast_to(lanes[:, :, None, :], (count, 2, 4, 128)).reshape(count * 8, 128)


def moved_by(block, move):
    return lax.ppermute(block, AXES, route_of(move))


def spread(block, groups):
    return lax.all_to_all(
        block, AXES, split_axis=0, concat_axis=0, axis_index_groups=groups, tiled=True
    )


def per_device(currents, near_tiles, radiation, child_phase, translators, far_targets, far_offsets):
    groups = exchange_groups()
    rows = currents.reshape(384, 128)
    core = (lax.axis_index("slab") % 2).astype(jnp.int32).reshape(1)
    slots, kinds = pair_words(far_targets, far_offsets)
    table = operator_table(translators)
    vmem = pl.BlockSpec(memory_space=pltpu.VMEM)
    smem = pl.BlockSpec(memory_space=pltpu.SMEM)
    hbm = pl.BlockSpec(memory_space=pl.ANY)

    patterns, down, up = call(
        aggregate_kernel,
        (f32(32, 3, 4, 128), f32(192, 128), f32(192, 128)),
        [
            pltpu.VMEM((384, 128), F32),
            pltpu.VMEM((2, 1024, 128), F32),
            pltpu.VMEM((8, 1024), F32),
            pltpu.SemaphoreType.DMA((6,)),
        ],
        in_specs=[hbm] * 3,
        flops=600_000_000,
        moved=2_000_000,
        vmem_bytes=62 * 1024 * 1024,
    )(rows, radiation, child_phase)
    moved = spread(patterns, groups)
    down = lax.ppermute(down, "dir", [(d, d + 1) for d in range(15)])
    up = lax.ppermute(up, "dir", [(d + 1, d) for d in range(15)])

    keep, swap, far = call(
        translate_kernel,
        (f32(3, 96, 4, 128), f32(3, 96, 4, 128), f32(96, 4, 128)),
        [pltpu.VMEM((5376, 128), F32)],
        in_specs=[smem, smem, vmem, vmem, hbm, hbm],
        flops=100_000_000,
        moved=3_000_000,
    )(slots, kinds, table, moved.reshape(96, 4, 128), down, up)
    far_in = moved_by(far, lambda z_hi, y, core, d: (z_hi, (y + 2) % 4, 1 - core, d))
    swap_in = moved_by(swap, lambda z_hi, y, core, d: (z_hi, y, 1 - core, d))
    back, mid, ahead, beside, away = call(
        fold_kernel,
        (f32(96, 4, 128),) * 3 + (f32(384, 128),) * 2,
        in_specs=[smem] + [vmem] * 5,
        flops=1_000_000,
        moved=2_000_000,
    )(core, keep, swap_in, rows, down, up)
    back_in = moved_by(back, lambda z_hi, y, core, d: (z_hi, (y + 3) % 4, core, d))
    ahead_in = moved_by(ahead, lambda z_hi, y, core, d: (z_hi, (y + 1) % 4, core, d))
    beside = moved_by(beside, lambda z_hi, y, core, d: (z_hi, y, 1 - core, d))
    away = lax.ppermute(
        away, "slab", [(s, s + 2 * (s % 2) - 1) for s in range(16) if 0 <= s + 2 * (s % 2) - 1 < 16]
    )
    incoming = call(
        join_kernel, f32(96, 4, 128), flops=1_000_000, moved=1_000_000
    )(mid, far_in, back_in, ahead_in)
    returned = spread(incoming.reshape(32, 3, 4, 128), groups)

    near = call(
        near_kernel,
        f32(192, 256),
        [
            pltpu.VMEM((27, 2, 128, 128), F32),
            pltpu.VMEM((4, 4, 48, 256), BF16),
            pltpu.VMEM((4, 4, 48, 256), BF16),
            pltpu.VMEM((4, 48, 256), F32),
            pltpu.SemaphoreType.DMA((3,)),
        ],
        in_specs=[smem] + [vmem] * 5 + [hbm],
        flops=2_000_000_000,
        moved=5_000_000,
        vmem_bytes=50 * 1024 * 1024,
    )(core, rows, beside, away, down, up, near_tiles)

    applied = call(
        disaggregate_kernel,
        f32(384, 128),
        [pltpu.VMEM((192, 256), F32)],
        flops=600_000_000,
        moved=2_000_000,
    )(returned, radiation, child_phase, near)
    return applied.reshape(currents.shape)


def solution(mesh):
    in_specs = (
        P("slab", "dir", None, None, None, None),
        P(),
        P(),
        P(),
        P(None, None, "dir"),
        P(),
        P(),
    )
    out_specs = P("slab", "dir", None, None, None, None)
    return jax.shard_map(
        per_device, mesh=mesh, in_specs=in_specs, out_specs=out_specs, check_vma=False
    )
```

```python
import functools

import jax
import jax.numpy as jnp
from jax import lax
from jax.experimental import pallas as pl
from jax.experimental.pallas import tpu as pltpu
from jax.sharding import PartitionSpec as P

F32 = jnp.float32
BF16 = jnp.bfloat16
AXES = ("slab", "dir")
VMEM_BYTES = 32 * 1024 * 1024
NT = (((1,), (1,)), ((), ()))
NN = (((1,), (0,)), ((), ()))


def linear(z_hi, y, core, d):
    return (z_hi * 8 + y * 2 + core) * 16 + d


def route_of(move):
    pairs = []
    for s in range(16):
        for d in range(16):
            to = move(s // 8, s // 2 % 4, s % 2, d)
            if to is not None:
                pairs.append((s * 16 + d, linear(*to)))
    return pairs


def exchange_groups():
    return [
        [linear(z_hi, j // 2, j % 2, d) for z_hi in range(2) for d in range(16)] for j in range(8)
    ]


def split(x):
    hi = x.astype(BF16)
    lo = (x - hi.astype(F32)).astype(BF16)
    return hi, lo


def dot3(a, b, dims):
    a_hi, a_lo = a
    b_hi, b_lo = b
    dot = functools.partial(lax.dot_general, dimension_numbers=dims, preferred_element_type=F32)
    return dot(a_hi, b_hi) + (dot(a_lo, b_hi) + dot(a_hi, b_lo))


def lane_sign(shape):
    lane = lax.broadcasted_iota(jnp.int32, shape, len(shape) - 1) % 128
    return jnp.where(lane < 64, -1.0, 1.0).astype(F32)


def times_i(x):
    return lane_sign(x.shape) * pltpu.roll(x, 64, 1)


def swap_bits(x):
    row = lax.broadcasted_iota(jnp.int32, x.shape, 0) // 4 % 2
    lane = lax.broadcasted_iota(jnp.int32, x.shape, 1) // 32 % 2
    other = pltpu.roll(x, 4, 0)
    moved = jnp.where(lane == 1, pltpu.roll(other, 32, 1), pltpu.roll(other, 96, 1))
    return jnp.where(row == lane, x, moved)


def radiation_copy(rad_hbm, rad_ref, sems, i):
    block = pl.ds(pl.multiple_of(i * 256, 256), 256)
    return pltpu.make_async_copy(rad_hbm.at[:, block], rad_ref.at[:, block], sems.at[i])


def tiles_copy(tiles_hbm, tiles_ref, sems, i):
    block = pl.ds(i * 9, 9)
    return pltpu.make_async_copy(tiles_hbm.at[block], tiles_ref.at[block], sems.at[i])


def radiation_block(rad_ref, start):
    re = rad_ref[0, pl.ds(start, 128), :]
    im = rad_ref[1, pl.ds(start, 128), :]
    top = jnp.concatenate([re, -im], axis=1)
    low = jnp.concatenate([im, re], axis=1)
    return split(jnp.concatenate([top[:64], low[:64], top[64:], low[64:]], axis=0))


def phase_block(phase_ref, start):
    phase = phase_ref[:, pl.ds(start, 128)]
    lane = lax.broadcasted_iota(jnp.int32, phase.shape, 1)

    def doubled(v):
        turned = pltpu.roll(v, 64, 1)
        return jnp.concatenate(
            [jnp.where(lane < 64, v, turned), jnp.where(lane < 64, turned, v)], axis=1
        )

    return doubled(jnp.cos(phase)), doubled(jnp.sin(phase))


def leaf_row(child, parent):
    i, j, l = child // 4, child // 2 % 2, child % 2
    return ((i * 2 + j) * 6 + parent * 2 + l) * 8


def aggregate_kernel(
    cur_hbm, rad_hbm, phase_hbm, out_ref, down_ref, up_ref, cur_ref, rad_ref, phase_ref, sems,
    unroll=8, groups=(8,),
):
    cur_copy = pltpu.make_async_copy(cur_hbm, cur_ref, sems.at[4])
    phase_copy = pltpu.make_async_copy(phase_hbm, phase_ref, sems.at[5])
    cur_copy.start()
    for i in range(4):
        radiation_copy(rad_hbm, rad_ref, sems, i).start()
        if i == 1:
            phase_copy.start()
    cur_copy.wait()
    for i in range(2):
        down_ref[pl.ds(i * 96, 96), :] = cur_ref[pl.ds(i * 192 + 96, 96), :]
        up_ref[pl.ds(i * 96, 96), :] = cur_ref[pl.ds(i * 192, 96), :]
    rows = cur_ref.shape[0] // 2
    x = jnp.concatenate(
        [cur_ref[pl.ds(0, rows, stride=2), :], cur_ref[pl.ds(1, rows, stride=2), :]], axis=1
    )
    x = split(x)

    def directions(step, carry):
        start = pl.multiple_of(step * 128, 128)
        leaf = dot3(x, radiation_block(rad_ref, start), NT)
        cos, sin = phase_block(phase_ref, start)
        for parent in range(3):
            a = jnp.zeros((8, 256), F32)
            b = jnp.zeros((8, 256), F32)
            for child in range(8):
                row = leaf_row(child, parent)
                part = leaf[row : row + 8]
                a = a + cos[child : child + 1] * part
                b = b + sin[child : child + 1] * part
            for pair in range(2):
                lanes = slice(pair * 128, pair * 128 + 128)
                block = swap_bits(a[:, lanes] + times_i(b[:, lanes]))
                d = step * 2 + pair
                out_ref[d, parent] = block[:4]
                out_ref[16 + d, parent] = block[4:]
        return carry

    phase_copy.wait()
    first = 0
    for count in groups:
        for i in range(first // 2, (first + count) // 2):
            radiation_copy(rad_hbm, rad_ref, sems, i).wait()
        lax.fori_loop(first, first + count, directions, 0, unroll=unroll)
        first += count


def disaggregate_kernel(in_ref, rad_ref, phase_ref, near_ref, out_ref, acc_ref, unroll=8):
    acc_ref[...] = near_ref[...]

    def directions(step, carry):
        start = pl.multiple_of(step * 128, 128)
        cos, sin = phase_block(phase_ref, start)
        parents = []
        for parent in range(3):
            halves = []
            for pair in range(2):
                d = step * 2 + pair
                block = jnp.concatenate([in_ref[d, parent], in_ref[16 + d, parent]], axis=0)
                halves.append(swap_bits(block))
            turned = jnp.concatenate([times_i(h) for h in halves], axis=1)
            parents.append((jnp.concatenate(halves, axis=1), turned))
        rows = [None] * 24
        for parent in range(3):
            plain, turned = parents[parent]
            for child in range(8):
                rows[leaf_row(child, parent) // 8] = (
                    cos[child : child + 1] * plain - sin[child : child + 1] * turned
                )
        children = split(jnp.concatenate(rows, axis=0))
        acc_ref[...] += dot3(children, radiation_block(rad_ref, start), NN)
        return carry

    lax.fori_loop(0, 8, directions, 0, unroll=unroll)
    rows = acc_ref.shape[0]
    out_ref[pl.ds(0, rows, stride=2), :] = acc_ref[:, :128]
    out_ref[pl.ds(1, rows, stride=2), :] = acc_ref[:, 128:]


def near_kernel(
    core_ref, own_ref, beside_ref, away_ref, down_ref, up_ref, tiles_hbm,
    out_ref, tiles_ref, hi_ref, lo_ref, acc_ref, sems,
):
    for i in range(3):
        tiles_copy(tiles_hbm, tiles_ref, sems, i).start()
    to_beside = jnp.where(core_ref[0] == 0, 3, 0)
    to_away = 3 - to_beside

    def put(ref, at_row, to_x, to_y):
        x = jnp.concatenate(
            [ref[pl.ds(at_row * 96, 48, stride=2), :], ref[pl.ds(at_row * 96 + 1, 48, stride=2), :]],
            axis=1,
        )
        hi, lo = split(x)
        hi_ref[to_x, to_y] = hi
        lo_ref[to_x, to_y] = lo

    for i in range(2):
        for j in range(2):
            put(own_ref, i * 2 + j, 1 + i, 1 + j)
        put(down_ref, i, 1 + i, 0)
        put(up_ref, i, 1 + i, 3)
    for i, to_y in enumerate((1, 2, 0, 3)):
        put(beside_ref, i, to_beside, to_y)
        put(away_ref, i, to_away, to_y)
    acc_ref[...] = jnp.zeros_like(acc_ref)

    @pl.loop(0, 3)
    def _(dx):
        tiles_copy(tiles_hbm, tiles_ref, sems, dx).wait()
        for dy in range(3):
            hi = hi_ref[pl.ds(dx, 2), dy : dy + 2].reshape(192, 256)
            lo = lo_ref[pl.ds(dx, 2), dy : dy + 2].reshape(192, 256)
            for dz in range(3):
                re = tiles_ref[dx * 9 + dy * 3 + dz, 0]
                im = tiles_ref[dx * 9 + dy * 3 + dz, 1]
                matrix = jnp.concatenate(
                    [jnp.concatenate([re, -im], axis=1), jnp.concatenate([im, re], axis=1)], axis=0
                )
                y = dot3((hi, lo), split(matrix), NT).reshape(4, 48, 256)
                if dz == 0:
                    acc_ref[:, 8:48] += y[:, 0:40]
                elif dz == 1:
                    acc_ref[...] += y
                else:
                    acc_ref[:, 0:40] += y[:, 8:48]

    out_ref[...] = acc_ref[...].reshape(192, 256)


def translate_kernel(
    slots_ref, kinds_ref, table_ref, src_ref, down_ref, up_ref,
    keep_ref, swap_ref, far_ref, acc_ref,
):
    acc_ref[...] = jnp.zeros_like(acc_ref)
    row = lax.broadcasted_iota(jnp.int32, (8, 128), 0)

    def tile(first):
        return pl.ds(pl.multiple_of(first, 8), 8)

    def source(s, carry):
        part = src_ref[s]
        both = jnp.concatenate([part, part], axis=0)
        both = jnp.where(row < 4, both, times_i(both))
        slots, sums = [], []
        for f in range(16):
            slot = slots_ref[s * 16 + f]
            slots.append(slot)
            kind = kinds_ref[s * 16 + f]
            sums.append(acc_ref[tile(slot), :] + table_ref[tile(kind), :] * both)
        for f in range(16):
            acc_ref[tile(slots[f]), :] = sums[f]
        return carry

    lax.fori_loop(0, 96, source, 0, unroll=4)

    def folded(block):
        part = acc_ref[pl.ds(block * 768, 768), :].reshape(96, 8, 128)
        return part[:, :4] + part[:, 4:]

    for block in range(3):
        keep_ref[block] = folded(block)
        swap_ref[block] = folded(block + 3)
    far_ref[...] = folded(6)


def fold_kernel(
    core_ref, keep_ref, got_ref, cur_ref, down_ref, up_ref,
    back_ref, mid_ref, ahead_ref, beside_ref, away_ref,
):
    back_ref[...] = keep_ref[0] + got_ref[0]
    mid_ref[...] = keep_ref[1] + got_ref[1]
    ahead_ref[...] = keep_ref[2] + got_ref[2]
    core = core_ref[0]
    for ref, row in ((beside_ref, 1 - core), (away_ref, core)):
        ref[pl.ds(0, 192), :] = cur_ref[pl.ds(pl.multiple_of(row * 192, 8), 192), :]
        ref[pl.ds(192, 96), :] = down_ref[pl.ds(pl.multiple_of(row * 96, 8), 96), :]
        ref[pl.ds(288, 96), :] = up_ref[pl.ds(pl.multiple_of(row * 96, 8), 96), :]


def join_kernel(mid_ref, far_ref, back_ref, ahead_ref, near_ref, out_ref):
    out_ref[...] = (mid_ref[...] + far_ref[...]) + (back_ref[...] + ahead_ref[...])


def call(kernel, out_shape, scratch=(), in_specs=None, flops=0, moved=0, vmem_bytes=VMEM_BYTES):
    extra = {} if in_specs is None else {"in_specs": in_specs}
    return pl.pallas_call(
        kernel,
        out_shape=out_shape,
        scratch_shapes=list(scratch),
        compiler_params=pltpu.CompilerParams(vmem_limit_bytes=vmem_bytes),
        cost_estimate=pl.CostEstimate(flops=flops, bytes_accessed=moved, transcendentals=0),
        **extra,
    )


def f32(*shape):
    return jax.ShapeDtypeStruct(shape, F32)


def pair_words(far_targets, far_offsets):
    slab = lax.axis_index("slab")
    ring = slab % 8
    y, core = ring // 2, ring % 2

    def own(table):
        return jnp.concatenate(
            [lax.dynamic_slice_in_dim(table, (ring + z_hi * 8) * 48, 48, 0) for z_hi in range(2)]
        )

    targets, kinds = own(far_targets), own(far_offsets)
    to_slab, row = targets // 48, targets % 48
    half, to_ring = to_slab // 8, to_slab % 8
    step = (to_ring // 2 - y + 4) % 4
    near_block = (step + 1) % 4 + jnp.where(to_ring % 2 == core, 0, 3)
    block = jnp.where(step == 2, 6, near_block)
    slot = block * 96 + half * 48 + row
    return (slot * 8).reshape(-1), (kinds * 8).reshape(-1)


def operator_table(translators):
    count = translators.shape[0]
    half = lax.axis_index("slab") // 8
    own = lax.dynamic_slice_in_dim(translators, half * 32, 32, 2)
    lanes = jnp.concatenate([own] * 4, axis=2)
    return jnp.broadcast_to(lanes[:, :, None, :], (count, 2, 4, 128)).reshape(count * 8, 128)


def moved_by(block, move):
    return lax.ppermute(block, AXES, route_of(move))


def spread(block, groups):
    return lax.all_to_all(
        block, AXES, split_axis=0, concat_axis=0, axis_index_groups=groups, tiled=True
    )


def per_device(currents, near_tiles, radiation, child_phase, translators, far_targets, far_offsets):
    groups = exchange_groups()
    rows = currents.reshape(384, 128)
    core = (lax.axis_index("slab") % 2).astype(jnp.int32).reshape(1)
    slots, kinds = pair_words(far_targets, far_offsets)
    table = operator_table(translators)
    vmem = pl.BlockSpec(memory_space=pltpu.VMEM)
    smem = pl.BlockSpec(memory_space=pltpu.SMEM)
    hbm = pl.BlockSpec(memory_space=pl.ANY)

    patterns, down, up = call(
        aggregate_kernel,
        (f32(32, 3, 4, 128), f32(192, 128), f32(192, 128)),
        [
            pltpu.VMEM((384, 128), F32),
            pltpu.VMEM((2, 1024, 128), F32),
            pltpu.VMEM((8, 1024), F32),
            pltpu.SemaphoreType.DMA((6,)),
        ],
        in_specs=[hbm] * 3,
        flops=600_000_000,
        moved=2_000_000,
        vmem_bytes=62 * 1024 * 1024,
    )(rows, radiation, child_phase)
    moved = spread(patterns, groups)
    down = lax.ppermute(down, "dir", [(d, d + 1) for d in range(15)])
    up = lax.ppermute(up, "dir", [(d + 1, d) for d in range(15)])

    keep, swap, far = call(
        translate_kernel,
        (f32(3, 96, 4, 128), f32(3, 96, 4, 128), f32(96, 4, 128)),
        [pltpu.VMEM((5376, 128), F32)],
        in_specs=[smem, smem, vmem, vmem, hbm, hbm],
        flops=100_000_000,
        moved=3_000_000,
    )(slots, kinds, table, moved.reshape(96, 4, 128), down, up)
    far_in = moved_by(far, lambda z_hi, y, core, d: (z_hi, (y + 2) % 4, 1 - core, d))
    swap_in = moved_by(swap, lambda z_hi, y, core, d: (z_hi, y, 1 - core, d))
    back, mid, ahead, beside, away = call(
        fold_kernel,
        (f32(96, 4, 128),) * 3 + (f32(384, 128),) * 2,
        in_specs=[smem] + [vmem] * 5,
        flops=1_000_000,
        moved=2_000_000,
    )(core, keep, swap_in, rows, down, up)
    back_in = moved_by(back, lambda z_hi, y, core, d: (z_hi, (y + 3) % 4, core, d))
    ahead_in = moved_by(ahead, lambda z_hi, y, core, d: (z_hi, (y + 1) % 4, core, d))
    beside = moved_by(beside, lambda z_hi, y, core, d: (z_hi, y, 1 - core, d))
    away = lax.ppermute(
        away, "slab", [(s, s + 2 * (s % 2) - 1) for s in range(16) if 0 <= s + 2 * (s % 2) - 1 < 16]
    )
    near = call(
        near_kernel,
        f32(192, 256),
        [
            pltpu.VMEM((27, 2, 128, 128), F32),
            pltpu.VMEM((4, 4, 48, 256), BF16),
            pltpu.VMEM((4, 4, 48, 256), BF16),
            pltpu.VMEM((4, 48, 256), F32),
            pltpu.SemaphoreType.DMA((3,)),
        ],
        in_specs=[smem] + [vmem] * 5 + [hbm],
        flops=2_000_000_000,
        moved=5_000_000,
        vmem_bytes=50 * 1024 * 1024,
    )(core, rows, beside, away, down, up, near_tiles)

    incoming = call(
        join_kernel,
        f32(96, 4, 128),
        in_specs=[vmem] * 4 + [hbm],
        flops=1_000_000,
        moved=1_000_000,
    )(mid, far_in, back_in, ahead_in, near)
    returned = spread(incoming.reshape(32, 3, 4, 128), groups)

    applied = call(
        disaggregate_kernel,
        f32(384, 128),
        [pltpu.VMEM((192, 256), F32)],
        flops=600_000_000,
        moved=2_000_000,
    )(returned, radiation, child_phase, near)
    return applied.reshape(currents.shape)


def solution(mesh):
    in_specs = (
        P("slab", "dir", None, None, None, None),
        P(),
        P(),
        P(),
        P(None, None, "dir"),
        P(),
        P(),
    )
    out_specs = P("slab", "dir", None, None, None, None)
    return jax.shard_map(
        per_device, mesh=mesh, in_specs=in_specs, out_specs=out_specs, check_vma=False
    )
```

```python
import functools

import jax
import jax.numpy as jnp
from jax import lax
from jax.experimental import pallas as pl
from jax.experimental.pallas import tpu as pltpu
from jax.sharding import PartitionSpec as P

F32 = jnp.float32
BF16 = jnp.bfloat16
AXES = ("slab", "dir")
VMEM_BYTES = 32 * 1024 * 1024
NT = (((1,), (1,)), ((), ()))
NN = (((1,), (0,)), ((), ()))


def linear(z_hi, y, core, d):
    return (z_hi * 8 + y * 2 + core) * 16 + d


def route_of(move):
    pairs = []
    for s in range(16):
        for d in range(16):
            to = move(s // 8, s // 2 % 4, s % 2, d)
            if to is not None:
                pairs.append((s * 16 + d, linear(*to)))
    return pairs


def exchange_groups():
    return [
        [linear(z_hi, j // 2, j % 2, d) for z_hi in range(2) for d in range(16)] for j in range(8)
    ]


def split(x):
    hi = x.astype(BF16)
    lo = (x - hi.astype(F32)).astype(BF16)
    return hi, lo


def dot3(a, b, dims):
    a_hi, a_lo = a
    b_hi, b_lo = b
    dot = functools.partial(lax.dot_general, dimension_numbers=dims, preferred_element_type=F32)
    return dot(a_hi, b_hi) + (dot(a_lo, b_hi) + dot(a_hi, b_lo))


def lane_sign(shape):
    lane = lax.broadcasted_iota(jnp.int32, shape, len(shape) - 1) % 128
    return jnp.where(lane < 64, -1.0, 1.0).astype(F32)


def times_i(x):
    return lane_sign(x.shape) * pltpu.roll(x, 64, 1)


def swap_bits(x):
    row = lax.broadcasted_iota(jnp.int32, x.shape, 0) // 4 % 2
    lane = lax.broadcasted_iota(jnp.int32, x.shape, 1) // 32 % 2
    other = pltpu.roll(x, 4, 0)
    moved = jnp.where(lane == 1, pltpu.roll(other, 32, 1), pltpu.roll(other, 96, 1))
    return jnp.where(row == lane, x, moved)


def radiation_copy(rad_hbm, rad_ref, sems, i):
    block = pl.ds(pl.multiple_of(i * 256, 256), 256)
    return pltpu.make_async_copy(rad_hbm.at[:, block], rad_ref.at[:, block], sems.at[i])


def tiles_copy(tiles_hbm, tiles_ref, sems, i):
    block = pl.ds(i * 9, 9)
    return pltpu.make_async_copy(tiles_hbm.at[block], tiles_ref.at[block], sems.at[i])


def radiation_block(rad_ref, start):
    re = rad_ref[0, pl.ds(start, 128), :]
    im = rad_ref[1, pl.ds(start, 128), :]
    top = jnp.concatenate([re, -im], axis=1)
    low = jnp.concatenate([im, re], axis=1)
    return split(jnp.concatenate([top[:64], low[:64], top[64:], low[64:]], axis=0))


def phase_block(phase_ref, start):
    phase = phase_ref[:, pl.ds(start, 128)]
    lane = lax.broadcasted_iota(jnp.int32, phase.shape, 1)

    def doubled(v):
        turned = pltpu.roll(v, 64, 1)
        return jnp.concatenate(
            [jnp.where(lane < 64, v, turned), jnp.where(lane < 64, turned, v)], axis=1
        )

    return doubled(jnp.cos(phase)), doubled(jnp.sin(phase))


def leaf_row(child, parent):
    i, j, l = child // 4, child // 2 % 2, child % 2
    return ((i * 2 + j) * 6 + parent * 2 + l) * 8


def aggregate_kernel(
    core_ref, cur_hbm, rad_hbm, phase_hbm, out_ref, one_ref, two_ref, cur_ref, rad_ref, phase_ref, sems,
    unroll=8, groups=(8,),
):
    cur_copy = pltpu.make_async_copy(cur_hbm, cur_ref, sems.at[4])
    phase_copy = pltpu.make_async_copy(phase_hbm, phase_ref, sems.at[5])
    cur_copy.start()
    for i in range(4):
        radiation_copy(rad_hbm, rad_ref, sems, i).start()
        if i == 1:
            phase_copy.start()
    cur_copy.wait()
    core = core_ref[0]
    for ref, j in ((one_ref, 1 - core), (two_ref, core)):
        for i in range(2):
            first = pl.multiple_of(i * 192 + j * 96, 8)
            ref[pl.ds(i * 96, 96), :] = cur_ref[pl.ds(first, 96), :]
    rows = cur_ref.shape[0] // 2
    x = jnp.concatenate(
        [cur_ref[pl.ds(0, rows, stride=2), :], cur_ref[pl.ds(1, rows, stride=2), :]], axis=1
    )
    x = split(x)

    def directions(step, carry):
        start = pl.multiple_of(step * 128, 128)
        leaf = dot3(x, radiation_block(rad_ref, start), NT)
        cos, sin = phase_block(phase_ref, start)
        for parent in range(3):
            a = jnp.zeros((8, 256), F32)
            b = jnp.zeros((8, 256), F32)
            for child in range(8):
                row = leaf_row(child, parent)
                part = leaf[row : row + 8]
                a = a + cos[child : child + 1] * part
                b = b + sin[child : child + 1] * part
            for pair in range(2):
                lanes = slice(pair * 128, pair * 128 + 128)
                block = swap_bits(a[:, lanes] + times_i(b[:, lanes]))
                d = step * 2 + pair
                out_ref[d, parent] = block[:4]
                out_ref[16 + d, parent] = block[4:]
        return carry

    phase_copy.wait()
    first = 0
    for count in groups:
        for i in range(first // 2, (first + count) // 2):
            radiation_copy(rad_hbm, rad_ref, sems, i).wait()
        lax.fori_loop(first, first + count, directions, 0, unroll=unroll)
        first += count


def disaggregate_kernel(in_ref, rad_ref, phase_ref, near_ref, out_ref, acc_ref, unroll=8):
    acc_ref[...] = near_ref[...]

    def directions(step, carry):
        start = pl.multiple_of(step * 128, 128)
        cos, sin = phase_block(phase_ref, start)
        parents = []
        for parent in range(3):
            halves = []
            for pair in range(2):
                d = step * 2 + pair
                block = jnp.concatenate([in_ref[d, parent], in_ref[16 + d, parent]], axis=0)
                halves.append(swap_bits(block))
            turned = jnp.concatenate([times_i(h) for h in halves], axis=1)
            parents.append((jnp.concatenate(halves, axis=1), turned))
        rows = [None] * 24
        for parent in range(3):
            plain, turned = parents[parent]
            for child in range(8):
                rows[leaf_row(child, parent) // 8] = (
                    cos[child : child + 1] * plain - sin[child : child + 1] * turned
                )
        children = split(jnp.concatenate(rows, axis=0))
        acc_ref[...] += dot3(children, radiation_block(rad_ref, start), NN)
        return carry

    lax.fori_loop(0, 8, directions, 0, unroll=unroll)
    rows = acc_ref.shape[0]
    out_ref[pl.ds(0, rows, stride=2), :] = acc_ref[:, :128]
    out_ref[pl.ds(1, rows, stride=2), :] = acc_ref[:, 128:]


def near_kernel(
    core_ref, own_ref, beside_ref, away_ref, one_ref, two_ref, tiles_hbm,
    out_ref, tiles_ref, hi_ref, lo_ref, acc_ref, sems,
):
    for i in range(3):
        tiles_copy(tiles_hbm, tiles_ref, sems, i).start()
    to_beside = jnp.where(core_ref[0] == 0, 3, 0)
    to_away = 3 - to_beside

    def put(ref, at_row, to_x, to_y):
        x = jnp.concatenate(
            [ref[pl.ds(at_row * 96, 48, stride=2), :], ref[pl.ds(at_row * 96 + 1, 48, stride=2), :]],
            axis=1,
        )
        hi, lo = split(x)
        hi_ref[to_x, to_y] = hi
        lo_ref[to_x, to_y] = lo

    for i in range(2):
        for j in range(2):
            put(own_ref, i * 2 + j, 1 + i, 1 + j)
        put(one_ref, i, 1 + i, 3 * core_ref[0])
        put(two_ref, i, 1 + i, 3 - 3 * core_ref[0])
    for i, to_y in enumerate((1, 2, 0, 3)):
        put(beside_ref, i, to_beside, to_y)
        put(away_ref, i, to_away, to_y)
    acc_ref[...] = jnp.zeros_like(acc_ref)

    @pl.loop(0, 3)
    def _(dx):
        tiles_copy(tiles_hbm, tiles_ref, sems, dx).wait()
        for dy in range(3):
            hi = hi_ref[pl.ds(dx, 2), dy : dy + 2].reshape(192, 256)
            lo = lo_ref[pl.ds(dx, 2), dy : dy + 2].reshape(192, 256)
            for dz in range(3):
                re = tiles_ref[dx * 9 + dy * 3 + dz, 0]
                im = tiles_ref[dx * 9 + dy * 3 + dz, 1]
                matrix = jnp.concatenate(
                    [jnp.concatenate([re, -im], axis=1), jnp.concatenate([im, re], axis=1)], axis=0
                )
                y = dot3((hi, lo), split(matrix), NT).reshape(4, 48, 256)
                if dz == 0:
                    acc_ref[:, 8:48] += y[:, 0:40]
                elif dz == 1:
                    acc_ref[...] += y
                else:
                    acc_ref[:, 0:40] += y[:, 8:48]

    out_ref[...] = acc_ref[...].reshape(192, 256)


def translate_kernel(
    slots_ref, kinds_ref, table_ref, src_ref, one_ref, two_ref,
    keep_ref, swap_ref, far_ref, acc_ref,
):
    acc_ref[...] = jnp.zeros_like(acc_ref)
    row = lax.broadcasted_iota(jnp.int32, (8, 128), 0)

    def tile(first):
        return pl.ds(pl.multiple_of(first, 8), 8)

    def source(s, carry):
        part = src_ref[s]
        both = jnp.concatenate([part, part], axis=0)
        both = jnp.where(row < 4, both, times_i(both))
        slots, sums = [], []
        for f in range(16):
            slot = slots_ref[s * 16 + f]
            slots.append(slot)
            kind = kinds_ref[s * 16 + f]
            sums.append(acc_ref[tile(slot), :] + table_ref[tile(kind), :] * both)
        for f in range(16):
            acc_ref[tile(slots[f]), :] = sums[f]
        return carry

    lax.fori_loop(0, 96, source, 0, unroll=4)

    def folded(block):
        part = acc_ref[pl.ds(block * 768, 768), :].reshape(96, 8, 128)
        return part[:, :4] + part[:, 4:]

    for block in range(3):
        keep_ref[block] = folded(block)
        swap_ref[block] = folded(block + 3)
    far_ref[...] = folded(6)


def fold_kernel(
    core_ref, keep_ref, got_ref, cur_ref, one_ref, two_ref,
    first_ref, mid_ref, second_ref, beside_ref, away_ref,
):
    core = core_ref[0]
    first_ref[...] = keep_ref[2 - 2 * core] + got_ref[2 - 2 * core]
    mid_ref[...] = keep_ref[1] + got_ref[1]
    second_ref[...] = keep_ref[2 * core] + got_ref[2 * core]
    for ref, row in ((beside_ref, 1 - core), (away_ref, core)):
        side = pl.ds(pl.multiple_of(row * 96, 8), 96)
        ref[pl.ds(0, 192), :] = cur_ref[pl.ds(pl.multiple_of(row * 192, 8), 192), :]
        ref[pl.ds(pl.multiple_of(192 + core * 96, 8), 96), :] = one_ref[side, :]
        ref[pl.ds(pl.multiple_of(288 - core * 96, 8), 96), :] = two_ref[side, :]


def join_kernel(mid_ref, far_ref, back_ref, ahead_ref, out_ref):
    out_ref[...] = (mid_ref[...] + far_ref[...]) + (back_ref[...] + ahead_ref[...])


def call(kernel, out_shape, scratch=(), in_specs=None, flops=0, moved=0, vmem_bytes=VMEM_BYTES):
    extra = {} if in_specs is None else {"in_specs": in_specs}
    return pl.pallas_call(
        kernel,
        out_shape=out_shape,
        scratch_shapes=list(scratch),
        compiler_params=pltpu.CompilerParams(vmem_limit_bytes=vmem_bytes),
        cost_estimate=pl.CostEstimate(flops=flops, bytes_accessed=moved, transcendentals=0),
        **extra,
    )


def f32(*shape):
    return jax.ShapeDtypeStruct(shape, F32)


def pair_words(far_targets, far_offsets):
    slab = lax.axis_index("slab")
    ring = slab % 8
    y, core = ring // 2, ring % 2

    def own(table):
        return jnp.concatenate(
            [lax.dynamic_slice_in_dim(table, (ring + z_hi * 8) * 48, 48, 0) for z_hi in range(2)]
        )

    targets, kinds = own(far_targets), own(far_offsets)
    to_slab, row = targets // 48, targets % 48
    half, to_ring = to_slab // 8, to_slab % 8
    step = (to_ring // 2 - y + 4) % 4
    near_block = (step + 1) % 4 + jnp.where(to_ring % 2 == core, 0, 3)
    block = jnp.where(step == 2, 6, near_block)
    slot = block * 96 + half * 48 + row
    return (slot * 8).reshape(-1), (kinds * 8).reshape(-1)


def operator_table(translators):
    count = translators.shape[0]
    half = lax.axis_index("slab") // 8
    own = lax.dynamic_slice_in_dim(translators, half * 32, 32, 2)
    lanes = jnp.concatenate([own] * 4, axis=2)
    return jnp.broadcast_to(lanes[:, :, None, :], (count, 2, 4, 128)).reshape(count * 8, 128)


def moved_by(block, move):
    return lax.ppermute(block, AXES, route_of(move))


def spread(block, groups):
    return lax.all_to_all(
        block, AXES, split_axis=0, concat_axis=0, axis_index_groups=groups, tiled=True
    )


def per_device(currents, near_tiles, radiation, child_phase, translators, far_targets, far_offsets):
    groups = exchange_groups()
    rows = currents.reshape(384, 128)
    core = (lax.axis_index("slab") % 2).astype(jnp.int32).reshape(1)
    slots, kinds = pair_words(far_targets, far_offsets)
    table = operator_table(translators)
    vmem = pl.BlockSpec(memory_space=pltpu.VMEM)
    smem = pl.BlockSpec(memory_space=pltpu.SMEM)
    hbm = pl.BlockSpec(memory_space=pl.ANY)

    patterns, one, two = call(
        aggregate_kernel,
        (f32(32, 3, 4, 128), f32(192, 128), f32(192, 128)),
        [
            pltpu.VMEM((384, 128), F32),
            pltpu.VMEM((2, 1024, 128), F32),
            pltpu.VMEM((8, 1024), F32),
            pltpu.SemaphoreType.DMA((6,)),
        ],
        in_specs=[smem] + [hbm] * 3,
        flops=600_000_000,
        moved=2_000_000,
        vmem_bytes=62 * 1024 * 1024,
    )(core, rows, radiation, child_phase)
    moved = spread(patterns, groups)

    def along_dir(block, sign):
        def move(z_hi, y, core, d):
            to = d + sign * (1 - 2 * core)
            return (z_hi, y, core, to) if 0 <= to < 16 else None

        return moved_by(block, move)

    one, two = along_dir(one, 1), along_dir(two, -1)

    keep, swap, far = call(
        translate_kernel,
        (f32(3, 96, 4, 128), f32(3, 96, 4, 128), f32(96, 4, 128)),
        [pltpu.VMEM((5376, 128), F32)],
        in_specs=[smem, smem, vmem, vmem, hbm, hbm],
        flops=100_000_000,
        moved=3_000_000,
    )(slots, kinds, table, moved.reshape(96, 4, 128), one, two)
    far_in = moved_by(far, lambda z_hi, y, core, d: (z_hi, (y + 2) % 4, 1 - core, d))
    swap_in = moved_by(swap, lambda z_hi, y, core, d: (z_hi, y, 1 - core, d))
    first, mid, second, beside, away = call(
        fold_kernel,
        (f32(96, 4, 128),) * 3 + (f32(384, 128),) * 2,
        in_specs=[smem] + [vmem] * 5,
        flops=1_000_000,
        moved=2_000_000,
    )(core, keep, swap_in, rows, one, two)
    first_in = moved_by(first, lambda z_hi, y, core, d: (z_hi, (y + 1 + 2 * core) % 4, core, d))
    second_in = moved_by(second, lambda z_hi, y, core, d: (z_hi, (y + 3 - 2 * core) % 4, core, d))
    beside = moved_by(beside, lambda z_hi, y, core, d: (z_hi, y, 1 - core, d))
    away = lax.ppermute(
        away, "slab", [(s, s + 2 * (s % 2) - 1) for s in range(16) if 0 <= s + 2 * (s % 2) - 1 < 16]
    )
    incoming = call(
        join_kernel, f32(96, 4, 128), flops=1_000_000, moved=1_000_000
    )(mid, far_in, first_in, second_in)
    returned = spread(incoming.reshape(32, 3, 4, 128), groups)

    near = call(
        near_kernel,
        f32(192, 256),
        [
            pltpu.VMEM((27, 2, 128, 128), F32),
            pltpu.VMEM((4, 4, 48, 256), BF16),
            pltpu.VMEM((4, 4, 48, 256), BF16),
            pltpu.VMEM((4, 48, 256), F32),
            pltpu.SemaphoreType.DMA((3,)),
        ],
        in_specs=[smem] + [vmem] * 5 + [hbm],
        flops=2_000_000_000,
        moved=5_000_000,
        vmem_bytes=50 * 1024 * 1024,
    )(core, rows, beside, away, one, two, near_tiles)

    applied = call(
        disaggregate_kernel,
        f32(384, 128),
        [pltpu.VMEM((192, 256), F32)],
        flops=600_000_000,
        moved=2_000_000,
    )(returned, radiation, child_phase, near)
    return applied.reshape(currents.shape)


def solution(mesh):
    in_specs = (
        P("slab", "dir", None, None, None, None),
        P(),
        P(),
        P(),
        P(None, None, "dir"),
        P(),
        P(),
    )
    out_specs = P("slab", "dir", None, None, None, None)
    return jax.shard_map(
        per_device, mesh=mesh, in_specs=in_specs, out_specs=out_specs, check_vma=False
    )
```

```python
import functools

import jax
import jax.numpy as jnp
from jax import lax
from jax.experimental import pallas as pl
from jax.experimental.pallas import tpu as pltpu
from jax.sharding import PartitionSpec as P

F32 = jnp.float32
BF16 = jnp.bfloat16
AXES = ("slab", "dir")
VMEM_BYTES = 32 * 1024 * 1024
NT = (((1,), (1,)), ((), ()))
NN = (((1,), (0,)), ((), ()))


def linear(z_hi, y, core, d):
    return (z_hi * 8 + y * 2 + core) * 16 + d


def route_of(move):
    pairs = []
    for s in range(16):
        for d in range(16):
            to = move(s // 8, s // 2 % 4, s % 2, d)
            if to is not None:
                pairs.append((s * 16 + d, linear(*to)))
    return pairs


def exchange_groups():
    return [
        [linear(z_hi, j // 2, j % 2, d) for z_hi in range(2) for d in range(16)] for j in range(8)
    ]


def split(x):
    hi = x.astype(BF16)
    lo = (x - hi.astype(F32)).astype(BF16)
    return hi, lo


def dot3(a, b, dims):
    a_hi, a_lo = a
    b_hi, b_lo = b
    dot = functools.partial(lax.dot_general, dimension_numbers=dims, preferred_element_type=F32)
    return dot(a_hi, b_hi) + (dot(a_lo, b_hi) + dot(a_hi, b_lo))


def lane_sign(shape):
    lane = lax.broadcasted_iota(jnp.int32, shape, len(shape) - 1) % 128
    return jnp.where(lane < 64, -1.0, 1.0).astype(F32)


def times_i(x):
    return lane_sign(x.shape) * pltpu.roll(x, 64, 1)


def swap_bits(x):
    row = lax.broadcasted_iota(jnp.int32, x.shape, 0) // 4 % 2
    lane = lax.broadcasted_iota(jnp.int32, x.shape, 1) // 32 % 2
    other = pltpu.roll(x, 4, 0)
    moved = jnp.where(lane == 1, pltpu.roll(other, 32, 1), pltpu.roll(other, 96, 1))
    return jnp.where(row == lane, x, moved)


def radiation_copy(rad_hbm, rad_ref, sems, i):
    block = pl.ds(pl.multiple_of(i * 256, 256), 256)
    return pltpu.make_async_copy(rad_hbm.at[:, block], rad_ref.at[:, block], sems.at[i])


def tiles_copy(tiles_hbm, tiles_ref, sems, i):
    block = pl.ds(i * 9, 9)
    return pltpu.make_async_copy(tiles_hbm.at[block], tiles_ref.at[block], sems.at[i])


def radiation_block(rad_ref, start):
    re = rad_ref[0, pl.ds(start, 128), :]
    im = rad_ref[1, pl.ds(start, 128), :]
    top = jnp.concatenate([re, -im], axis=1)
    low = jnp.concatenate([im, re], axis=1)
    return split(jnp.concatenate([top[:64], low[:64], top[64:], low[64:]], axis=0))


def phase_block(phase_ref, start):
    phase = phase_ref[:, pl.ds(start, 128)]
    lane = lax.broadcasted_iota(jnp.int32, phase.shape, 1)

    def doubled(v):
        turned = pltpu.roll(v, 64, 1)
        return jnp.concatenate(
            [jnp.where(lane < 64, v, turned), jnp.where(lane < 64, turned, v)], axis=1
        )

    return doubled(jnp.cos(phase)), doubled(jnp.sin(phase))


def leaf_row(child, parent):
    i, j, l = child // 4, child // 2 % 2, child % 2
    return ((i * 2 + j) * 6 + parent * 2 + l) * 8


def aggregate_kernel(
    cur_hbm, rad_hbm, phase_hbm, out_ref, down_ref, up_ref, cur_ref, rad_ref, phase_ref, sems,
    unroll=8, groups=(8,),
):
    cur_copy = pltpu.make_async_copy(cur_hbm, cur_ref, sems.at[4])
    phase_copy = pltpu.make_async_copy(phase_hbm, phase_ref, sems.at[5])
    cur_copy.start()
    for i in range(4):
        radiation_copy(rad_hbm, rad_ref, sems, i).start()
        if i == 1:
            phase_copy.start()
    cur_copy.wait()
    for i in range(2):
        down_ref[pl.ds(i * 96, 96), :] = cur_ref[pl.ds(i * 192 + 96, 96), :]
        up_ref[pl.ds(i * 96, 96), :] = cur_ref[pl.ds(i * 192, 96), :]
    rows = cur_ref.shape[0] // 2
    x = jnp.concatenate(
        [cur_ref[pl.ds(0, rows, stride=2), :], cur_ref[pl.ds(1, rows, stride=2), :]], axis=1
    )
    x = split(x)

    def directions(step, carry):
        start = pl.multiple_of(step * 128, 128)
        leaf = dot3(x, radiation_block(rad_ref, start), NT)
        cos, sin = phase_block(phase_ref, start)
        for parent in range(3):
            a = jnp.zeros((8, 256), F32)
            b = jnp.zeros((8, 256), F32)
            for child in range(8):
                row = leaf_row(child, parent)
                part = leaf[row : row + 8]
                a = a + cos[child : child + 1] * part
                b = b + sin[child : child + 1] * part
            for pair in range(2):
                lanes = slice(pair * 128, pair * 128 + 128)
                block = swap_bits(a[:, lanes] + times_i(b[:, lanes]))
                d = step * 2 + pair
                out_ref[d, parent] = block[:4]
                out_ref[16 + d, parent] = block[4:]
        return carry

    phase_copy.wait()
    first = 0
    for count in groups:
        for i in range(first // 2, (first + count) // 2):
            radiation_copy(rad_hbm, rad_ref, sems, i).wait()
        lax.fori_loop(first, first + count, directions, 0, unroll=unroll)
        first += count


def disaggregate_kernel(in_ref, rad_ref, phase_ref, near_ref, out_ref, acc_ref, unroll=8):
    acc_ref[...] = near_ref[...]

    def directions(step, carry):
        start = pl.multiple_of(step * 128, 128)
        cos, sin = phase_block(phase_ref, start)
        parents = []
        for parent in range(3):
            halves = []
            for pair in range(2):
                d = step * 2 + pair
                block = jnp.concatenate([in_ref[d, parent], in_ref[16 + d, parent]], axis=0)
                halves.append(swap_bits(block))
            turned = jnp.concatenate([times_i(h) for h in halves], axis=1)
            parents.append((jnp.concatenate(halves, axis=1), turned))
        rows = [None] * 24
        for parent in range(3):
            plain, turned = parents[parent]
            for child in range(8):
                rows[leaf_row(child, parent) // 8] = (
                    cos[child : child + 1] * plain - sin[child : child + 1] * turned
                )
        children = split(jnp.concatenate(rows, axis=0))
        acc_ref[...] += dot3(children, radiation_block(rad_ref, start), NN)
        return carry

    lax.fori_loop(0, 8, directions, 0, unroll=unroll)
    rows = acc_ref.shape[0]
    out_ref[pl.ds(0, rows, stride=2), :] = acc_ref[:, :128]
    out_ref[pl.ds(1, rows, stride=2), :] = acc_ref[:, 128:]


def near_kernel(
    core_ref, own_ref, beside_ref, away_ref, down_ref, up_ref, tiles_hbm,
    out_ref, tiles_ref, hi_ref, lo_ref, acc_ref, sems,
):
    for i in range(3):
        tiles_copy(tiles_hbm, tiles_ref, sems, i).start()
    to_beside = jnp.where(core_ref[0] == 0, 3, 0)
    to_away = 3 - to_beside

    def put(ref, at_row, to_x, to_y):
        x = jnp.concatenate(
            [ref[pl.ds(at_row * 96, 48, stride=2), :], ref[pl.ds(at_row * 96 + 1, 48, stride=2), :]],
            axis=1,
        )
        hi, lo = split(x)
        hi_ref[to_x, to_y] = hi
        lo_ref[to_x, to_y] = lo

    for i in range(2):
        for j in range(2):
            put(own_ref, i * 2 + j, 1 + i, 1 + j)
        put(down_ref, i, 1 + i, 0)
        put(up_ref, i, 1 + i, 3)
    for i, to_y in enumerate((1, 2, 0, 3)):
        put(beside_ref, i, to_beside, to_y)
        put(away_ref, i, to_away, to_y)
    acc_ref[...] = jnp.zeros_like(acc_ref)

    @pl.loop(0, 3)
    def _(dx):
        tiles_copy(tiles_hbm, tiles_ref, sems, dx).wait()
        for dy in range(3):
            hi = hi_ref[pl.ds(dx, 2), dy : dy + 2].reshape(192, 256)
            lo = lo_ref[pl.ds(dx, 2), dy : dy + 2].reshape(192, 256)
            for dz in range(3):
                re = tiles_ref[dx * 9 + dy * 3 + dz, 0]
                im = tiles_ref[dx * 9 + dy * 3 + dz, 1]
                matrix = jnp.concatenate(
                    [jnp.concatenate([re, -im], axis=1), jnp.concatenate([im, re], axis=1)], axis=0
                )
                y = dot3((hi, lo), split(matrix), NT).reshape(4, 48, 256)
                if dz == 0:
                    acc_ref[:, 8:48] += y[:, 0:40]
                elif dz == 1:
                    acc_ref[...] += y
                else:
                    acc_ref[:, 0:40] += y[:, 8:48]

    out_ref[...] = acc_ref[...].reshape(192, 256)


def translate_kernel(
    slots_ref, kinds_ref, table_ref, src_ref, down_ref, up_ref,
    keep_ref, swap_ref, far_ref, acc_ref,
):
    acc_ref[...] = jnp.zeros_like(acc_ref)
    row = lax.broadcasted_iota(jnp.int32, (8, 128), 0)

    def tile(first):
        return pl.ds(pl.multiple_of(first, 8), 8)

    def source(s, carry):
        part = src_ref[s]
        both = jnp.concatenate([part, part], axis=0)
        both = jnp.where(row < 4, both, times_i(both))
        slots, sums = [], []
        for f in range(16):
            slot = slots_ref[s * 16 + f]
            slots.append(slot)
            kind = kinds_ref[s * 16 + f]
            sums.append(acc_ref[tile(slot), :] + table_ref[tile(kind), :] * both)
        for f in range(16):
            acc_ref[tile(slots[f]), :] = sums[f]
        return carry

    lax.fori_loop(0, 96, source, 0, unroll=4)

    def folded(block):
        tiles = acc_ref.reshape(672, 8, 128)
        rows = pl.ds(block * 96, 96)
        return tiles[rows, 0:4, :] + tiles[rows, 4:8, :]

    for block in range(3):
        keep_ref[block] = folded(block)
        swap_ref[block] = folded(block + 3)
    far_ref[...] = folded(6)


def fold_kernel(
    core_ref, keep_ref, got_ref, cur_ref, down_ref, up_ref,
    back_ref, mid_ref, ahead_ref, beside_ref, away_ref,
):
    back_ref[...] = keep_ref[0] + got_ref[0]
    mid_ref[...] = keep_ref[1] + got_ref[1]
    ahead_ref[...] = keep_ref[2] + got_ref[2]
    core = core_ref[0]
    for ref, row in ((beside_ref, 1 - core), (away_ref, core)):
        ref[pl.ds(0, 192), :] = cur_ref[pl.ds(pl.multiple_of(row * 192, 8), 192), :]
        ref[pl.ds(192, 96), :] = down_ref[pl.ds(pl.multiple_of(row * 96, 8), 96), :]
        ref[pl.ds(288, 96), :] = up_ref[pl.ds(pl.multiple_of(row * 96, 8), 96), :]


def join_kernel(mid_ref, far_ref, back_ref, ahead_ref, out_ref):
    out_ref[...] = (mid_ref[...] + far_ref[...]) + (back_ref[...] + ahead_ref[...])


def call(kernel, out_shape, scratch=(), in_specs=None, flops=0, moved=0, vmem_bytes=VMEM_BYTES):
    extra = {} if in_specs is None else {"in_specs": in_specs}
    return pl.pallas_call(
        kernel,
        out_shape=out_shape,
        scratch_shapes=list(scratch),
        compiler_params=pltpu.CompilerParams(vmem_limit_bytes=vmem_bytes),
        cost_estimate=pl.CostEstimate(flops=flops, bytes_accessed=moved, transcendentals=0),
        **extra,
    )


def f32(*shape):
    return jax.ShapeDtypeStruct(shape, F32)


def pair_words(far_targets, far_offsets):
    slab = lax.axis_index("slab")
    ring = slab % 8
    y, core = ring // 2, ring % 2

    def own(table):
        return jnp.concatenate(
            [lax.dynamic_slice_in_dim(table, (ring + z_hi * 8) * 48, 48, 0) for z_hi in range(2)]
        )

    targets, kinds = own(far_targets), own(far_offsets)
    to_slab, row = targets // 48, targets % 48
    half, to_ring = to_slab // 8, to_slab % 8
    step = (to_ring // 2 - y + 4) % 4
    near_block = (step + 1) % 4 + jnp.where(to_ring % 2 == core, 0, 3)
    block = jnp.where(step == 2, 6, near_block)
    slot = block * 96 + half * 48 + row
    return (slot * 8).reshape(-1), (kinds * 8).reshape(-1)


def operator_table(translators):
    count = translators.shape[0]
    half = lax.axis_index("slab") // 8
    own = lax.dynamic_slice_in_dim(translators, half * 32, 32, 2)
    lanes = jnp.concatenate([own] * 4, axis=2)
    return jnp.broadcast_to(lanes[:, :, None, :], (count, 2, 4, 128)).reshape(count * 8, 128)


def moved_by(block, move):
    return lax.ppermute(block, AXES, route_of(move))


def spread(block, groups):
    return lax.all_to_all(
        block, AXES, split_axis=0, concat_axis=0, axis_index_groups=groups, tiled=True
    )


def per_device(currents, near_tiles, radiation, child_phase, translators, far_targets, far_offsets):
    groups = exchange_groups()
    rows = currents.reshape(384, 128)
    core = (lax.axis_index("slab") % 2).astype(jnp.int32).reshape(1)
    slots, kinds = pair_words(far_targets, far_offsets)
    table = operator_table(translators)
    vmem = pl.BlockSpec(memory_space=pltpu.VMEM)
    smem = pl.BlockSpec(memory_space=pltpu.SMEM)
    hbm = pl.BlockSpec(memory_space=pl.ANY)

    patterns, down, up = call(
        aggregate_kernel,
        (f32(32, 3, 4, 128), f32(192, 128), f32(192, 128)),
        [
            pltpu.VMEM((384, 128), F32),
            pltpu.VMEM((2, 1024, 128), F32),
            pltpu.VMEM((8, 1024), F32),
            pltpu.SemaphoreType.DMA((6,)),
        ],
        in_specs=[hbm] * 3,
        flops=600_000_000,
        moved=2_000_000,
        vmem_bytes=62 * 1024 * 1024,
    )(rows, radiation, child_phase)
    moved = spread(patterns, groups)
    down = lax.ppermute(down, "dir", [(d, d + 1) for d in range(15)])
    up = lax.ppermute(up, "dir", [(d + 1, d) for d in range(15)])

    keep, swap, far = call(
        translate_kernel,
        (f32(3, 96, 4, 128), f32(3, 96, 4, 128), f32(96, 4, 128)),
        [pltpu.VMEM((5376, 128), F32)],
        in_specs=[smem, smem, vmem, vmem, hbm, hbm],
        flops=100_000_000,
        moved=3_000_000,
    )(slots, kinds, table, moved.reshape(96, 4, 128), down, up)
    far_in = moved_by(far, lambda z_hi, y, core, d: (z_hi, (y + 2) % 4, 1 - core, d))
    swap_in = moved_by(swap, lambda z_hi, y, core, d: (z_hi, y, 1 - core, d))
    back, mid, ahead, beside, away = call(
        fold_kernel,
        (f32(96, 4, 128),) * 3 + (f32(384, 128),) * 2,
        in_specs=[smem] + [vmem] * 5,
        flops=1_000_000,
        moved=2_000_000,
    )(core, keep, swap_in, rows, down, up)
    back_in = moved_by(back, lambda z_hi, y, core, d: (z_hi, (y + 3) % 4, core, d))
    ahead_in = moved_by(ahead, lambda z_hi, y, core, d: (z_hi, (y + 1) % 4, core, d))
    beside = moved_by(beside, lambda z_hi, y, core, d: (z_hi, y, 1 - core, d))
    away = lax.ppermute(
        away, "slab", [(s, s + 2 * (s % 2) - 1) for s in range(16) if 0 <= s + 2 * (s % 2) - 1 < 16]
    )
    incoming = call(
        join_kernel, f32(96, 4, 128), flops=1_000_000, moved=1_000_000
    )(mid, far_in, back_in, ahead_in)
    returned = spread(incoming.reshape(32, 3, 4, 128), groups)

    near = call(
        near_kernel,
        f32(192, 256),
        [
            pltpu.VMEM((27, 2, 128, 128), F32),
            pltpu.VMEM((4, 4, 48, 256), BF16),
            pltpu.VMEM((4, 4, 48, 256), BF16),
            pltpu.VMEM((4, 48, 256), F32),
            pltpu.SemaphoreType.DMA((3,)),
        ],
        in_specs=[smem] + [vmem] * 5 + [hbm],
        flops=2_000_000_000,
        moved=5_000_000,
        vmem_bytes=50 * 1024 * 1024,
    )(core, rows, beside, away, down, up, near_tiles)

    applied = call(
        disaggregate_kernel,
        f32(384, 128),
        [pltpu.VMEM((192, 256), F32)],
        flops=600_000_000,
        moved=2_000_000,
    )(returned, radiation, child_phase, near)
    return applied.reshape(currents.shape)


def solution(mesh):
    in_specs = (
        P("slab", "dir", None, None, None, None),
        P(),
        P(),
        P(),
        P(None, None, "dir"),
        P(),
        P(),
    )
    out_specs = P("slab", "dir", None, None, None, None)
    return jax.shard_map(
        per_device, mesh=mesh, in_specs=in_specs, out_specs=out_specs, check_vma=False
    )
```
